32 devices in a mesh: blk: 8 (over z, x), dp: 4 (over y, core).
Axes of the slice: x: 2, y: 2, z: 4, core: 2. Of those that a mesh axis runs over, the one named last changes fastest.
Arguments:
- layer_input: bfloat16 [4, 1024, 1024], P('dp', 'blk'), may hold values from -6 to 6
- memory: bfloat16 [4, 512, 1024], P('dp', 'blk'), may hold values from -6 to 6
- cotangent: bfloat16 [4, 1024, 1024], P('dp', 'blk'), may hold values from -6 to 6
- block_order: int32 [8], replicated, may hold values from 0 to 7, each once
- w_query: float32 [1024, 1024], P(('blk', 'dp')), may hold values from -0.1875 to 0.1875
- w_key: float32 [1024, 1024], P(('blk', 'dp')), may hold values from -0.1875 to 0.1875
- w_value: float32 [1024, 1024], P(('blk', 'dp')), may hold values from -0.1875 to 0.1875
- w_output: float32 [1024, 1024], P(('blk', 'dp')), may hold values from -1.5 to 1.5
- w_in: float32 [1024, 4096], P(('blk', 'dp')), may hold values from -0.1875 to 0.1875
- w_out: float32 [4096, 1024], P(('blk', 'dp')), may hold values from -0.09375 to 0.09375
- vectors: float32 [8, 1024], P(None, ('blk', 'dp')), may hold values from -2 to 2, as said below
- b_in: float32 [4096], P(('blk', 'dp')), may hold values from -3 to 3
Outputs:
- layer_out: bfloat16 [4, 1024, 1024], P('dp', 'blk')
- input_grad: float32 [4, 1024, 1024], P('dp', 'blk')
- grad_query: float32 [1024, 1024], P(('blk', 'dp'))
- grad_key: float32 [1024, 1024], P(('blk', 'dp'))
- grad_value: float32 [1024, 1024], P(('blk', 'dp'))
- grad_output: float32 [1024, 1024], P(('blk', 'dp'))
- grad_inner: float32 [1024, 4096], P(('blk', 'dp'))
- grad_outer: float32 [4096, 1024], P(('blk', 'dp'))
- grad_vectors: float32 [8, 1024], P(None, ('blk', 'dp'))
- grad_hidden_bias: float32 [4096], P(('blk', 'dp'))
The draws below stay inside these ranges and needn't reach their ends.
Inputs may be any that keep to these rules, and one draw needn't show every extreme that they name: Device i of blk holds the positions block_order[i] * 128 to block_order[i] * 128 + 127 of every segment; every block is held once. `vectors`: rows 0 and 5 are gains between 0.5 and 1.5.
All inputs are finite; a program needn't handle non-finite values.
Results may differ from the reference program's by a relative error of at most 0.015.
Values may be sent and summed in bfloat16 or wider, within the bound.
A program may use at most 256 MiB of HBM per device.

```python
import jax
import jax.numpy as jnp
from jax import lax

D = 1024
HEADS = 16
HEAD_DIM = 64
FF = 4096
TOK_DEV = 128
SEQ = 1024
MEM = 512
SEGS = 4
N_BLK = 8


def draw_vectors(key, part):
    key = jax.random.fold_in(key, 7)
    gain_key, shift_key = jax.random.split(key)
    gains = jax.random.uniform(gain_key, (8, D), jnp.float32, 0.5, 1.5)
    shifts = jnp.clip(0.5 * jax.random.normal(shift_key, (8, D), jnp.float32), -2.0, 2.0)
    rows = jnp.arange(8)[:, None]
    return jnp.where((rows == 0) | (rows == 5), gains, shifts).astype(jnp.float32)


def shard_levels(rng, shape, pieces, least, high):
    level = 1.0
    for position, parts in pieces:
        draws = jax.random.uniform(jax.random.fold_in(jax.random.fold_in(rng, 6), position), (parts,), jnp.float32, least / len(pieces), high / len(pieces))
        level = level * jnp.repeat(jnp.exp(draws), shape[position] // parts).reshape((-1,) + (1,) * (len(shape) - 1 - position))
    return level


def normal_values(own_key, shape, scale, limit, pieces=(), kind=jnp.bfloat16):
    drawn = jax.random.normal(own_key, shape, jnp.float32) * scale
    if len(pieces) > 0:
        drawn = shard_levels(own_key, shape, pieces, -0.22, 0.18) * drawn
    return jnp.clip(drawn, min=-limit, max=limit).astype(kind)


def setup_inputs(seed: int = 0) -> dict:
    seeds = jax.random.split(jax.random.key(seed), 13)
    layer_input = normal_values(seeds[0], (SEGS, SEQ, D), 1.0, 6.0, ((0, 4), (1, 8)))
    memory = normal_values(seeds[1], (SEGS, MEM, D), 1.0, 6.0, ((0, 4), (1, 8)))
    cotangent = normal_values(seeds[2], (SEGS, SEQ, D), 1.0, 6.0, ((0, 4), (1, 8)))
    block_order = jax.random.permutation(seeds[3], N_BLK).astype(jnp.int32)
    w_query = normal_values(seeds[4], (D, D), D ** -0.5, 0.1875, ((0, 32),), jnp.float32)
    w_key = normal_values(seeds[5], (D, D), D ** -0.5, 0.1875, ((0, 32),), jnp.float32)
    w_value = normal_values(seeds[6], (D, D), D ** -0.5, 0.1875, ((0, 32),), jnp.float32)
    w_output = normal_values(seeds[7], (D, D), (D // 64) ** -0.5, 1.5, ((0, 32),), jnp.float32)
    w_in = normal_values(seeds[8], (D, FF), D ** -0.5, 0.1875, ((0, 32),), jnp.float32)
    w_out = normal_values(seeds[9], (FF, D), FF ** -0.5, 0.09375, ((0, 32),), jnp.float32)
    vectors = draw_vectors(jax.random.fold_in(seeds[12], 71), 0)
    b_in = normal_values(seeds[11], (FF,), 0.5, 3.0, ((0, 32),), jnp.float32)
    return dict(layer_input=layer_input, memory=memory, cotangent=cotangent, block_order=block_order, w_query=w_query, w_key=w_key, w_value=w_value, w_output=w_output, w_in=w_in, w_out=w_out, vectors=vectors, b_in=b_in)


@jax.custom_vjp
def low(v):
    return lax.optimization_barrier(v.astype(jnp.bfloat16)).astype(jnp.float32)

@jax.custom_vjp
def low_back(v):
    return v

def low_keep(v):
    return (low(v), None)

def low_pass(kept, grad):
    return (grad,)

def back_keep(v):
    return (v, None)

def back_low(kept, grad):
    return (low(grad),)
low.defvjp(low_keep, low_pass)
low_back.defvjp(back_keep, back_low)

def layer_norm(values, gain, shift):
    center = values - lax.optimization_barrier(jnp.mean(values, axis=-1, keepdims=True))
    spread = lax.optimization_barrier(jnp.mean(center * center, axis=-1, keepdims=True))
    return center * lax.rsqrt(spread + 1e-05) * gain + shift

def matmul(left, right):
    return jnp.dot(left, right, precision=lax.Precision.HIGHEST)

def reference(layer_input, memory, cotangent, block_order, w_query, w_key, w_value, w_output, w_in, w_out, vectors, b_in):
    highest = lax.Precision.HIGHEST
    positions = (block_order[:, None] * TOK_DEV + jnp.arange(TOK_DEV, dtype=jnp.int32)[None, :]).reshape(SEQ).astype(jnp.int32)
    key_pos = jnp.concatenate([jnp.full((MEM,), -1, jnp.int32), positions]).astype(jnp.int32)
    block = min(512, SEQ)
    count = SEQ // block
    recalled_all = memory.astype(jnp.float32)

    def forward(params, tokens):
        query_w, key_w, value_w, output_w, inner_w, outer_w, vector_rows, inner_bias = [low(param) for param in params]

        def segment(pair):
            rows, recalled = pair
            normed = low(layer_norm(jnp.concatenate([recalled, rows], axis=0), vector_rows[0], vector_rows[1]))
            normed_tok = normed[MEM:]
            queries = low_back(low(matmul(normed_tok, query_w) + vector_rows[2]))
            keys = low_back(low(matmul(normed, key_w)))
            values = low_back(low(matmul(normed, value_w) + vector_rows[3]))
            key_heads = keys.reshape(MEM + SEQ, HEADS, HEAD_DIM)
            value_heads = values.reshape(MEM + SEQ, HEADS, HEAD_DIM)

            def attend(inputs):
                query_rows, query_pos = inputs
                scores = jnp.einsum('qhd,khd->hqk', query_rows.reshape(block, HEADS, HEAD_DIM), key_heads, precision=highest)
                scores = low_back(scores * 0.125)
                scores = jnp.where(key_pos[None, None, :] <= query_pos[None, :, None], scores, -jnp.inf)
                weights = low(jax.nn.softmax(scores, axis=-1))
                mixed = jnp.einsum('hqk,khd->qhd', weights, value_heads, precision=highest)
                return low_back(low(mixed.reshape(block, D)))
            context = lax.map(jax.checkpoint(attend), (queries.reshape(count, block, D), positions.reshape(count, block)))
            context = context.reshape(SEQ, D)
            attended = low_back(matmul(context, output_w) + vector_rows[4])
            middle = rows + attended
            normed_two = low(layer_norm(middle, vector_rows[5], vector_rows[6]))
            inner = low_back(matmul(normed_two, inner_w) + inner_bias)
            activated = low(jax.nn.gelu(inner, approximate=True))
            return middle + matmul(activated, outer_w) + vector_rows[7]
        return lax.map(segment, (tokens, recalled_all))
    params = (w_query, w_key, w_value, w_output, w_in, w_out, vectors, b_in)
    result, back = jax.vjp(forward, params, layer_input.astype(jnp.float32))
    grads, input_grad = back(cotangent.astype(jnp.float32))
    return (result.astype(jnp.bfloat16), input_grad, grads[0], grads[1], grads[2], grads[3], grads[4], grads[5], grads[6], grads[7])
```

```python
import functools

import jax
import jax.numpy as jnp
from jax import lax
from jax.experimental import pallas as pl
from jax.experimental.pallas import tpu as pltpu
from jax.sharding import PartitionSpec as P

HEADS = 16
BF = jnp.bfloat16
F32 = jnp.float32
MESH = pl.DeviceIdType.MESH
EXACT = lax.Precision.HIGHEST


def dot(a, b):
    return lax.dot_general(a, b, (((1,), (0,)), ((), ())), preferred_element_type=F32)


def dot_nt(a, b, precision=None):
    return lax.dot_general(
        a, b, (((1,), (1,)), ((), ())), preferred_element_type=F32, precision=precision
    )


def dot_tn(a, b):
    return lax.dot_general(a, b, (((0,), (0,)), ((), ())), preferred_element_type=F32)


def flat(value):
    return value.reshape(-1, value.shape[-1])


def col_sum(value):
    return jnp.sum(value.astype(F32), axis=0, keepdims=True)


def norm_parts(rows):
    center = rows - jnp.mean(rows, axis=-1, keepdims=True)
    spread = jnp.mean(center * center, axis=-1, keepdims=True)
    scale = lax.rsqrt(spread + 1e-05)
    return center * scale, scale


def gelu_parts(v):
    square = v * v
    t = jnp.tanh(0.7978845608 * v * (1.0 + 0.044715 * square))
    half = 0.5 * (1.0 + t)
    slope = half + 0.5 * v * (1.0 - t * t) * (0.7978845608 * (1.0 + 3 * 0.044715 * square))
    return v * half, slope


IN_NAMES = ["x", "mem", "cot", "order", "wq", "wk", "wv", "wo", "win", "wout", "vec", "bias"]
OUT_NAMES = ["lo", "ig", "gq", "gk", "gv", "go", "gin", "gout", "gvec", "gbin"]
PLANE = [(1, 1, 1), (1, 1, 0), (1, 0, 1), (1, 0, 0), (0, 1, 1), (0, 1, 0), (0, 0, 1)]
CLASS = [(1, 1, 0), (1, 0, 0), (0, 1, 0)]
QUADS = CLASS + [(0, 0, 0)]
SIB = (0, 0, 1)


def scratch_list(T, M, D, FF):
    R = T + M
    H = FF // 8
    Q = D // 4
    W = D // 8
    S = 8 * T
    K = 8 * R
    return dict(
        n_all=((8, R, D), BF),
        xm=((M, D), BF),
        xt=((T, D), BF),
        cot_all=((8, T, D), BF),
        n2_all=((8, T, D), BF),
        pq=((8, D // 32, 3 * W), BF),
        pi=((8, D // 32, H), BF),
        wqkv=((4, 8, D // 32, 3 * W), BF),
        w_in=((4, 8, D // 32, H), BF),
        w_out=((4, H // 4, D), BF),
        w_o=((4, 8, D // 32, D), BF),
        vg1=((8, 8, W), F32),
        vg2=((4, 2, 8, W), F32),
        bslot=((4, 8, H // 4), F32),
        prm=((8, D), F32),
        qkv=((8, R, 3 * W), BF),
        qs=((S, W), BF),
        kk=((K, W), BF),
        vv=((K, W), BF),
        wts=((2, S, K), BF),
        ctx=((S, W), F32),
        ctx_send=((8, T, W), BF),
        ctx_own=((8, T, W), BF),
        ctx2d=((T, D), BF),
        mid=((T, D), F32),
        act=((4, S, H // 4), BF),
        inner=((S, H), BF),
        pb_a=((8, T, D), BF),
        r1_a=((4, T, D), BF),
        r3_a=((3, T, D), BF),
        pb_b=((8, T, D), BF),
        r1_b=((4, T, D), BF),
        r3_b=((3, T, D), BF),
        pb_n=((8, T, D), BF),
        r1_n=((4, T, D), BF),
        r3_n=((3, T, D), BF),
        mg=((T, D), F32),
        attg=((T, D), BF),
        cg_send=((8, T, W), BF),
        cg_all=((8, T, W), BF),
        go_buf=((4, 8, D // 32, D), BF),
        go_r1=((4, 4, D // 32, D), BF),
        go_r3=((3, 4, D // 32, D), BF),
        go_sum=((4, D // 32, D), BF),
        go_z=((3, D // 32, D), BF),
        cg_sorted=((S, W), BF),
        dq=((S, W), F32),
        dk=((K, W), F32),
        dv=((K, W), F32),
        dqkv=((8, R, 3 * W), BF),
        gout_s=((4, H // 4, D), BF),
        gout_own=((H // 4, D), F32),
        gout_r=((3, H // 4, D), BF),
        gin_s=((4, 8, D // 32, H), BF),
        gin_own=((Q, H), F32),
        gin_r=((3, 8, D // 32, H), BF),
        gin_a=((8, D // 32, H), BF),
        gin_b=((8, D // 32, H), BF),
        gqkv_s=((4, 8, D // 32, 3 * W), BF),
        gqkv_own=((Q, 3 * W), F32),
        gqkv_r=((3, 8, D // 32, 3 * W), BF),
        gqkv_a=((8, D // 32, 3 * W), BF),
        gqkv_b=((8, D // 32, 3 * W), BF),
        vp=((8, 8, W), F32),
        vr=((3, 2, 8, W), F32),
        vs=((2, 8, W), F32),
        va=((8, 8, W), F32),
        bp=((4, 8, H // 4), F32),
        br=((3, 8, H // 4), F32),
        lo_s=((T, D), BF),
        ig_s=((T, D), BF),
    )


SEMS = 200


class Sender:
    def __init__(self, ssem, rsem):
        self.ssem, self.rsem, self.count, self.pending = ssem, rsem, 0, []

    def make(self, src, dst, target):
        at = self.count
        self.count += 1
        return pltpu.make_async_remote_copy(
            src_ref=src,
            dst_ref=dst,
            send_sem=self.ssem.at[at],
            recv_sem=self.rsem.at[at],
            device_id=target,
            device_id_type=MESH,
        )

    def send(self, src, dst, target):
        copy = self.make(src, dst, target)
        copy.start()
        self.pending.append(copy)
        return copy

    def drain(self):
        for copy in self.pending:
            copy.wait_send()


def layer_kernel(T, M, D, FF, *refs):
    names = IN_NAMES + OUT_NAMES + list(scratch_list(T, M, D, FF))
    r = dict(zip(names, refs))
    ssem, rsem = refs[len(names):]
    g = type("Refs", (), r)
    R, H, Q, W, S = T + M, FF // 8, D // 4, D // 8, 8 * T
    H4, D32 = H // 4, D // 32
    MK = 8 * M
    tx = Sender(ssem, rsem)

    b, d = lax.axis_index("blk"), lax.axis_index("dp")
    z, x, y, c = b // 2, b % 2, d // 2, d % 2
    p = 4 * x + 2 * y + c

    def dev(z, x, y, c):
        return (2 * z + x, 2 * y + c)

    def near(rel):
        return dev(z, (x + rel[0]) % 2, (y + rel[1]) % 2, (c + rel[2]) % 2)

    def slot(rel):
        return 4 * ((x + rel[0]) % 2) + 2 * ((y + rel[1]) % 2) + (c + rel[2]) % 2

    def along(dz):
        return dev((z + dz) % 4, x, y, c)

    home_z = y + c * (3 - 2 * y)
    home_y, home_c = (z + z // 2) % 2, z // 2
    partner = dev(home_z, x, home_y, home_c)
    partner_slot = 4 * x + 2 * home_y + home_c
    stays = home_z == z
    moves = jnp.logical_not(stays)

    barrier = pltpu.get_barrier_semaphore()
    for rel in PLANE:
        pl.semaphore_signal(barrier, inc=1, device_id=near(rel), device_id_type=MESH)
    for dz in (1, 2, 3):
        pl.semaphore_signal(barrier, inc=1, device_id=along(dz), device_id_type=MESH)

    @pl.when(moves)
    def _():
        pl.semaphore_signal(barrier, inc=1, device_id=partner, device_id_type=MESH)

    for q in range(8):
        for i, w in enumerate((g.wq, g.wk, g.wv)):
            g.pq[q, :, i * W : (i + 1) * W] = w[:, q * W : (q + 1) * W].astype(BF)
        for k in range(4):
            at = (8 * k + q) * H4
            g.pi[q, :, k * H4 : (k + 1) * H4] = g.win[:, at : at + H4].astype(BF)
    g.w_out[z] = g.wout[...].astype(BF)
    g.w_o[z, p] = g.wo[...].astype(BF)
    g.wqkv[z, p] = g.pq[p]
    g.w_in[z, p] = g.pi[p]
    g.vg1[p] = g.vec[...]
    g.bslot[z] = g.bias[...]

    @pl.when(moves)
    def _():
        pl.semaphore_wait(barrier, 11)

    @pl.when(stays)
    def _():
        pl.semaphore_wait(barrier, 10)

    def swap(src, dst_there, dst_here):
        copy = tx.make(src, dst_there, partner)

        @pl.when(moves)
        def _():
            copy.start()

        @pl.when(stays)
        def _():
            dst_here[...] = src[...]

        return copy

    def swap_wait(copy):
        @pl.when(moves)
        def _():
            copy.wait_recv()

    def gather_start(ref):
        at = ref(p)
        return [tx.send(at, at, near(rel)) for rel in CLASS + [SIB]]

    def gather_finish(ref, copies):
        forwards = [copies[3]]
        for rel, copy in zip(CLASS, copies):
            copy.wait_recv()
            at = ref(slot(rel))
            forwards.append(tx.send(at, at, near(SIB)))
        for copy in forwards:
            copy.wait_recv()

    def scatter_pair(buf, first, order):
        rel = QUADS[order]
        return tx.send(buf(slot((rel[0], rel[1], 1))), first.at[order], near(SIB))

    def scatter_add(buf, first, third, order, copy):
        rel = QUADS[order]
        copy.wait_recv()
        own = buf(slot(rel))
        own[...] = (own[...].astype(F32) + first[order].astype(F32)).astype(BF)
        if order < 3:
            return tx.send(own, third.at[order], near(rel))
        return None

    def scatter_total(buf, third, copies):
        for copy in copies:
            copy.wait_recv()
        total = buf(p)[...].astype(F32)
        for k in range(3):
            total = total + third[k].astype(F32)
        return total

    swap_x = swap(g.x, g.xt, g.xt)
    swap_m = swap(g.mem, g.xm, g.xm)
    vec_copies = [tx.send(g.vg1.at[p], g.vg1.at[p], near(rel)) for rel in PLANE]
    qkv_copies = [
        tx.send(g.pq.at[slot(rel)], g.wqkv.at[z, p], near(rel)) for rel in PLANE
    ]
    for copy in vec_copies:
        copy.wait_recv()
    for k in range(2):
        total = g.vg1[4 * k]
        for i in range(1, 4):
            total = total + g.vg1[4 * k + i]
        g.vg2[z, k] = total
    vec_copies = [tx.send(g.vg2.at[z], g.vg2.at[z], along(dz)) for dz in (1, 2, 3)]
    bias_copies = [tx.send(g.bslot.at[z], g.bslot.at[z], along(dz)) for dz in (1, 2, 3)]
    for copy in qkv_copies:
        copy.wait_recv()
    qkv_copies = [tx.send(g.wqkv.at[z], g.wqkv.at[z], along(dz)) for dz in (1, 2, 3)]
    swap_c = swap(g.cot, g.cot_all.at[partner_slot], g.cot_all.at[p])
    wo_copies = [tx.send(g.w_o.at[z, p], g.w_o.at[z, p], along(dz)) for dz in (1, 2, 3)]
    for copy in vec_copies + bias_copies:
        copy.wait_recv()
    for k in range(8):
        g.prm[:, k * W : (k + 1) * W] = g.vg2[k // 2, k % 2]
    prm = g.prm

    swap_wait(swap_m)
    swap_wait(swap_x)
    for src, at, count in ((g.xm, 0, M), (g.xt, M, T)):

        def norm_rows(i, _, src=src, at=at):
            rows = pl.ds(pl.multiple_of(i * 32, 32), 32)
            hat, _unused = norm_parts(src[rows, :].astype(F32))
            out = (hat * prm[0:1] + prm[1:2]).astype(BF)
            g.n_all[p, pl.ds(pl.multiple_of(at + i * 32, 32), 32), :] = out
            return 0

        lax.fori_loop(0, count // 32, norm_rows, 0)
    n_at = lambda q: g.n_all.at[q]
    n_copies = gather_start(n_at)
    win_copies = [tx.send(g.pi.at[slot(rel)], g.w_in.at[z, p], near(rel)) for rel in PLANE]
    gather_finish(n_at, n_copies)
    for copy in qkv_copies:
        copy.wait_recv()
    wout_copies = [tx.send(g.w_out.at[z], g.w_out.at[z], along(dz)) for dz in (1, 2, 3)]
    for copy in win_copies:
        copy.wait_recv()
    win_copies = [tx.send(g.w_in.at[z], g.w_in.at[z], along(dz)) for dz in (1, 2, 3)]
    for copy in wo_copies:
        copy.wait_recv()
    wo_at = lambda q: g.w_o.at[:, q]
    wo_copies = gather_start(wo_at)
    swap_wait(swap_c)
    cot_at = lambda q: g.cot_all.at[q]
    cot_copies = gather_start(cot_at)

    wqkv = flat(g.wqkv[...].reshape(32, D32, 3 * W))
    own_vec = g.vg2[p // 2, p % 2]
    qkv_bias = jnp.concatenate(
        [own_vec[2:3], jnp.zeros((1, W), F32), own_vec[3:4]], axis=1
    )

    def project(i, _):
        rows = flat(g.n_all[pl.ds(2 * i, 2)])
        out = dot(rows, wqkv) + qkv_bias
        g.qkv[pl.ds(2 * i, 2)] = out.astype(BF).reshape(2, R, 3 * W)
        return 0

    lax.fori_loop(0, 4, project, 0)

    place = [
        g.order[2 * (qy + qc * (3 - 2 * qy)) + qx]
        for qx in (0, 1)
        for qy in (0, 1)
        for qc in (0, 1)
    ]

    def pick(blocks, wanted):
        out = blocks[0]
        for block, (left, right) in zip(blocks[1:], wanted[1:]):
            out = jnp.where(jnp.full(out.shape, left, jnp.int32) == right, block, out)
        return out

    def to_sorted(load, store):
        def step(i, _):
            at = pl.multiple_of(i * 16, 16)
            blocks = [load(q, at).astype(F32) for q in range(8)]
            for j in range(8):
                store(j, at, pick(blocks, [(place[q], j) for q in range(8)]))
            return 0

        lax.fori_loop(0, T // 16, step, 0)

    def from_sorted(load, store):
        def step(i, _):
            at = pl.multiple_of(i * 16, 16)
            blocks = [load(j, at).astype(F32) for j in range(8)]
            for q in range(8):
                store(q, at, pick(blocks, [(place[q], j) for j in range(8)]))
            return 0

        lax.fori_loop(0, T // 16, step, 0)

    def store_qkv(j, at, rows):
        g.qs[pl.ds(j * T + at, 16), :] = (rows[:, :W] * 0.125).astype(BF)
        g.kk[pl.ds(MK + j * T + at, 16), :] = rows[:, W : 2 * W].astype(BF)
        g.vv[pl.ds(MK + j * T + at, 16), :] = rows[:, 2 * W :].astype(BF)

    to_sorted(lambda q, at: g.qkv[q, pl.ds(M + at, 16), :], store_qkv)
    for j in range(8):
        g.kk[j * M : (j + 1) * M, :] = g.qkv[j, :M, W : 2 * W]
        g.vv[j * M : (j + 1) * M, :] = g.qkv[j, :M, 2 * W :]

    B = 2 * T
    lane = lax.broadcasted_iota(jnp.int32, (B, W), 1)
    head_lanes = [lane < W // 2, lane >= W // 2]
    below = lax.broadcasted_iota(jnp.int32, (B, B), 1) <= lax.broadcasted_iota(
        jnp.int32, (B, B), 0
    )

    def only(value, h):
        return jnp.where(head_lanes[h], value, jnp.zeros_like(value))

    for i in range(S // B):
        rows = slice(i * B, (i + 1) * B)
        past = MK + i * B
        end = past + B
        q_rows = g.qs[rows, :]
        parts = []
        for h in range(2):
            qh = only(q_rows, h)
            s0 = dot_nt(qh, g.kk[:past, :])
            s1 = dot_nt(qh, g.kk[past:end, :])
            s1 = jnp.where(below, s1, -1e30)
            top = jnp.maximum(
                jnp.max(s0, axis=1, keepdims=True), jnp.max(s1, axis=1, keepdims=True)
            )
            e0 = jnp.exp(s0 - top)
            e1 = jnp.exp(s1 - top)
            total = jnp.sum(e0, axis=1, keepdims=True) + jnp.sum(e1, axis=1, keepdims=True)
            scale = 1.0 / total
            w0 = (e0 * scale).astype(BF)
            w1 = (e1 * scale).astype(BF)
            g.wts[h, rows, :past] = w0
            g.wts[h, rows, past:end] = w1
            parts.append(dot(w0, g.vv[:past, :]) + dot(w1, g.vv[past:end, :]))
        g.ctx[rows, :] = jnp.where(head_lanes[0], parts[0], parts[1])

    def store_ctx(q, at, rows):
        g.ctx_send[q, pl.ds(at, 16), :] = rows.astype(BF)

    from_sorted(lambda j, at: g.ctx[pl.ds(j * T + at, 16), :], store_ctx)
    ctx_copies = [tx.send(g.ctx_send.at[slot(rel)], g.ctx_own.at[p], near(rel)) for rel in PLANE]
    g.ctx_own[p] = g.ctx_send[p]
    gather_finish(wo_at, wo_copies)
    gather_finish(cot_at, cot_copies)
    for copy in ctx_copies:
        copy.wait_recv()
    for q in range(8):
        g.ctx2d[:, q * W : (q + 1) * W] = g.ctx_own[q]
    w_o = lambda: flat(g.w_o[...].reshape(32, D32, D))
    g.mid[...] = dot(g.ctx2d[...], w_o()) + g.xt[...].astype(F32) + prm[4:5]

    def norm_mid(i, _):
        rows = pl.ds(pl.multiple_of(i * 32, 32), 32)
        hat, _unused = norm_parts(g.mid[rows, :])
        g.n2_all[p, rows, :] = (hat * prm[5:6] + prm[6:7]).astype(BF)
        return 0

    lax.fori_loop(0, T // 32, norm_mid, 0)
    n2_at = lambda q: g.n2_all.at[q]
    n2_copies = gather_start(n2_at)
    gather_finish(n2_at, n2_copies)
    for copy in wout_copies + win_copies:
        copy.wait_recv()

    hidden_bias = jnp.concatenate([g.bslot[k, 0:1, :] for k in range(4)], axis=1)
    pb_a = lambda q: g.pb_a.at[q]
    pb_b = lambda q: g.pb_b.at[q]
    sib_a, sib_b, class_a, class_b = [], [], [], []
    for order in range(4):
        rel = QUADS[order]
        pair = 4 * ((x + rel[0]) % 2) + 2 * ((y + rel[1]) % 2)
        w_in = flat(g.w_in[...].reshape(32, D32, H))
        w_out = flat(g.w_out[...])
        inner = dot(flat(g.n2_all[pl.ds(pair, 2)]), w_in) + hidden_bias
        act, slope = gelu_parts(inner)
        act = act.astype(BF)
        act_grad = dot_nt(flat(g.cot_all[pl.ds(pair, 2)]), w_out)
        inner_grad = (act_grad * slope).astype(BF)
        at = pl.ds(pl.multiple_of(pair * T, 2 * T), 2 * T)
        g.inner[at, :] = inner_grad
        for k in range(4):
            g.act[k, at, :] = act[:, k * H4 : (k + 1) * H4]
        g.pb_b[pl.ds(pair, 2)] = dot_nt(inner_grad, w_in).astype(BF).reshape(2, T, D)
        sib_b.append(scatter_pair(pb_b, g.r1_b, order))
        g.pb_a[pl.ds(pair, 2)] = dot(act, w_out).astype(BF).reshape(2, T, D)
        if order:
            class_b.append(scatter_add(pb_b, g.r1_b, g.r3_b, order - 1, sib_b[order - 1]))
    scatter_add(pb_b, g.r1_b, g.r3_b, 3, sib_b[3])
    for order in range(4):
        sib_a.append(scatter_pair(pb_a, g.r1_a, order))
    for order in range(4):
        class_a.append(scatter_add(pb_a, g.r1_a, g.r3_a, order, sib_a[order]))

    gout_copies, gin_copies, gb_copies = [], [], []
    cot = lambda: flat(g.cot_all[...])
    inner_sum = col_sum(g.inner[...])
    for k in range(4):
        g.bp[k] = jnp.broadcast_to(inner_sum[:, k * H4 : (k + 1) * H4], (8, H4))
    for dz in (1, 2, 3, 0):
        to = (z + dz) % 4
        grad = dot_tn(g.act[to], cot())
        if dz:
            g.gout_s[to] = grad.astype(BF)
            gout_copies.append(tx.send(g.gout_s.at[to], g.gout_r.at[dz - 1], along(dz)))
            gb_copies.append(tx.send(g.bp.at[to], g.br.at[dz - 1], along(dz)))
        else:
            g.gout_own[...] = grad
    for dz in (1, 2, 3, 0):
        to = (z + dz) % 4
        cols = pl.ds(pl.multiple_of(to * Q, Q), Q)
        grad = dot_tn(flat(g.n2_all[:, :, cols]), g.inner[...])
        if dz:
            g.gin_s[to] = grad.astype(BF).reshape(8, D32, H)
            gin_copies.append(tx.send(g.gin_s.at[to], g.gin_r.at[dz - 1], along(dz)))
        else:
            g.gin_own[...] = grad

    g.mg[...] = scatter_total(pb_b, g.r3_b, class_b[:3])

    def norm_two_back(i, sums):
        rows = pl.ds(pl.multiple_of(i * 32, 32), 32)
        up = g.mg[rows, :]
        hat, scale = norm_parts(g.mid[rows, :])
        pull = up * prm[5:6]
        mean = jnp.mean(pull, axis=-1, keepdims=True)
        along_hat = jnp.mean(pull * hat, axis=-1, keepdims=True)
        cot_rows = g.cot_all[p, rows, :].astype(F32)
        out = cot_rows + scale * (pull - mean - hat * along_hat)
        low = out.astype(BF)
        g.mg[rows, :] = out
        g.attg[rows, :] = low
        return (
            sums[0] + col_sum(up * hat),
            sums[1] + col_sum(up),
            sums[2] + col_sum(low),
            sums[3] + col_sum(cot_rows),
        )

    zero_row = jnp.zeros((1, D), F32)
    gain_two, shift_two, bias_o, bias_out = lax.fori_loop(
        0, T // 32, norm_two_back, (zero_row, zero_row, zero_row, zero_row)
    )
    attg = g.attg[...]
    cg = dot_nt(attg, w_o()).astype(BF)
    for q in range(8):
        g.cg_send[q] = cg[:, q * W : (q + 1) * W]
    cg_copies = [tx.send(g.cg_send.at[slot(rel)], g.cg_all.at[p], near(rel)) for rel in PLANE]
    g.cg_all[p] = g.cg_send[p]

    go_at = lambda q: g.go_buf.at[:, q]
    for k in range(4):
        grad = dot_tn(g.ctx2d[:, k * Q : (k + 1) * Q], attg)
        g.go_buf[k] = grad.astype(BF).reshape(8, D32, D)
    sib_o = [scatter_pair(go_at, g.go_r1, order) for order in range(4)]
    class_o = [scatter_add(go_at, g.go_r1, g.go_r3, order, sib_o[order]) for order in range(4)]

    for copy in cg_copies:
        copy.wait_recv()

    def store_cg(j, at, rows):
        g.cg_sorted[pl.ds(j * T + at, 16), :] = rows.astype(BF)

    to_sorted(lambda q, at: g.cg_all[q, pl.ds(at, 16), :], store_cg)
    g.dk[...] = jnp.zeros_like(g.dk)
    g.dv[...] = jnp.zeros_like(g.dv)
    for i in range(S // B):
        rows = slice(i * B, (i + 1) * B)
        end = MK + (i + 1) * B
        cg_rows = g.cg_sorted[rows, :]
        q_rows = g.qs[rows, :]
        product = cg_rows.astype(F32) * g.ctx[rows, :]
        parts = []
        for h in range(2):
            qh, ch = only(q_rows, h), only(cg_rows, h)
            delta = jnp.sum(only(product, h), axis=1, keepdims=True)
            w = g.wts[h, rows, :end]
            pull = dot_nt(ch, g.vv[:end, :])
            ds = (w.astype(F32) * (pull - delta)).astype(BF)
            parts.append(dot(ds, g.kk[:end, :]))
            g.dk[:end, :] += dot_tn(ds, qh)
            g.dv[:end, :] += dot_tn(w, ch)
        g.dq[rows, :] = jnp.where(head_lanes[0], parts[0], parts[1]) * 0.125

    def load_grads(j, at):
        keys = pl.ds(MK + j * T + at, 16)
        return jnp.concatenate(
            [g.dq[pl.ds(j * T + at, 16), :], g.dk[keys, :], g.dv[keys, :]], axis=1
        )

    def store_grads(q, at, rows):
        g.dqkv[q, pl.ds(M + at, 16), :] = rows.astype(BF)

    from_sorted(load_grads, store_grads)
    for q in range(8):
        mt = slice(q * M, (q + 1) * M)
        g.dqkv[q, :M, :W] = jnp.zeros((M, W), BF)
        g.dqkv[q, :M, W : 2 * W] = g.dk[mt, :].astype(BF)
        g.dqkv[q, :M, 2 * W :] = g.dv[mt, :].astype(BF)

    lo = scatter_total(pb_a, g.r3_a, class_a[:3]) + g.mid[...] + prm[7:8]
    g.lo_s[...] = lo.astype(BF)
    swap_lo = swap(g.lo_s, g.lo, g.lo)
    go_total = scatter_total(go_at, g.go_r3, class_o[:3])
    g.go_sum[...] = go_total.astype(BF)
    go_copies = [
        tx.send(g.go_sum.at[(z + dz) % 4], g.go_z.at[dz - 1], along(dz)) for dz in (1, 2, 3)
    ]

    sib_n, class_n = [], []
    for order in range(4):
        rel = QUADS[order]
        pair = 4 * ((x + rel[0]) % 2) + 2 * ((y + rel[1]) % 2)
        rows = flat(g.dqkv[pl.ds(pair, 2), M:, :])
        w = flat(g.wqkv[...].reshape(32, D32, 3 * W))
        g.pb_n[pl.ds(pair, 2)] = dot_nt(rows, w).astype(BF).reshape(2, T, D)
        sib_n.append(scatter_pair(lambda q: g.pb_n.at[q], g.r1_n, order))
        if order:
            class_n.append(
                scatter_add(lambda q: g.pb_n.at[q], g.r1_n, g.r3_n, order - 1, sib_n[order - 1])
            )
    scatter_add(lambda q: g.pb_n.at[q], g.r1_n, g.r3_n, 3, sib_n[3])

    g.vp[...] = jnp.zeros_like(g.vp)
    qkv_sum = jnp.zeros((1, 3 * W), F32)
    for q in range(8):
        qkv_sum = qkv_sum + col_sum(g.dqkv[q])
    qkv_sum8 = jnp.broadcast_to(qkv_sum, (8, 3 * W))
    ones = jnp.ones((8, 3 * W), F32)
    gqkv_copies = []
    for dz in (1, 2, 3, 0):
        to = (z + dz) % 4
        cols = pl.ds(pl.multiple_of(to * Q, Q), Q)
        grad = dot_tn(flat(g.n_all[:, :, cols]), flat(g.dqkv[...]))
        if dz:
            g.gqkv_s[to] = grad.astype(BF).reshape(8, D32, 3 * W)
            gqkv_copies.append(tx.send(g.gqkv_s.at[to], g.gqkv_r.at[dz - 1], along(dz)))
        else:
            g.gqkv_own[...] = grad
        w = flat(g.wqkv[to]).astype(F32)
        gains = dot_nt(ones, grad * w, EXACT)
        shifts = dot_nt(qkv_sum8, w, EXACT)
        for k in range(2):
            at = slice(k * W, (k + 1) * W)
            shift = shifts[0:1, at]
            vec = g.vg2[to, k]
            g.vp[2 * to + k, 0:1, :] = (gains[0:1, at] - vec[1:2] * shift) / vec[0:1]
            g.vp[2 * to + k, 1:2, :] = shift
    g.vp[p, 2:3, :] = qkv_sum[:, :W]
    g.vp[p, 3:4, :] = qkv_sum[:, 2 * W :]
    for k in range(8):
        at = slice(k * W, (k + 1) * W)
        g.vp[k, 4:5, :] = bias_o[:, at]
        g.vp[k, 5:6, :] = gain_two[:, at]
        g.vp[k, 6:7, :] = shift_two[:, at]
        g.vp[k, 7:8, :] = bias_out[:, at]
    vec_copies = [
        tx.send(g.vp.at[pl.ds(2 * ((z + dz) % 4), 2)], g.vr.at[dz - 1], along(dz))
        for dz in (1, 2, 3)
    ]

    for copy in gout_copies + gb_copies + gin_copies + go_copies:
        copy.wait_recv()
    g.gout[...] = g.gout_own[...] + sum(g.gout_r[k].astype(F32) for k in range(3))
    g.gbin[...] = g.bp[z] + g.br[0] + g.br[1] + g.br[2]
    total = g.gin_own[...] + sum(flat(g.gin_r[k]).astype(F32) for k in range(3))
    g.gin_a[...] = total.astype(BF).reshape(8, D32, H)
    gin_copies = [tx.send(g.gin_a.at[slot(rel)], g.gin_b.at[p], near(rel)) for rel in PLANE]
    g.gin_b[p] = g.gin_a[p]
    g.go[...] = g.go_sum[z].astype(F32) + sum(g.go_z[k].astype(F32) for k in range(3))

    g.mid[...] = scatter_total(lambda q: g.pb_n.at[q], g.r3_n, class_n[:3])

    def norm_one_back(i, _):
        rows = pl.ds(pl.multiple_of(i * 32, 32), 32)
        hat, scale = norm_parts(g.xt[rows, :].astype(F32))
        pull = g.mid[rows, :] * prm[0:1]
        mean = jnp.mean(pull, axis=-1, keepdims=True)
        along_hat = jnp.mean(pull * hat, axis=-1, keepdims=True)
        out = g.mg[rows, :] + scale * (pull - mean - hat * along_hat)
        g.ig_s[rows, :] = out.astype(BF)
        return 0

    lax.fori_loop(0, T // 32, norm_one_back, 0)
    swap_ig = swap(g.ig_s, g.ig, g.ig)

    for copy in gqkv_copies + vec_copies:
        copy.wait_recv()
    total = g.gqkv_own[...] + sum(flat(g.gqkv_r[k]).astype(F32) for k in range(3))
    g.gqkv_a[...] = total.astype(BF).reshape(8, D32, 3 * W)
    gqkv_copies = [tx.send(g.gqkv_a.at[slot(rel)], g.gqkv_b.at[p], near(rel)) for rel in PLANE]
    g.gqkv_b[p] = g.gqkv_a[p]
    g.vs[...] = g.vp[pl.ds(2 * z, 2)] + g.vr[0] + g.vr[1] + g.vr[2]
    vec_copies = [tx.send(g.vs.at[(x + rel[0]) % 2], g.va.at[p], near(rel)) for rel in PLANE]
    g.va[p] = g.vs[x]

    for copy in gin_copies:
        copy.wait_recv()
    for q in range(8):
        for k in range(4):
            at = (8 * k + q) * H4
            g.gin[:, at : at + H4] = g.gin_b[q, :, k * H4 : (k + 1) * H4].astype(F32)
    for copy in gqkv_copies + vec_copies:
        copy.wait_recv()
    for q in range(8):
        for i, out in enumerate((g.gq, g.gk, g.gv)):
            out[:, q * W : (q + 1) * W] = g.gqkv_b[q, :, i * W : (i + 1) * W].astype(F32)
    total = g.va[0]
    for q in range(1, 8):
        total = total + g.va[q]
    g.gvec[...] = total

    for copy in (swap_lo, swap_ig):
        swap_wait(copy)
    tx.drain()

    @pl.when(moves)
    def _():
        for copy in (swap_x, swap_m, swap_c, swap_lo, swap_ig):
            copy.wait_send()


def run_layer(layer_input, memory, cotangent, block_order, w_query, w_key, w_value, w_output, w_in, w_out, vectors, b_in):
    T, D = layer_input.shape[1:]
    M = memory.shape[1]
    FF = w_in.shape[1]
    W = D // 8
    share = vectors.shape[1]
    low = vectors.astype(BF).astype(F32)
    lanes = lax.broadcasted_iota(jnp.int32, (8, W), 1) // share
    mine = lanes == lax.axis_index("dp")
    vec = jnp.where(mine, jnp.tile(low, (1, W // share)), 0.0)
    bias = jnp.broadcast_to(b_in.astype(BF).astype(F32)[None], (8, b_in.shape[0]))
    shapes = scratch_list(T, M, D, FF)
    vmem = pl.BlockSpec(memory_space=pltpu.VMEM)
    smem = pl.BlockSpec(memory_space=pltpu.SMEM)
    outs = pl.pallas_call(
        functools.partial(layer_kernel, T, M, D, FF),
        out_shape=(
            jax.ShapeDtypeStruct((T, D), BF),
            jax.ShapeDtypeStruct((T, D), BF),
            jax.ShapeDtypeStruct(w_query.shape, F32),
            jax.ShapeDtypeStruct(w_key.shape, F32),
            jax.ShapeDtypeStruct(w_value.shape, F32),
            jax.ShapeDtypeStruct(w_output.shape, F32),
            jax.ShapeDtypeStruct(w_in.shape, F32),
            jax.ShapeDtypeStruct(w_out.shape, F32),
            jax.ShapeDtypeStruct((8, W), F32),
            jax.ShapeDtypeStruct((8, b_in.shape[0]), F32),
        ),
        in_specs=[vmem, vmem, vmem, smem] + [vmem] * 8,
        out_specs=[vmem] * 10,
        scratch_shapes=[pltpu.VMEM(shape, kind) for shape, kind in shapes.values()]
        + [pltpu.SemaphoreType.DMA((SEMS,)), pltpu.SemaphoreType.DMA((SEMS,))],
        compiler_params=pltpu.CompilerParams(
            collective_id=0, has_side_effects=True, vmem_limit_bytes=63 * 2**20
        ),
    )(layer_input[0], memory[0], cotangent[0], block_order, w_query, w_key, w_value, w_output, w_in, w_out, vec, bias)
    lo, ig, gq, gk, gv, go, gin, gout, gvec, gbin = outs
    gvec = lax.dynamic_slice(gvec, (0, lax.axis_index("dp") * share), (8, share))
    return (lo[None], ig.astype(F32)[None], gq, gk, gv, go, gin, gout, gvec, gbin[0])


masked_value = -1e30


def passed_along(block, axis, distance):
    devices = range(lax.axis_size(axis))
    route = [((i - distance) % len(devices), i) for i in devices]
    return lax.ppermute(block, axis, route)


def layer_norm(values, gain, shift):
    center = values - jnp.mean(values, axis=-1, keepdims=True)
    spread = jnp.mean(center * center, axis=-1, keepdims=True)
    return center * lax.rsqrt(spread + 1e-05) * gain + shift


def contract_rows(left, right):
    return lax.dot_general(
        left, right, (((0,), (0,)), ((), ())), preferred_element_type=jnp.float32
    )


def times_transposed(left, right):
    return lax.dot_general(
        left, right, (((1,), (1,)), ((), ())), preferred_element_type=jnp.float32
    )


def split_heads(matrix, heads):
    return matrix.reshape(matrix.shape[0], heads, matrix.shape[1] // heads)


def score_block(query_heads, key_rows):
    key_heads = split_heads(key_rows, query_heads.shape[1])
    return (
        jnp.einsum("qhd,khd->hqk", query_heads, key_heads, preferred_element_type=jnp.float32)
        * 0.125
    )


def lookup_block(order, device):
    return jnp.sum(jnp.where(jnp.arange(order.shape[0]) == device, order, 0))


def split_piece(piece, rows_dev, mem_rows):
    shards = piece.shape[0] // rows_dev
    blocks = piece.reshape(shards, rows_dev, piece.shape[1])
    memory_part = blocks[:, :mem_rows].reshape(shards * mem_rows, piece.shape[1])
    token_part = blocks[:, mem_rows:].reshape(shards * (rows_dev - mem_rows), piece.shape[1])
    return (shards, memory_part, token_part)


def piece_positions(order, shards, tok_rows):
    shard_ids = jnp.arange(shards)
    hits = shard_ids[:, None] == jnp.arange(order.shape[0])[None, :]
    starts = jnp.sum(jnp.where(hits, order[None, :], 0), axis=1)
    positions = (starts[:, None] * tok_rows + jnp.arange(tok_rows)[None, :]).reshape(
        shards * tok_rows
    )
    return (starts, positions)


def softmax_stats(carry, scores):
    running, total = carry
    top = jnp.maximum(running, jnp.max(scores, axis=2))
    total = total * jnp.exp(running - top) + jnp.sum(jnp.exp(scores - top[:, :, None]), axis=2)
    return (top, total)


def per_device(
    layer_input,
    memory,
    cotangent,
    block_order,
    w_query,
    w_key,
    w_value,
    w_output,
    w_in,
    w_out,
    vectors,
    b_in,
):
    bf16 = jnp.bfloat16
    gathered = (
        lax.all_gather(w_query.astype(bf16), ("blk", "dp"), axis=0, tiled=True),
        lax.all_gather(w_key.astype(bf16), ("blk", "dp"), axis=0, tiled=True),
        lax.all_gather(w_value.astype(bf16), ("blk", "dp"), axis=0, tiled=True),
        lax.all_gather(w_output.astype(bf16), ("blk", "dp"), axis=0, tiled=True),
        lax.all_gather(w_in.astype(bf16), ("blk", "dp"), axis=0, tiled=True),
        lax.all_gather(w_out.astype(bf16), ("blk", "dp"), axis=0, tiled=True),
        lax.all_gather(vectors.astype(bf16), ("blk", "dp"), axis=1, tiled=True),
        lax.all_gather(b_in.astype(bf16), ("blk", "dp"), axis=0, tiled=True),
    )
    (
        query_full,
        key_full,
        value_full,
        output_full,
        inner_full,
        outer_full,
        vector_full,
        inner_low,
    ) = gathered
    params = vector_full.astype(jnp.float32)
    inner_shift = inner_low.astype(jnp.float32)
    heads = HEADS
    tokens = layer_input[0].astype(jnp.float32)
    recalled = memory[0].astype(jnp.float32)
    tok_rows = tokens.shape[0]
    mem_rows = recalled.shape[0]
    rows_dev = tok_rows + mem_rows
    width = tokens.shape[1]
    blocks_total = lax.axis_size("blk")
    here = lax.axis_index("blk")
    own_block = lookup_block(block_order, here)
    query_pos = own_block * tok_rows + jnp.arange(tok_rows)
    both_rows = jnp.concatenate([recalled, tokens], axis=0)
    normed = layer_norm(both_rows, params[0], params[1]).astype(bf16)
    normed_tok = normed[mem_rows:]
    queries = (
        jnp.dot(normed_tok, query_full, preferred_element_type=jnp.float32) + params[2]
    ).astype(bf16)
    keys_all = jnp.dot(normed, key_full, preferred_element_type=jnp.float32).astype(bf16)
    values_all = (
        jnp.dot(normed, value_full, preferred_element_type=jnp.float32) + params[3]
    ).astype(bf16)
    query_heads = split_heads(queries, heads)

    def causal(scores, key_pos):
        return jnp.where(key_pos[None, None, :] <= query_pos[None, :, None], scores, masked_value)

    start_stats = (
        jnp.full((heads, tok_rows), masked_value, jnp.float32),
        jnp.zeros((heads, tok_rows), jnp.float32),
    )
    carry = start_stats
    shards, memory_part, token_part = split_piece(
        lax.all_gather(keys_all, "blk", axis=0, tiled=True), rows_dev, mem_rows
    )
    starts, token_pos = piece_positions(block_order, shards, tok_rows)
    carry = softmax_stats(carry, score_block(query_heads, memory_part))

    def with_tokens(state):
        return softmax_stats(state, causal(score_block(query_heads, token_part), token_pos))

    def without_tokens(state):
        return state

    running, total = lax.cond(jnp.any(starts <= own_block), with_tokens, without_tokens, carry)
    log_total = running + jnp.log(total)

    def value_part(context, part, key_pos):
        scores = score_block(query_heads, part[:, :width])
        if key_pos is not None:
            scores = causal(scores, key_pos)
        weights = jnp.exp(scores - log_total[:, :, None]).astype(bf16)
        return context + jnp.einsum(
            "hqk,khd->qhd",
            weights,
            split_heads(part[:, width:], heads),
            preferred_element_type=jnp.float32,
        )

    key_values = jnp.concatenate([keys_all, values_all], axis=1)
    context = jnp.zeros((tok_rows, heads, width // heads), jnp.float32)
    shards, memory_part, add_token_part = split_piece(
        lax.all_gather(key_values, "blk", axis=0, tiled=True), rows_dev, mem_rows
    )
    starts, add_token_pos = piece_positions(block_order, shards, tok_rows)
    context = value_part(context, memory_part, None)

    def with_tokens(state):
        return value_part(state, add_token_part, add_token_pos)

    def without_tokens(state):
        return state

    context = lax.cond(jnp.any(starts <= own_block), with_tokens, without_tokens, context)
    context_low = context.reshape(tok_rows, width).astype(bf16)
    attended = jnp.dot(context_low, output_full, preferred_element_type=jnp.float32) + params[4]
    middle = tokens + attended
    normed_two = layer_norm(middle, params[5], params[6]).astype(bf16)
    inner = jnp.dot(normed_two, inner_full, preferred_element_type=jnp.float32) + inner_shift
    activated = jax.nn.gelu(inner, approximate=True).astype(bf16)
    result = middle + jnp.dot(activated, outer_full, preferred_element_type=jnp.float32) + params[7]
    output = result.astype(bf16)
    upstream = cotangent[0]
    upstream_full = upstream.astype(jnp.float32)
    grad_outer = contract_rows(activated, upstream)
    grad_outer_bias = jnp.sum(upstream_full, axis=0)
    act_grad = times_transposed(upstream, outer_full)
    _, gelu_back = jax.vjp(functools.partial(jax.nn.gelu, approximate=True), inner)
    inner_grad = gelu_back(act_grad)[0].astype(bf16)
    grad_inner = contract_rows(normed_two, inner_grad)
    grad_inner_bias = jnp.sum(inner_grad.astype(jnp.float32), axis=0)
    normed_two_grad = times_transposed(inner_grad, inner_full)
    _, norm_two_back = jax.vjp(layer_norm, middle, params[5], params[6])
    middle_part, grad_gain_two, grad_shift_two = norm_two_back(normed_two_grad)
    middle_grad = upstream_full + middle_part
    attended_grad = middle_grad.astype(bf16)
    grad_output = contract_rows(context_low, attended_grad)
    grad_output_bias = jnp.sum(attended_grad.astype(jnp.float32), axis=0)
    context_grad = times_transposed(attended_grad, output_full).astype(bf16)
    context_heads = split_heads(context_grad, heads)
    delta = jnp.einsum("qhd,qhd->hq", context_heads.astype(jnp.float32), context)

    def attend_back(queries_grad, part, key_pos):
        count = part.shape[0]
        key_heads = split_heads(part[:, :width], heads)
        value_heads = split_heads(part[:, width:], heads)
        scores = score_block(query_heads, part[:, :width])
        if key_pos is not None:
            scores = causal(scores, key_pos)
        exact = jnp.exp(scores - log_total[:, :, None])
        weight_low = exact.astype(bf16)
        weight_grad = jnp.einsum(
            "qhd,khd->hqk", context_heads, value_heads, preferred_element_type=jnp.float32
        )
        score_grad = (exact * (weight_grad - delta[:, :, None])).astype(bf16)
        queries_grad = (
            queries_grad
            + jnp.einsum("hqk,khd->qhd", score_grad, key_heads, preferred_element_type=jnp.float32)
            * 0.125
        )
        key_grad = (
            jnp.einsum("hqk,qhd->khd", score_grad, query_heads, preferred_element_type=jnp.float32)
            * 0.125
        )
        value_grad = jnp.einsum(
            "hqk,qhd->khd", weight_low, context_heads, preferred_element_type=jnp.float32
        )
        return (
            queries_grad,
            jnp.concatenate(
                [key_grad.reshape(count, width), value_grad.reshape(count, width)], axis=1
            ),
        )

    def visit(queries_grad, travelling, travel_grad, anchor):
        anchor_block = lookup_block(block_order, anchor)
        queries_grad, memory_grad = attend_back(queries_grad, travelling[:mem_rows], None)
        token_pos = anchor_block * tok_rows + jnp.arange(tok_rows)

        def with_tokens(state):
            return attend_back(state, travelling[mem_rows:], token_pos)

        def without_tokens(state):
            return (state, jnp.zeros((tok_rows, 2 * width), jnp.float32))

        queries_grad, token_grad = lax.cond(
            anchor_block <= own_block, with_tokens, without_tokens, queries_grad
        )
        return (queries_grad, travel_grad + jnp.concatenate([memory_grad, token_grad], axis=0))

    def pass_grads(values):
        return passed_along(values.astype(jnp.bfloat16), "blk", 1).astype(values.dtype)

    queries_grad, travel_grad = visit(
        jnp.zeros((tok_rows, heads, width // heads), jnp.float32),
        key_values,
        jnp.zeros((rows_dev, 2 * width), jnp.float32),
        here,
    )

    def turn(step, state):
        queries_grad, travelling, travel_grad = state
        travelling = passed_along(travelling, "blk", 1)
        travel_grad = pass_grads(travel_grad)
        anchor = (here - step) % blocks_total
        queries_grad, travel_grad = visit(queries_grad, travelling, travel_grad, anchor)
        return (queries_grad, travelling, travel_grad)

    queries_grad, travelling, travel_grad = lax.fori_loop(
        1, blocks_total, turn, (queries_grad, key_values, travel_grad)
    )
    travel_grad = pass_grads(travel_grad)
    pair_grad = travel_grad.astype(bf16)
    key_grad = pair_grad[:, :width]
    value_grad = pair_grad[:, width:]
    query_grad = queries_grad.reshape(tok_rows, width).astype(bf16)
    grad_query = contract_rows(normed_tok, query_grad)
    grad_query_bias = jnp.sum(query_grad.astype(jnp.float32), axis=0)
    grad_key = contract_rows(normed, key_grad)
    grad_value = contract_rows(normed, value_grad)
    grad_value_bias = jnp.sum(value_grad.astype(jnp.float32), axis=0)
    normed_grad = times_transposed(key_grad, key_full) + times_transposed(value_grad, value_full)
    query_part = times_transposed(query_grad, query_full)
    normed_grad = normed_grad + jnp.concatenate(
        [jnp.zeros((mem_rows, width), jnp.float32), query_part], axis=0
    )
    _, norm_one_back = jax.vjp(layer_norm, both_rows, params[0], params[1])
    rows_grad, grad_gain_one, grad_shift_one = norm_one_back(normed_grad)
    input_grad = middle_grad + rows_grad[mem_rows:]
    vector_grad = jnp.stack(
        [
            grad_gain_one,
            grad_shift_one,
            grad_query_bias,
            grad_value_bias,
            grad_output_bias,
            grad_gain_two,
            grad_shift_two,
            grad_outer_bias,
        ]
    )
    out_query, out_key, out_value, out_output, out_inner, out_outer, out_vectors, out_bias = (
        lax.psum_scatter(grad_query, ("blk", "dp"), scatter_dimension=0, tiled=True),
        lax.psum_scatter(grad_key, ("blk", "dp"), scatter_dimension=0, tiled=True),
        lax.psum_scatter(grad_value, ("blk", "dp"), scatter_dimension=0, tiled=True),
        lax.psum_scatter(grad_output, ("blk", "dp"), scatter_dimension=0, tiled=True),
        lax.psum_scatter(grad_inner, ("blk", "dp"), scatter_dimension=0, tiled=True),
        lax.psum_scatter(grad_outer, ("blk", "dp"), scatter_dimension=0, tiled=True),
        lax.psum_scatter(vector_grad, ("blk", "dp"), scatter_dimension=1, tiled=True),
        lax.psum_scatter(grad_inner_bias, ("blk", "dp"), scatter_dimension=0, tiled=True),
    )
    return (
        output[None],
        input_grad[None],
        out_query,
        out_key,
        out_value,
        out_output,
        out_inner,
        out_outer,
        out_vectors,
        out_bias,
    )


def solution(mesh):
    rows = P("dp", "blk", None)
    shard = P(("blk", "dp"), None)
    in_specs = (rows, rows, rows, P()) + (shard,) * 6 + (P(None, ("blk", "dp")), P(("blk", "dp")))
    out_specs = (rows, rows) + (shard,) * 6 + (P(None, ("blk", "dp")), P(("blk", "dp")))
    planes = mesh.shape["blk"] == 8 and mesh.shape["dp"] == 4
    return jax.shard_map(
        run_layer if planes else per_device,
        mesh=mesh,
        in_specs=in_specs,
        out_specs=out_specs,
        check_vma=False,
    )
```

```python
import functools

import jax
import jax.numpy as jnp
from jax import lax
from jax.experimental import pallas as pl
from jax.experimental.pallas import tpu as pltpu
from jax.sharding import PartitionSpec as P

HEADS = 16
BF = jnp.bfloat16
F32 = jnp.float32
MESH = pl.DeviceIdType.MESH
EXACT = lax.Precision.HIGHEST


def dot(a, b):
    return lax.dot_general(a, b, (((1,), (0,)), ((), ())), preferred_element_type=F32)


def dot_nt(a, b, precision=None):
    return lax.dot_general(
        a, b, (((1,), (1,)), ((), ())), preferred_element_type=F32, precision=precision
    )


def dot_tn(a, b):
    return lax.dot_general(a, b, (((0,), (0,)), ((), ())), preferred_element_type=F32)


def flat(value):
    return value.reshape(-1, value.shape[-1])


def col_sum(value):
    return jnp.sum(value.astype(F32), axis=0, keepdims=True)


def norm_parts(rows):
    center = rows - jnp.mean(rows, axis=-1, keepdims=True)
    spread = jnp.mean(center * center, axis=-1, keepdims=True)
    scale = lax.rsqrt(spread + 1e-05)
    return center * scale, scale


def gelu_parts(v):
    square = v * v
    t = jnp.tanh(0.7978845608 * v * (1.0 + 0.044715 * square))
    half = 0.5 * (1.0 + t)
    slope = half + 0.5 * v * (1.0 - t * t) * (0.7978845608 * (1.0 + 3 * 0.044715 * square))
    return v * half, slope


IN_NAMES = ["x", "mem", "cot", "order", "wq", "wk", "wv", "wo", "win", "wout", "vec", "bias"]
OUT_NAMES = ["lo", "ig", "gq", "gk", "gv", "go", "gin", "gout", "gvec", "gbin"]
TEAM = [(1, 1, 1), (1, 1, 0), (1, 0, 1), (1, 0, 0), (0, 1, 1), (0, 1, 0), (0, 0, 1)]
FAR = [(1, 0), (0, 1), (1, 1)]
QUADS = [(1, 1, 0), (0, 1, 0), (1, 0, 0), (0, 0, 0)]
SIB, XN, ZN = (0, 0, 1), (0, 1, 0), (1, 0, 0)


def scratch_list(T, M, D, FF):
    R = T + M
    H = FF // 8
    H4 = H // 4
    W = D // 8
    B = D // 32
    S = 8 * T
    K = 8 * R
    grid = (2, 4, 2, 2, B)
    return dict(
        f_qkv=((3, B, D), F32),
        f_o=((B, D), F32),
        f_in=((B, FF), F32),
        f_out=((H4, D), F32),
        n_all=((8, R, D), BF),
        xm=((M, D), BF),
        xt=((T, D), BF),
        cot_all=((8, T, D), BF),
        n2_all=((8, T, D), BF),
        pq=((8, B, 3 * W), BF),
        pi=((8, B, H), BF),
        wqkv=(grid + (3 * W,), BF),
        w_in=(grid + (H,), BF),
        w_out=((2, 2, H4, D), BF),
        w_o=(grid + (D,), BF),
        vg1=((8, 8, W), F32),
        vg2=((4, 4, 8, W), F32),
        pg=((8, 8, W), F32),
        bslot=((4, 8, H4), F32),
        prm=((8, D), F32),
        qkv=((8, R, 3 * W), BF),
        qs=((S, W), BF),
        kk=((K, W), BF),
        vv=((K, W), BF),
        wts=((2, S, K), BF),
        ctx=((S, W), F32),
        ctx_send=((8, T, W), BF),
        ctx_own=((8, T, W), BF),
        ctx2d=((T, D), BF),
        mid=((T, D), F32),
        act=((4, S, H4), BF),
        inner=((S, H), BF),
        pb_a=((8, T, D), BF),
        r1_a=((4, T, D), BF),
        rx_a=((2, T, D), BF),
        rz_a=((T, D), BF),
        pb_b=((8, T, D), BF),
        r1_b=((4, T, D), BF),
        rx_b=((2, T, D), BF),
        rz_b=((T, D), BF),
        pb_n=((8, T, D), BF),
        r1_n=((4, T, D), BF),
        rx_n=((2, T, D), BF),
        rz_n=((T, D), BF),
        mg=((T, D), F32),
        attg=((T, D), BF),
        cg_send=((8, T, W), BF),
        cg_all=((8, T, W), BF),
        pb_o=(grid + (D,), BF),
        r1_o=((4, 2, 2, B, D), BF),
        rx_o=((2, 2, 2, B, D), BF),
        rz_o=((2, 2, B, D), BF),
        go_s=((2, 2, B, D), BF),
        go_a=((2, B, D), BF),
        go_b=((B, D), BF),
        go_c=((B, D), BF),
        cg_sorted=((S, W), BF),
        dq=((S, W), F32),
        dk=((K, W), F32),
        dv=((K, W), F32),
        dqkv=((8, R, 3 * W), BF),
        gout_s=((2, 2, H4, D), BF),
        gout_a=((2, H4, D), BF),
        gout_b=((H4, D), BF),
        gout_c=((H4, D), BF),
        gin_s=(grid + (H,), BF),
        gin_a=((2, 4, 2, B, H), BF),
        gin_b=((4, 2, B, H), BF),
        gin_c=((4, 2, B, H), BF),
        gin_d=((8, B, H), BF),
        gin_e=((8, B, H), BF),
        gqkv_s=(grid + (3 * W,), BF),
        gqkv_a=((2, 4, 2, B, 3 * W), BF),
        gqkv_b=((4, 2, B, 3 * W), BF),
        gqkv_c=((4, 2, B, 3 * W), BF),
        gqkv_d=((8, B, 3 * W), BF),
        gqkv_e=((8, B, 3 * W), BF),
        vp=((8, 8, W), F32),
        vr=((3, 4, 8, W), F32),
        vs=((4, 8, W), F32),
        va=((8, 8, W), F32),
        bp=((4, 8, H4), F32),
        br=((3, 8, H4), F32),
        lo_s=((T, D), BF),
        ig_s=((T, D), BF),
    )


SEMS = 320


class Sender:
    def __init__(self, ssem, rsem):
        self.ssem, self.rsem, self.count, self.pending = ssem, rsem, 0, []

    def make(self, src, dst, target):
        at = self.count
        self.count += 1
        return pltpu.make_async_remote_copy(
            src_ref=src,
            dst_ref=dst,
            send_sem=self.ssem.at[at],
            recv_sem=self.rsem.at[at],
            device_id=target,
            device_id_type=MESH,
        )

    def local(self, src, dst):
        at = self.count
        self.count += 1
        copy = pltpu.make_async_copy(src, dst, self.rsem.at[at])
        copy.start()
        return copy

    def send(self, src, dst, target):
        copy = self.make(src, dst, target)
        copy.start()
        self.pending.append(copy)
        return copy

    def drain(self):
        for copy in self.pending:
            copy.wait_send()


class TeamGather:
    def __init__(self, tx, near, slot, ref):
        self.tx, self.near, self.slot, self.ref = tx, near, slot, ref
        self.sib, self.zn, self.xn, self.diag = [], {}, {}, {}

    def pass_on(self, rel, half, to):
        at = self.ref(self.slot(rel), half)
        return self.tx.send(at, at, self.near(to))

    def start(self, half):
        own = (0, 0, 0)
        self.zn[half] = self.pass_on(own, half, ZN)
        self.xn[half] = self.pass_on(own, half, XN)
        self.sib.append(self.pass_on(own, half, SIB))

    def forward(self, half):
        self.zn[half].wait_recv()
        self.diag[half] = self.pass_on(ZN, half, XN)
        self.sib.append(self.pass_on(ZN, half, SIB))

    def finish(self):
        for half in (0, 1):
            self.xn[half].wait_recv()
            self.sib.append(self.pass_on(XN, half, SIB))
        for half in (0, 1):
            self.diag[half].wait_recv()
            self.sib.append(self.pass_on((1, 1, 0), half, SIB))
        for copy in self.sib:
            copy.wait_recv()


class TeamScatter:
    def __init__(self, tx, near, slot, buf, first, cross, last, halves):
        self.tx, self.near, self.slot, self.buf = tx, near, slot, buf
        self.first, self.cross, self.last, self.halves = first, cross, last, halves
        self.sib, self.turned, self.ended = {}, [], []

    def push(self, order):
        rel = QUADS[order]
        src = self.buf(self.slot((rel[0], rel[1], 1)))
        self.sib[order] = self.tx.send(src, self.first.at[order], self.near(SIB))

    def add(self, order):
        self.sib[order].wait_recv()
        own = self.buf(self.slot(QUADS[order]))
        for half in self.halves:
            part, more = own.at[half], self.first.at[order].at[half]
            part[...] = (part[...].astype(F32) + more[...].astype(F32)).astype(BF)
            if order == 0:
                self.turned.append(self.tx.send(part, self.cross.at[0].at[half], self.near(XN)))
            if order == 1:
                self.ended.append(self.tx.send(part, self.cross.at[1].at[half], self.near(XN)))

    def turn(self):
        own = self.buf(self.slot(ZN))
        for half, copy in zip(self.halves, self.turned):
            copy.wait_recv()
            part, more = own.at[half], self.cross.at[0].at[half]
            part[...] = (part[...].astype(F32) + more[...].astype(F32)).astype(BF)
            self.ended.append(self.tx.send(part, self.last.at[half], self.near(ZN)))

    def total(self, own):
        for copy in self.ended:
            copy.wait_recv()
        return (
            self.buf(own)[...].astype(F32)
            + self.cross[1].astype(F32)
            + self.last[...].astype(F32)
        )


def layer_kernel(T, M, D, FF, share, *refs):
    names = IN_NAMES + OUT_NAMES + list(scratch_list(T, M, D, FF))
    ssem, rsem = refs[len(names) :]
    g = type("Refs", (), dict(zip(names, refs)))
    R, H, Q, W, S = T + M, FF // 8, D // 4, D // 8, 8 * T
    H4, B = H // 4, D // 32
    MK = 8 * M
    tx = Sender(ssem, rsem)

    b, d = lax.axis_index("blk"), lax.axis_index("dp")
    z, x, y, c = b // 2, b % 2, d // 2, d % 2
    zh, zl = z // 2, z % 2
    zx = 2 * zl + x
    p = 2 * zx + c
    e = 2 * zh + y

    def dev(zh, zl, x, y, c):
        return (4 * zh + 2 * zl + x, 2 * y + c)

    def near(rel):
        return dev(zh, (zl + rel[0]) % 2, (x + rel[1]) % 2, y, (c + rel[2]) % 2)

    def slot(rel):
        return 4 * ((zl + rel[0]) % 2) + 2 * ((x + rel[1]) % 2) + (c + rel[2]) % 2

    def far(rel):
        return dev((zh + rel[0]) % 2, zl, x, (y + rel[1]) % 2, c)

    partner = dev(c, zl, x, y, zh)
    partner_slot = 2 * zx + zh
    stays = c == zh
    moves = jnp.logical_not(stays)

    barrier = pltpu.get_barrier_semaphore()
    for rel in TEAM:
        pl.semaphore_signal(barrier, inc=1, device_id=near(rel), device_id_type=MESH)
    for rel in FAR:
        pl.semaphore_signal(barrier, inc=1, device_id=far(rel), device_id_type=MESH)

    @pl.when(moves)
    def _():
        pl.semaphore_signal(barrier, inc=1, device_id=partner, device_id_type=MESH)

    loads = [tx.local(w, g.f_qkv.at[i]) for i, w in enumerate((g.wq, g.wk, g.wv))]
    loads_o = tx.local(g.wo, g.f_o)
    loads_in = tx.local(g.win, g.f_in)
    loads_out = tx.local(g.wout, g.f_out)
    share_lane = lax.broadcasted_iota(jnp.int32, (8, W), 1) // share
    low = g.vec[...].astype(BF).astype(F32)
    spread = jnp.concatenate([low] * (W // share), axis=1)
    g.vg1[p] = jnp.where(share_lane == 2 * y + c, spread, 0.0)
    g.bslot[e] = jnp.broadcast_to(g.bias[...].astype(BF).astype(F32), (8, H4))
    for copy in loads:
        copy.wait()
    for q in range(8):
        for i in range(3):
            g.pq[q, :, i * W : (i + 1) * W] = g.f_qkv[i, :, q * W : (q + 1) * W].astype(BF)
    g.wqkv[zh, zx, y, c] = g.pq[p]
    loads_o.wait()
    g.w_o[zh, zx, y, c] = g.f_o[...].astype(BF)
    @pl.when(moves)
    def _():
        pl.semaphore_wait(barrier, 11)

    @pl.when(stays)
    def _():
        pl.semaphore_wait(barrier, 10)

    swaps = []

    def swap(src, dst_there, dst_here):
        copy = tx.make(src, dst_there, partner)
        here = pltpu.make_async_copy(src, dst_here, rsem.at[tx.count - 1])

        @pl.when(moves)
        def _():
            copy.start()

        @pl.when(stays)
        def _():
            here.start()

        swaps.append(copy)
        return copy

    def far_start(ref):
        at = ref(zh, y)
        return [tx.send(at, at, far(rel)) for rel in FAR[:2]]

    def far_forward(ref, copies):
        copies[0].wait_recv()
        at = ref(1 - zh, y)
        copies.append(tx.send(at, at, far((0, 1))))

    def far_finish(copies):
        for copy in copies[1:]:
            copy.wait_recv()

    def team_send(src, dst):
        return [tx.send(src(slot(rel)), dst, near(rel)) for rel in TEAM]

    def wait_all(copies):
        for copy in copies:
            copy.wait_recv()

    early = 32
    swap_m = swap(g.mem, g.xm, g.xm)
    swap_a = swap(g.x.at[:early], g.xt.at[:early], g.xt.at[:early])
    swap_b = swap(g.x.at[early:], g.xt.at[early:], g.xt.at[early:])
    vec_copies = [tx.send(g.vg1.at[p], g.vg1.at[p], near(rel)) for rel in TEAM]
    qkv_copies = team_send(lambda q: g.pq.at[q], g.wqkv.at[zh, zx, y, c])
    wait_all(vec_copies)
    for k in range(4):
        g.vg2[e, k] = g.vg1[2 * k] + g.vg1[2 * k + 1]
    vec_copies = [tx.send(g.vg2.at[e], g.vg2.at[e], far(rel)) for rel in FAR]
    vec_copies += [tx.send(g.bslot.at[e], g.bslot.at[e], far(rel)) for rel in FAR]
    wait_all(qkv_copies)
    qkv_at = lambda i, j: g.wqkv.at[i, :, j]
    qkv_copies = far_start(qkv_at)
    wo_at = lambda i, j: g.w_o.at[i, zx, j, c]
    wo_copies = far_start(wo_at)
    swap_c = swap(g.cot, g.cot_all.at[partner_slot], g.cot_all.at[p])
    loads_in.wait()
    for q in range(8):
        for k in range(4):
            at = (16 * (k // 2) + 4 * (q // 2) + 2 * (k % 2) + q % 2) * H4
            g.pi[q, :, k * H4 : (k + 1) * H4] = g.f_in[:, at : at + H4].astype(BF)
    g.w_in[zh, zx, y, c] = g.pi[p]
    loads_out.wait()
    g.w_out[zh, y] = g.f_out[...].astype(BF)
    wait_all(vec_copies)
    for k in range(8):
        group = g.vg2[2 * (k // 4), k % 4] + g.vg2[2 * (k // 4) + 1, k % 4]
        g.pg[k] = group
        g.prm[:, k * W : (k + 1) * W] = group
    prm = g.prm
    half_rows = R // 2
    n_gather = TeamGather(
        tx, near, slot, lambda q, h: g.n_all.at[q, pl.ds(h * half_rows, half_rows)]
    )

    def norm_rows(src, first, count, at):
        def step(i, _):
            rows = pl.ds(pl.multiple_of(first + i * 32, 32), 32)
            hat, _unused = norm_parts(src[rows, :].astype(F32))
            out = (hat * prm[0:1] + prm[1:2]).astype(BF)
            g.n_all[p, pl.ds(pl.multiple_of(at + i * 32, 32), 32), :] = out
            return 0

        lax.fori_loop(0, count // 32, step, 0)

    swap_m.wait_recv()
    norm_rows(g.xm, 0, M, 0)
    swap_a.wait_recv()
    norm_rows(g.xt, 0, early, M)
    n_gather.start(0)
    swap_b.wait_recv()
    norm_rows(g.xt, early, T - early, M + early)
    n_gather.start(1)
    win_copies = team_send(lambda q: g.pi.at[q], g.w_in.at[zh, zx, y, c])
    far_forward(qkv_at, qkv_copies)
    n_gather.forward(0)
    n_gather.forward(1)
    far_forward(wo_at, wo_copies)
    wait_all(win_copies)
    win_at = lambda i, j: g.w_in.at[i, :, j]
    win_copies = far_start(win_at)
    wout_at = lambda i, j: g.w_out.at[i, j]
    wout_copies = far_start(wout_at)
    n_gather.finish()
    far_finish(qkv_copies)
    wqkv = flat(g.wqkv[...].reshape(32, B, 3 * W))
    own_vec = g.pg[p]
    qkv_bias = jnp.concatenate(
        [own_vec[2:3], jnp.zeros((1, W), F32), own_vec[3:4]], axis=1
    )

    def project(i, _):
        rows = flat(g.n_all[pl.ds(2 * i, 2)])
        out = dot(rows, wqkv) + qkv_bias
        g.qkv[pl.ds(2 * i, 2)] = out.astype(BF).reshape(2, R, 3 * W)
        return 0

    lax.fori_loop(0, 4, project, 0)
    far_finish(wo_copies)
    wo_gather = TeamGather(
        tx, near, slot, lambda q, h: g.w_o.at[h, q // 2, :, q % 2]
    )
    swap_c.wait_recv()
    half_tok = T // 2
    cot_gather = TeamGather(
        tx, near, slot, lambda q, h: g.cot_all.at[q, pl.ds(h * half_tok, half_tok)]
    )
    for gather in (wo_gather, cot_gather):
        gather.start(0)
        gather.start(1)
    place = [
        g.order[4 * qc + 2 * qz + qx] for qz in (0, 1) for qx in (0, 1) for qc in (0, 1)
    ]

    def pick(blocks, wanted):
        out = blocks[0]
        for block, (left, right) in zip(blocks[1:], wanted[1:]):
            out = jnp.where(jnp.full(out.shape, left, jnp.int32) == right, block, out)
        return out

    def to_sorted(load, store):
        def step(i, _):
            at = pl.multiple_of(i * 16, 16)
            blocks = [load(q, at).astype(F32) for q in range(8)]
            for j in range(8):
                store(j, at, pick(blocks, [(place[q], j) for q in range(8)]))
            return 0

        lax.fori_loop(0, T // 16, step, 0)

    def from_sorted(load, store):
        def step(i, _):
            at = pl.multiple_of(i * 16, 16)
            blocks = [load(j, at).astype(F32) for j in range(8)]
            for q in range(8):
                store(q, at, pick(blocks, [(place[q], j) for j in range(8)]))
            return 0

        lax.fori_loop(0, T // 16, step, 0)

    def store_qkv(j, at, rows):
        g.qs[pl.ds(j * T + at, 16), :] = (rows[:, :W] * 0.125).astype(BF)
        g.kk[pl.ds(MK + j * T + at, 16), :] = rows[:, W : 2 * W].astype(BF)
        g.vv[pl.ds(MK + j * T + at, 16), :] = rows[:, 2 * W :].astype(BF)

    to_sorted(lambda q, at: g.qkv[q, pl.ds(M + at, 16), :], store_qkv)
    for j in range(8):
        g.kk[j * M : (j + 1) * M, :] = g.qkv[j, :M, W : 2 * W]
        g.vv[j * M : (j + 1) * M, :] = g.qkv[j, :M, 2 * W :]
    N = 2 * T
    lane = lax.broadcasted_iota(jnp.int32, (N, W), 1)
    head_lanes = [lane < W // 2, lane >= W // 2]
    below = lax.broadcasted_iota(jnp.int32, (N, N), 1) <= lax.broadcasted_iota(
        jnp.int32, (N, N), 0
    )

    def only(value, h):
        return jnp.where(head_lanes[h], value, jnp.zeros_like(value))

    def attend(i):
        rows = slice(i * N, (i + 1) * N)
        past = MK + i * N
        end = past + N
        q_rows = g.qs[rows, :]
        parts = []
        for h in range(2):
            qh = only(q_rows, h)
            s0 = dot_nt(qh, g.kk[:past, :])
            s1 = dot_nt(qh, g.kk[past:end, :])
            s1 = jnp.where(below, s1, -1e30)
            top = jnp.maximum(
                jnp.max(s0, axis=1, keepdims=True), jnp.max(s1, axis=1, keepdims=True)
            )
            e0 = jnp.exp(s0 - top)
            e1 = jnp.exp(s1 - top)
            total = jnp.sum(e0, axis=1, keepdims=True) + jnp.sum(e1, axis=1, keepdims=True)
            scale = 1.0 / total
            w0 = (e0 * scale).astype(BF)
            w1 = (e1 * scale).astype(BF)
            g.wts[h, rows, :past] = w0
            g.wts[h, rows, past:end] = w1
            parts.append(dot(w0, g.vv[:past, :]) + dot(w1, g.vv[past:end, :]))
        g.ctx[rows, :] = jnp.where(head_lanes[0], parts[0], parts[1])

    attend(0)
    attend(1)
    attend(2)
    wo_gather.forward(0)
    wo_gather.forward(1)
    attend(3)
    def store_ctx(q, at, rows):
        g.ctx_send[q, pl.ds(at, 16), :] = rows.astype(BF)

    from_sorted(lambda j, at: g.ctx[pl.ds(j * T + at, 16), :], store_ctx)
    ctx_copies = team_send(lambda q: g.ctx_send.at[q], g.ctx_own.at[p])
    g.ctx_own[p] = g.ctx_send[p]
    cot_gather.forward(0)
    cot_gather.forward(1)
    far_forward(win_at, win_copies)
    wo_gather.finish()
    wait_all(ctx_copies)
    for q in range(8):
        g.ctx2d[:, q * W : (q + 1) * W] = g.ctx_own[q]
    w_o = lambda: flat(g.w_o[...].reshape(32, B, D))
    g.mid[...] = dot(g.ctx2d[...], w_o()) + g.xt[...].astype(F32) + prm[4:5]
    n2_gather = TeamGather(
        tx, near, slot, lambda q, h: g.n2_all.at[q, pl.ds(h * half_tok, half_tok)]
    )

    def norm_mid(i, _):
        rows = pl.ds(pl.multiple_of(i * 32, 32), 32)
        hat, _unused = norm_parts(g.mid[rows, :])
        g.n2_all[p, rows, :] = (hat * prm[5:6] + prm[6:7]).astype(BF)
        return 0

    for half in (0, 1):
        lax.fori_loop(half * (half_tok // 32), (half + 1) * (half_tok // 32), norm_mid, 0)
        n2_gather.start(half)
    far_forward(wout_at, wout_copies)
    n2_gather.forward(0)
    n2_gather.forward(1)
    cot_gather.finish()
    n2_gather.finish()
    far_finish(win_copies)
    far_finish(wout_copies)
    tok_halves = [pl.ds(h * half_tok, half_tok) for h in (0, 1)]
    hidden_bias = jnp.concatenate([g.bslot[k, 0:1, :] for k in range(4)], axis=1)
    out_sum = TeamScatter(
        tx, near, slot, lambda q: g.pb_a.at[q], g.r1_a, g.rx_a, g.rz_a, tok_halves
    )
    n2_sum = TeamScatter(
        tx, near, slot, lambda q: g.pb_b.at[q], g.r1_b, g.rx_b, g.rz_b, tok_halves
    )
    for order in range(4):
        pair = 2 * (slot(QUADS[order]) // 2)
        w_in = flat(g.w_in[...].reshape(32, B, H))
        w_out = g.w_out[...].reshape(H, D)
        inner = dot(flat(g.n2_all[pl.ds(pair, 2)]), w_in) + hidden_bias
        act, slope = gelu_parts(inner)
        act = act.astype(BF)
        act_grad = dot_nt(flat(g.cot_all[pl.ds(pair, 2)]), w_out)
        inner_grad = (act_grad * slope).astype(BF)
        at = pl.ds(pl.multiple_of(pair * T, 2 * T), 2 * T)
        g.inner[at, :] = inner_grad
        for k in range(4):
            g.act[k, at, :] = act[:, k * H4 : (k + 1) * H4]
        g.pb_b[pl.ds(pair, 2)] = dot_nt(inner_grad, w_in).astype(BF).reshape(2, T, D)
        n2_sum.push(order)
        g.pb_a[pl.ds(pair, 2)] = dot(act, w_out).astype(BF).reshape(2, T, D)
        out_sum.push(order)
        if order:
            n2_sum.add(order - 1)
    n2_sum.add(3)
    cot = lambda: flat(g.cot_all[...])
    for j in (1 - y, y):
        for k in range(2):
            g.gout_s[k, j] = dot_tn(g.act[2 * k + j], cot()).astype(BF)
    gout_copy = tx.send(g.gout_s.at[:, 1 - y], g.gout_a, far((0, 1)))
    n2_sum.turn()
    out_sum.add(0)
    for k in range(4):
        grad = dot_tn(flat(g.n2_all[:, :, k * Q : (k + 1) * Q]), g.inner[...])
        cut = slice(2 * (k % 2), 2 * (k % 2) + 2)
        g.gin_s[k // 2, cut] = grad.astype(BF).reshape(2, 2, 2, B, H)
    gin_copy = tx.send(g.gin_s.at[:, :, 1 - y], g.gin_a, far((0, 1)))
    inner_sum = col_sum(g.inner[...])
    for k in range(4):
        g.bp[k] = jnp.broadcast_to(inner_sum[:, k * H4 : (k + 1) * H4], (8, H4))
    gb_copies = []
    for i, rel in enumerate(FAR):
        to = 2 * ((zh + rel[0]) % 2) + (y + rel[1]) % 2
        gb_copies.append(tx.send(g.bp.at[to], g.br.at[i], far(rel)))
    g.mg[...] = n2_sum.total(p)
    def norm_two_back(i, sums):
        rows = pl.ds(pl.multiple_of(i * 32, 32), 32)
        up = g.mg[rows, :]
        hat, scale = norm_parts(g.mid[rows, :])
        pull = up * prm[5:6]
        mean = jnp.mean(pull, axis=-1, keepdims=True)
        along_hat = jnp.mean(pull * hat, axis=-1, keepdims=True)
        cot_rows = g.cot_all[p, rows, :].astype(F32)
        out = cot_rows + scale * (pull - mean - hat * along_hat)
        low = out.astype(BF)
        g.mg[rows, :] = out
        g.attg[rows, :] = low
        return (
            sums[0] + col_sum(up * hat),
            sums[1] + col_sum(up),
            sums[2] + col_sum(low),
            sums[3] + col_sum(cot_rows),
        )

    zero_row = jnp.zeros((1, D), F32)
    gain_two, shift_two, bias_o, bias_out = lax.fori_loop(
        0, T // 32, norm_two_back, (zero_row, zero_row, zero_row, zero_row)
    )
    attg = g.attg[...]
    cg = dot_nt(attg, w_o()).astype(BF)
    for q in range(8):
        g.cg_send[q] = cg[:, q * W : (q + 1) * W]
    cg_copies = team_send(lambda q: g.cg_send.at[q], g.cg_all.at[p])
    g.cg_all[p] = g.cg_send[p]
    for order in (1, 2, 3):
        out_sum.add(order)
    for k in range(4):
        grad = dot_tn(g.ctx2d[:, k * Q : (k + 1) * Q], attg)
        cut = slice(2 * (k % 2), 2 * (k % 2) + 2)
        g.pb_o[k // 2, cut] = grad.astype(BF).reshape(2, 2, 2, B, D)
    o_sum = TeamScatter(
        tx, near, slot, lambda q: g.pb_o.at[:, q // 2, :, q % 2], g.r1_o, g.rx_o, g.rz_o, [0, 1]
    )
    for order in range(4):
        o_sum.push(order)

    def far_turn(copy, own, got, out, last):
        copy.wait_recv()
        out[...] = (own(1 - zh)[...].astype(F32) + got[1 - zh].astype(F32)).astype(BF)
        return tx.send(out, last, far((1, 0)))

    def far_total(copy, own, got, last):
        copy.wait_recv()
        return own(zh)[...].astype(F32) + got[zh].astype(F32) + last[...].astype(F32)

    gout_own = lambda i: g.gout_s.at[i, y]
    gin_own = lambda i: g.gin_s.at[i, :, y]
    gqkv_own = lambda i: g.gqkv_s.at[i, :, y]
    go_own = lambda i: g.go_s.at[i, y]
    wait_all(cg_copies)

    def store_cg(j, at, rows):
        g.cg_sorted[pl.ds(j * T + at, 16), :] = rows.astype(BF)

    to_sorted(lambda q, at: g.cg_all[q, pl.ds(at, 16), :], store_cg)
    g.dk[...] = jnp.zeros_like(g.dk)
    g.dv[...] = jnp.zeros_like(g.dv)

    def attend_back(i):
        rows = slice(i * N, (i + 1) * N)
        end = MK + (i + 1) * N
        cg_rows = g.cg_sorted[rows, :]
        q_rows = g.qs[rows, :]
        product = cg_rows.astype(F32) * g.ctx[rows, :]
        parts = []
        for h in range(2):
            qh, ch = only(q_rows, h), only(cg_rows, h)
            delta = jnp.sum(only(product, h), axis=1, keepdims=True)
            w = g.wts[h, rows, :end]
            pull = dot_nt(ch, g.vv[:end, :])
            ds = (w.astype(F32) * (pull - delta)).astype(BF)
            parts.append(dot(ds, g.kk[:end, :]))
            g.dk[:end, :] += dot_tn(ds, qh)
            g.dv[:end, :] += dot_tn(w, ch)
        g.dq[rows, :] = jnp.where(head_lanes[0], parts[0], parts[1]) * 0.125

    attend_back(0)
    attend_back(1)
    gout_copy = far_turn(gout_copy, gout_own, g.gout_a, g.gout_b, g.gout_c)
    attend_back(2)
    out_sum.turn()
    attend_back(3)
    def load_grads(j, at):
        keys = pl.ds(MK + j * T + at, 16)
        return jnp.concatenate(
            [g.dq[pl.ds(j * T + at, 16), :], g.dk[keys, :], g.dv[keys, :]], axis=1
        )

    def store_grads(q, at, rows):
        g.dqkv[q, pl.ds(M + at, 16), :] = rows.astype(BF)

    from_sorted(load_grads, store_grads)
    for q in range(8):
        mt = slice(q * M, (q + 1) * M)
        g.dqkv[q, :M, :W] = jnp.zeros((M, W), BF)
        g.dqkv[q, :M, W : 2 * W] = g.dk[mt, :].astype(BF)
        g.dqkv[q, :M, 2 * W :] = g.dv[mt, :].astype(BF)
    n_sum = TeamScatter(
        tx, near, slot, lambda q: g.pb_n.at[q], g.r1_n, g.rx_n, g.rz_n, tok_halves
    )
    for order in range(4):
        pair = 2 * (slot(QUADS[order]) // 2)
        rows = flat(g.dqkv[pl.ds(pair, 2), M:, :])
        w = flat(g.wqkv[...].reshape(32, B, 3 * W))
        g.pb_n[pl.ds(pair, 2)] = dot_nt(rows, w).astype(BF).reshape(2, T, D)
        n_sum.push(order)
        if order:
            n_sum.add(order - 1)
    n_sum.add(3)
    gin_copy = far_turn(gin_copy, gin_own, g.gin_a, g.gin_b, g.gin_c)
    g.vp[...] = jnp.zeros_like(g.vp)
    qkv_sum = jnp.zeros((1, 3 * W), F32)
    for q in range(8):
        qkv_sum = qkv_sum + col_sum(g.dqkv[q])
    qkv_sum8 = jnp.broadcast_to(qkv_sum, (8, 3 * W))
    ones = jnp.ones((8, 3 * W), F32)
    for k in range(4):
        grad = dot_tn(flat(g.n_all[:, :, k * Q : (k + 1) * Q]), flat(g.dqkv[...]))
        cut = slice(2 * (k % 2), 2 * (k % 2) + 2)
        g.gqkv_s[k // 2, cut] = grad.astype(BF).reshape(2, 2, 2, B, 3 * W)
        w = flat(g.wqkv[k // 2, cut].reshape(8, B, 3 * W)).astype(F32)
        gains = dot_nt(ones, grad * w, EXACT)
        shifts = dot_nt(qkv_sum8, w, EXACT)
        for i in range(2):
            at = slice(i * W, (i + 1) * W)
            shift = shifts[0:1, at]
            vec = g.pg[2 * k + i]
            g.vp[2 * k + i, 0:1, :] = (gains[0:1, at] - vec[1:2] * shift) / vec[0:1]
            g.vp[2 * k + i, 1:2, :] = shift
    gqkv_copy = tx.send(g.gqkv_s.at[:, :, 1 - y], g.gqkv_a, far((0, 1)))
    n_sum.turn()
    g.vp[p, 2:3, :] = qkv_sum[:, :W]
    g.vp[p, 3:4, :] = qkv_sum[:, 2 * W :]
    for k in range(8):
        at = slice(k * W, (k + 1) * W)
        g.vp[k, 4:5, :] = bias_o[:, at]
        g.vp[k, 5:6, :] = gain_two[:, at]
        g.vp[k, 6:7, :] = shift_two[:, at]
        g.vp[k, 7:8, :] = bias_out[:, at]
    vec_copies = []
    for i, rel in enumerate(FAR):
        to = pl.ds(4 * ((zh + rel[0]) % 2), 4)
        vec_copies.append(tx.send(g.vp.at[to], g.vr.at[i], far(rel)))
    for order in range(4):
        o_sum.add(order)
    lo = out_sum.total(p) + g.mid[...] + prm[7:8]
    g.lo_s[...] = lo.astype(BF)
    swap_lo = swap(g.lo_s, g.lo, g.lo)
    gqkv_copy = far_turn(gqkv_copy, gqkv_own, g.gqkv_a, g.gqkv_b, g.gqkv_c)
    o_sum.turn()
    g.gout[...] = far_total(gout_copy, gout_own, g.gout_a, g.gout_c)
    g.gin_d[...] = flat_team(far_total(gin_copy, gin_own, g.gin_a, g.gin_c))
    gin_copies = team_send(lambda q: g.gin_d.at[q], g.gin_e.at[p])
    g.gin_e[p] = g.gin_d[p]
    wait_all(gb_copies)
    g.gbin[...] = g.bp[e] + g.br[0] + g.br[1] + g.br[2]
    wait_all(vec_copies)
    g.vs[...] = g.vp[pl.ds(4 * zh, 4)] + g.vr[0] + g.vr[1] + g.vr[2]
    vec_copies = team_send(lambda q: g.vs.at[q // 2], g.va.at[p])
    g.va[p] = g.vs[zx]
    g.mid[...] = n_sum.total(p)

    def norm_one_back(i, _):
        rows = pl.ds(pl.multiple_of(i * 32, 32), 32)
        hat, scale = norm_parts(g.xt[rows, :].astype(F32))
        pull = g.mid[rows, :] * prm[0:1]
        mean = jnp.mean(pull, axis=-1, keepdims=True)
        along_hat = jnp.mean(pull * hat, axis=-1, keepdims=True)
        out = g.mg[rows, :] + scale * (pull - mean - hat * along_hat)
        g.ig_s[rows, :] = out.astype(BF)
        return 0

    lax.fori_loop(0, T // 32, norm_one_back, 0)
    swap_ig = swap(g.ig_s, g.ig, g.ig)
    g.gqkv_d[...] = flat_team(far_total(gqkv_copy, gqkv_own, g.gqkv_a, g.gqkv_c))
    gqkv_copies = team_send(lambda q: g.gqkv_d.at[q], g.gqkv_e.at[p])
    g.gqkv_e[p] = g.gqkv_d[p]
    g.go_s[...] = o_sum.total(p).astype(BF)
    go_copy = tx.send(g.go_s.at[:, 1 - y], g.go_a, far((0, 1)))
    wait_all(gin_copies)
    for q in range(8):
        for k in range(4):
            at = (16 * (k // 2) + 4 * (q // 2) + 2 * (k % 2) + q % 2) * H4
            g.gin[:, at : at + H4] = g.gin_e[q, :, k * H4 : (k + 1) * H4].astype(F32)
    go_copy = far_turn(go_copy, go_own, g.go_a, g.go_b, g.go_c)
    wait_all(vec_copies)
    total = g.va[0]
    for q in range(1, 8):
        total = total + g.va[q]
    g.gvec[...] = total
    wait_all(gqkv_copies)
    for q in range(8):
        for i, out in enumerate((g.gq, g.gk, g.gv)):
            out[:, q * W : (q + 1) * W] = g.gqkv_e[q, :, i * W : (i + 1) * W].astype(F32)
    g.go[...] = far_total(go_copy, go_own, g.go_a, g.go_c)
    swap_lo.wait_recv()
    swap_ig.wait_recv()
    tx.drain()

    @pl.when(moves)
    def _():
        for copy in swaps:
            copy.wait_send()


def flat_team(value):
    return value.astype(BF).reshape((8,) + value.shape[2:])


def run_layer(layer_input, memory, cotangent, block_order, w_query, w_key, w_value, w_output, w_in, w_out, vectors, b_in):
    T, D = layer_input.shape[1:]
    M = memory.shape[1]
    FF = w_in.shape[1]
    W = D // 8
    share = vectors.shape[1]
    shapes = scratch_list(T, M, D, FF)
    vmem = pl.BlockSpec(memory_space=pltpu.VMEM)
    smem = pl.BlockSpec(memory_space=pltpu.SMEM)
    hbm = pl.BlockSpec(memory_space=pl.ANY)
    outs = pl.pallas_call(
        functools.partial(layer_kernel, T, M, D, FF, share),
        out_shape=(
            jax.ShapeDtypeStruct((T, D), BF),
            jax.ShapeDtypeStruct((T, D), BF),
            jax.ShapeDtypeStruct(w_query.shape, F32),
            jax.ShapeDtypeStruct(w_key.shape, F32),
            jax.ShapeDtypeStruct(w_value.shape, F32),
            jax.ShapeDtypeStruct(w_output.shape, F32),
            jax.ShapeDtypeStruct(w_in.shape, F32),
            jax.ShapeDtypeStruct(w_out.shape, F32),
            jax.ShapeDtypeStruct((8, W), F32),
            jax.ShapeDtypeStruct((8, b_in.shape[0]), F32),
        ),
        in_specs=[hbm, hbm, hbm, smem] + [hbm] * 6 + [vmem] * 2,
        out_specs=[vmem] * 10,
        scratch_shapes=[pltpu.VMEM(shape, kind) for shape, kind in shapes.values()]
        + [pltpu.SemaphoreType.DMA((SEMS,)), pltpu.SemaphoreType.DMA((SEMS,))],
        compiler_params=pltpu.CompilerParams(
            collective_id=0, has_side_effects=True, vmem_limit_bytes=63 * 2**20
        ),
    )(layer_input[0], memory[0], cotangent[0], block_order, w_query, w_key, w_value, w_output, w_in, w_out, vectors, b_in[None])
    lo, ig, gq, gk, gv, go, gin, gout, gvec, gbin = outs
    gvec = lax.dynamic_slice(gvec, (0, lax.axis_index("dp") * share), (8, share))
    return (lo[None], ig.astype(F32)[None], gq, gk, gv, go, gin, gout, gvec, gbin[0])


masked_value = -1e30


def passed_along(block, axis, distance):
    devices = range(lax.axis_size(axis))
    route = [((i - distance) % len(devices), i) for i in devices]
    return lax.ppermute(block, axis, route)


def layer_norm(values, gain, shift):
    center = values - jnp.mean(values, axis=-1, keepdims=True)
    spread = jnp.mean(center * center, axis=-1, keepdims=True)
    return center * lax.rsqrt(spread + 1e-05) * gain + shift


def contract_rows(left, right):
    return lax.dot_general(
        left, right, (((0,), (0,)), ((), ())), preferred_element_type=jnp.float32
    )


def times_transposed(left, right):
    return lax.dot_general(
        left, right, (((1,), (1,)), ((), ())), preferred_element_type=jnp.float32
    )


def split_heads(matrix, heads):
    return matrix.reshape(matrix.shape[0], heads, matrix.shape[1] // heads)


def score_block(query_heads, key_rows):
    key_heads = split_heads(key_rows, query_heads.shape[1])
    return (
        jnp.einsum("qhd,khd->hqk", query_heads, key_heads, preferred_element_type=jnp.float32)
        * 0.125
    )


def lookup_block(order, device):
    return jnp.sum(jnp.where(jnp.arange(order.shape[0]) == device, order, 0))


def split_piece(piece, rows_dev, mem_rows):
    shards = piece.shape[0] // rows_dev
    blocks = piece.reshape(shards, rows_dev, piece.shape[1])
    memory_part = blocks[:, :mem_rows].reshape(shards * mem_rows, piece.shape[1])
    token_part = blocks[:, mem_rows:].reshape(shards * (rows_dev - mem_rows), piece.shape[1])
    return (shards, memory_part, token_part)


def piece_positions(order, shards, tok_rows):
    shard_ids = jnp.arange(shards)
    hits = shard_ids[:, None] == jnp.arange(order.shape[0])[None, :]
    starts = jnp.sum(jnp.where(hits, order[None, :], 0), axis=1)
    positions = (starts[:, None] * tok_rows + jnp.arange(tok_rows)[None, :]).reshape(
        shards * tok_rows
    )
    return (starts, positions)


def softmax_stats(carry, scores):
    running, total = carry
    top = jnp.maximum(running, jnp.max(scores, axis=2))
    total = total * jnp.exp(running - top) + jnp.sum(jnp.exp(scores - top[:, :, None]), axis=2)
    return (top, total)


def per_device(
    layer_input,
    memory,
    cotangent,
    block_order,
    w_query,
    w_key,
    w_value,
    w_output,
    w_in,
    w_out,
    vectors,
    b_in,
):
    bf16 = jnp.bfloat16
    gathered = (
        lax.all_gather(w_query.astype(bf16), ("blk", "dp"), axis=0, tiled=True),
        lax.all_gather(w_key.astype(bf16), ("blk", "dp"), axis=0, tiled=True),
        lax.all_gather(w_value.astype(bf16), ("blk", "dp"), axis=0, tiled=True),
        lax.all_gather(w_output.astype(bf16), ("blk", "dp"), axis=0, tiled=True),
        lax.all_gather(w_in.astype(bf16), ("blk", "dp"), axis=0, tiled=True),
        lax.all_gather(w_out.astype(bf16), ("blk", "dp"), axis=0, tiled=True),
        lax.all_gather(vectors.astype(bf16), ("blk", "dp"), axis=1, tiled=True),
        lax.all_gather(b_in.astype(bf16), ("blk", "dp"), axis=0, tiled=True),
    )
    (
        query_full,
        key_full,
        value_full,
        output_full,
        inner_full,
        outer_full,
        vector_full,
        inner_low,
    ) = gathered
    params = vector_full.astype(jnp.float32)
    inner_shift = inner_low.astype(jnp.float32)
    heads = HEADS
    tokens = layer_input[0].astype(jnp.float32)
    recalled = memory[0].astype(jnp.float32)
    tok_rows = tokens.shape[0]
    mem_rows = recalled.shape[0]
    rows_dev = tok_rows + mem_rows
    width = tokens.shape[1]
    blocks_total = lax.axis_size("blk")
    here = lax.axis_index("blk")
    own_block = lookup_block(block_order, here)
    query_pos = own_block * tok_rows + jnp.arange(tok_rows)
    both_rows = jnp.concatenate([recalled, tokens], axis=0)
    normed = layer_norm(both_rows, params[0], params[1]).astype(bf16)
    normed_tok = normed[mem_rows:]
    queries = (
        jnp.dot(normed_tok, query_full, preferred_element_type=jnp.float32) + params[2]
    ).astype(bf16)
    keys_all = jnp.dot(normed, key_full, preferred_element_type=jnp.float32).astype(bf16)
    values_all = (
        jnp.dot(normed, value_full, preferred_element_type=jnp.float32) + params[3]
    ).astype(bf16)
    query_heads = split_heads(queries, heads)

    def causal(scores, key_pos):
        return jnp.where(key_pos[None, None, :] <= query_pos[None, :, None], scores, masked_value)

    start_stats = (
        jnp.full((heads, tok_rows), masked_value, jnp.float32),
        jnp.zeros((heads, tok_rows), jnp.float32),
    )
    carry = start_stats
    shards, memory_part, token_part = split_piece(
        lax.all_gather(keys_all, "blk", axis=0, tiled=True), rows_dev, mem_rows
    )
    starts, token_pos = piece_positions(block_order, shards, tok_rows)
    carry = softmax_stats(carry, score_block(query_heads, memory_part))

    def with_tokens(state):
        return softmax_stats(state, causal(score_block(query_heads, token_part), token_pos))

    def without_tokens(state):
        return state

    running, total = lax.cond(jnp.any(starts <= own_block), with_tokens, without_tokens, carry)
    log_total = running + jnp.log(total)

    def value_part(context, part, key_pos):
        scores = score_block(query_heads, part[:, :width])
        if key_pos is not None:
            scores = causal(scores, key_pos)
        weights = jnp.exp(scores - log_total[:, :, None]).astype(bf16)
        return context + jnp.einsum(
            "hqk,khd->qhd",
            weights,
            split_heads(part[:, width:], heads),
            preferred_element_type=jnp.float32,
        )

    key_values = jnp.concatenate([keys_all, values_all], axis=1)
    context = jnp.zeros((tok_rows, heads, width // heads), jnp.float32)
    shards, memory_part, add_token_part = split_piece(
        lax.all_gather(key_values, "blk", axis=0, tiled=True), rows_dev, mem_rows
    )
    starts, add_token_pos = piece_positions(block_order, shards, tok_rows)
    context = value_part(context, memory_part, None)

    def with_tokens(state):
        return value_part(state, add_token_part, add_token_pos)

    def without_tokens(state):
        return state

    context = lax.cond(jnp.any(starts <= own_block), with_tokens, without_tokens, context)
    context_low = context.reshape(tok_rows, width).astype(bf16)
    attended = jnp.dot(context_low, output_full, preferred_element_type=jnp.float32) + params[4]
    middle = tokens + attended
    normed_two = layer_norm(middle, params[5], params[6]).astype(bf16)
    inner = jnp.dot(normed_two, inner_full, preferred_element_type=jnp.float32) + inner_shift
    activated = jax.nn.gelu(inner, approximate=True).astype(bf16)
    result = middle + jnp.dot(activated, outer_full, preferred_element_type=jnp.float32) + params[7]
    output = result.astype(bf16)
    upstream = cotangent[0]
    upstream_full = upstream.astype(jnp.float32)
    grad_outer = contract_rows(activated, upstream)
    grad_outer_bias = jnp.sum(upstream_full, axis=0)
    act_grad = times_transposed(upstream, outer_full)
    _, gelu_back = jax.vjp(functools.partial(jax.nn.gelu, approximate=True), inner)
    inner_grad = gelu_back(act_grad)[0].astype(bf16)
    grad_inner = contract_rows(normed_two, inner_grad)
    grad_inner_bias = jnp.sum(inner_grad.astype(jnp.float32), axis=0)
    normed_two_grad = times_transposed(inner_grad, inner_full)
    _, norm_two_back = jax.vjp(layer_norm, middle, params[5], params[6])
    middle_part, grad_gain_two, grad_shift_two = norm_two_back(normed_two_grad)
    middle_grad = upstream_full + middle_part
    attended_grad = middle_grad.astype(bf16)
    grad_output = contract_rows(context_low, attended_grad)
    grad_output_bias = jnp.sum(attended_grad.astype(jnp.float32), axis=0)
    context_grad = times_transposed(attended_grad, output_full).astype(bf16)
    context_heads = split_heads(context_grad, heads)
    delta = jnp.einsum("qhd,qhd->hq", context_heads.astype(jnp.float32), context)

    def attend_back(queries_grad, part, key_pos):
        count = part.shape[0]
        key_heads = split_heads(part[:, :width], heads)
        value_heads = split_heads(part[:, width:], heads)
        scores = score_block(query_heads, part[:, :width])
        if key_pos is not None:
            scores = causal(scores, key_pos)
        exact = jnp.exp(scores - log_total[:, :, None])
        weight_low = exact.astype(bf16)
        weight_grad = jnp.einsum(
            "qhd,khd->hqk", context_heads, value_heads, preferred_element_type=jnp.float32
        )
        score_grad = (exact * (weight_grad - delta[:, :, None])).astype(bf16)
        queries_grad = (
            queries_grad
            + jnp.einsum("hqk,khd->qhd", score_grad, key_heads, preferred_element_type=jnp.float32)
            * 0.125
        )
        key_grad = (
            jnp.einsum("hqk,qhd->khd", score_grad, query_heads, preferred_element_type=jnp.float32)
            * 0.125
        )
        value_grad = jnp.einsum(
            "hqk,qhd->khd", weight_low, context_heads, preferred_element_type=jnp.float32
        )
        return (
            queries_grad,
            jnp.concatenate(
                [key_grad.reshape(count, width), value_grad.reshape(count, width)], axis=1
            ),
        )

    def visit(queries_grad, travelling, travel_grad, anchor):
        anchor_block = lookup_block(block_order, anchor)
        queries_grad, memory_grad = attend_back(queries_grad, travelling[:mem_rows], None)
        token_pos = anchor_block * tok_rows + jnp.arange(tok_rows)

        def with_tokens(state):
            return attend_back(state, travelling[mem_rows:], token_pos)

        def without_tokens(state):
            return (state, jnp.zeros((tok_rows, 2 * width), jnp.float32))

        queries_grad, token_grad = lax.cond(
            anchor_block <= own_block, with_tokens, without_tokens, queries_grad
        )
        return (queries_grad, travel_grad + jnp.concatenate([memory_grad, token_grad], axis=0))

    def pass_grads(values):
        return passed_along(values.astype(jnp.bfloat16), "blk", 1).astype(values.dtype)

    queries_grad, travel_grad = visit(
        jnp.zeros((tok_rows, heads, width // heads), jnp.float32),
        key_values,
        jnp.zeros((rows_dev, 2 * width), jnp.float32),
        here,
    )

    def turn(step, state):
        queries_grad, travelling, travel_grad = state
        travelling = passed_along(travelling, "blk", 1)
        travel_grad = pass_grads(travel_grad)
        anchor = (here - step) % blocks_total
        queries_grad, travel_grad = visit(queries_grad, travelling, travel_grad, anchor)
        return (queries_grad, travelling, travel_grad)

    queries_grad, travelling, travel_grad = lax.fori_loop(
        1, blocks_total, turn, (queries_grad, key_values, travel_grad)
    )
    travel_grad = pass_grads(travel_grad)
    pair_grad = travel_grad.astype(bf16)
    key_grad = pair_grad[:, :width]
    value_grad = pair_grad[:, width:]
    query_grad = queries_grad.reshape(tok_rows, width).astype(bf16)
    grad_query = contract_rows(normed_tok, query_grad)
    grad_query_bias = jnp.sum(query_grad.astype(jnp.float32), axis=0)
    grad_key = contract_rows(normed, key_grad)
    grad_value = contract_rows(normed, value_grad)
    grad_value_bias = jnp.sum(value_grad.astype(jnp.float32), axis=0)
    normed_grad = times_transposed(key_grad, key_full) + times_transposed(value_grad, value_full)
    query_part = times_transposed(query_grad, query_full)
    normed_grad = normed_grad + jnp.concatenate(
        [jnp.zeros((mem_rows, width), jnp.float32), query_part], axis=0
    )
    _, norm_one_back = jax.vjp(layer_norm, both_rows, params[0], params[1])
    rows_grad, grad_gain_one, grad_shift_one = norm_one_back(normed_grad)
    input_grad = middle_grad + rows_grad[mem_rows:]
    vector_grad = jnp.stack(
        [
            grad_gain_one,
            grad_shift_one,
            grad_query_bias,
            grad_value_bias,
            grad_output_bias,
            grad_gain_two,
            grad_shift_two,
            grad_outer_bias,
        ]
    )
    out_query, out_key, out_value, out_output, out_inner, out_outer, out_vectors, out_bias = (
        lax.psum_scatter(grad_query, ("blk", "dp"), scatter_dimension=0, tiled=True),
        lax.psum_scatter(grad_key, ("blk", "dp"), scatter_dimension=0, tiled=True),
        lax.psum_scatter(grad_value, ("blk", "dp"), scatter_dimension=0, tiled=True),
        lax.psum_scatter(grad_output, ("blk", "dp"), scatter_dimension=0, tiled=True),
        lax.psum_scatter(grad_inner, ("blk", "dp"), scatter_dimension=0, tiled=True),
        lax.psum_scatter(grad_outer, ("blk", "dp"), scatter_dimension=0, tiled=True),
        lax.psum_scatter(vector_grad, ("blk", "dp"), scatter_dimension=1, tiled=True),
        lax.psum_scatter(grad_inner_bias, ("blk", "dp"), scatter_dimension=0, tiled=True),
    )
    return (
        output[None],
        input_grad[None],
        out_query,
        out_key,
        out_value,
        out_output,
        out_inner,
        out_outer,
        out_vectors,
        out_bias,
    )


def solution(mesh):
    rows = P("dp", "blk", None)
    shard = P(("blk", "dp"), None)
    in_specs = (rows, rows, rows, P()) + (shard,) * 6 + (P(None, ("blk", "dp")), P(("blk", "dp")))
    out_specs = (rows, rows) + (shard,) * 6 + (P(None, ("blk", "dp")), P(("blk", "dp")))
    planes = mesh.shape["blk"] == 8 and mesh.shape["dp"] == 4
    return jax.shard_map(
        run_layer if planes else per_device,
        mesh=mesh,
        in_specs=in_specs,
        out_specs=out_specs,
        check_vma=False,
    )
```

```python
import functools

import jax
import jax.numpy as jnp
from jax import lax
from jax.experimental import pallas as pl
from jax.experimental.pallas import tpu as pltpu
from jax.sharding import PartitionSpec as P

HEADS = 16
BF = jnp.bfloat16
F32 = jnp.float32
MESH = pl.DeviceIdType.MESH
EXACT = lax.Precision.HIGHEST


def dot(a, b):
    return lax.dot_general(a, b, (((1,), (0,)), ((), ())), preferred_element_type=F32)


def dot_nt(a, b, precision=None):
    return lax.dot_general(
        a, b, (((1,), (1,)), ((), ())), preferred_element_type=F32, precision=precision
    )


def dot_tn(a, b):
    return lax.dot_general(a, b, (((0,), (0,)), ((), ())), preferred_element_type=F32)


def flat(value):
    return value.reshape(-1, value.shape[-1])


def col_sum(value):
    return jnp.sum(value.astype(F32), axis=0, keepdims=True)


def norm_parts(rows):
    center = rows - jnp.mean(rows, axis=-1, keepdims=True)
    spread = jnp.mean(center * center, axis=-1, keepdims=True)
    scale = lax.rsqrt(spread + 1e-05)
    return center * scale, scale


def gelu_parts(v):
    square = v * v
    t = jnp.tanh(0.7978845608 * v * (1.0 + 0.044715 * square))
    half = 0.5 * (1.0 + t)
    slope = half + 0.5 * v * (1.0 - t * t) * (0.7978845608 * (1.0 + 3 * 0.044715 * square))
    return v * half, slope


IN_NAMES = ["x", "mem", "cot", "order", "wq", "wk", "wv", "wo", "win", "wout", "vec", "bias"]
OUT_NAMES = ["lo", "ig", "gq", "gk", "gv", "go", "gin", "gout", "gvec", "gbin"]
TEAM = [(1, 1, 1), (1, 1, 0), (1, 0, 1), (1, 0, 0), (0, 1, 1), (0, 1, 0), (0, 0, 1)]
FAR = [(1, 0), (0, 1), (1, 1)]
QUADS = [(1, 1, 0), (0, 1, 0), (1, 0, 0), (0, 0, 0)]
SIB, XN, ZN = (0, 0, 1), (0, 1, 0), (1, 0, 0)


def scratch_list(T, M, D, FF):
    R = T + M
    H = FF // 8
    H4 = H // 4
    W = D // 8
    B = D // 32
    S = 8 * T
    K = 8 * R
    grid = (2, 4, 2, 2, B)
    return dict(
        f_qkv=((3, B, D), F32),
        f_o=((B, D), F32),
        f_in=((B, FF), F32),
        f_out=((H4, D), F32),
        n_all=((8, R, D), BF),
        raw=((8, R, D), BF),
        cot_all=((8, T, D), BF),
        n2_all=((8, T, D), BF),
        pq=((8, B, 3 * W), BF),
        pi=((8, B, H), BF),
        wqkv=(grid + (3 * W,), BF),
        w_in=(grid + (H,), BF),
        w_out=((2, 2, H4, D), BF),
        w_o=(grid + (D,), BF),
        vg1=((8, 8, W), F32),
        vg2=((4, 4, 8, W), F32),
        pg=((8, 8, W), F32),
        bslot=((4, 8, H4), F32),
        prm=((8, D), F32),
        qkv=((8, R, 3 * W), BF),
        qs=((S, W), BF),
        kk=((K, W), BF),
        vv=((K, W), BF),
        wts=((2, S, K), BF),
        ctx=((S, W), F32),
        ctx_send=((8, T, W), BF),
        ctx_own=((8, T, W), BF),
        ctx2d=((T, D), BF),
        mid=((T, D), F32),
        act=((4, S, H4), BF),
        inner=((S, H), BF),
        pb_a=((8, T, D), BF),
        r1_a=((4, T, D), BF),
        rx_a=((2, T, D), BF),
        rz_a=((T, D), BF),
        pb_b=((8, T, D), BF),
        r1_b=((4, T, D), BF),
        rx_b=((2, T, D), BF),
        rz_b=((T, D), BF),
        pb_n=((8, T, D), BF),
        r1_n=((4, T, D), BF),
        rx_n=((2, T, D), BF),
        rz_n=((T, D), BF),
        mg=((T, D), F32),
        attg=((T, D), BF),
        cg_send=((8, T, W), BF),
        cg_all=((8, T, W), BF),
        pb_o=(grid + (D,), BF),
        r1_o=((4, 2, 2, B, D), BF),
        rx_o=((2, 2, 2, B, D), BF),
        rz_o=((2, 2, B, D), BF),
        go_s=((2, 2, B, D), BF),
        go_a=((2, B, D), BF),
        go_b=((B, D), BF),
        go_c=((B, D), BF),
        cg_sorted=((S, W), BF),
        dq=((S, W), F32),
        dk=((K, W), F32),
        dv=((K, W), F32),
        dqkv=((8, R, 3 * W), BF),
        gout_s=((2, 2, H4, D), BF),
        gout_a=((2, H4, D), BF),
        gout_b=((H4, D), BF),
        gout_c=((H4, D), BF),
        gin_s=(grid + (H,), BF),
        gin_a=((2, 4, 2, B, H), BF),
        gin_b=((4, 2, B, H), BF),
        gin_c=((4, 2, B, H), BF),
        gin_d=((8, B, H), BF),
        gin_e=((8, B, H), BF),
        gqkv_s=(grid + (3 * W,), BF),
        gqkv_a=((2, 4, 2, B, 3 * W), BF),
        gqkv_b=((4, 2, B, 3 * W), BF),
        gqkv_c=((4, 2, B, 3 * W), BF),
        gqkv_d=((8, B, 3 * W), BF),
        gqkv_e=((8, B, 3 * W), BF),
        vp=((8, 8, W), F32),
        vr=((3, 4, 8, W), F32),
        vs=((4, 8, W), F32),
        va=((8, 8, W), F32),
        bp=((4, 8, H4), F32),
        br=((3, 8, H4), F32),
        lo_s=((T, D), BF),
        ig_s=((T, D), BF),
    )


SEMS = 320


class Sender:
    def __init__(self, ssem, rsem):
        self.ssem, self.rsem, self.count, self.pending = ssem, rsem, 0, []

    def make(self, src, dst, target):
        at = self.count
        self.count += 1
        return pltpu.make_async_remote_copy(
            src_ref=src,
            dst_ref=dst,
            send_sem=self.ssem.at[at],
            recv_sem=self.rsem.at[at],
            device_id=target,
            device_id_type=MESH,
        )

    def local(self, src, dst):
        at = self.count
        self.count += 1
        copy = pltpu.make_async_copy(src, dst, self.rsem.at[at])
        copy.start()
        return copy

    def plan(self, src, dst, target):
        copy = self.make(src, dst, target)
        self.pending.append(copy)
        return copy

    def send(self, src, dst, target):
        copy = self.plan(src, dst, target)
        copy.start()
        return copy

    def drain(self):
        for copy in self.pending:
            copy.wait_send()


class TeamGather:
    def __init__(self, tx, near, slot, ref):
        def plan(rel, to):
            ats = [ref(slot(rel), half) for half in (0, 1)]
            return [tx.plan(at, at, near(to)) for at in ats]

        self.zn, self.xn = plan((0, 0, 0), ZN), plan((0, 0, 0), XN)
        self.diag = plan(ZN, XN)
        self.sib = {rel: plan(rel, SIB) for rel in QUADS}

    def start(self, half):
        self.zn[half].start()
        self.xn[half].start()
        self.sib[(0, 0, 0)][half].start()

    def forward(self):
        for half in (0, 1):
            self.zn[half].wait_recv()
            self.diag[half].start()
            self.sib[ZN][half].start()

    def pass_xn(self):
        for half in (0, 1):
            self.xn[half].wait_recv()
            self.sib[XN][half].start()

    def pass_diag(self):
        for half in (0, 1):
            self.diag[half].wait_recv()
            self.sib[(1, 1, 0)][half].start()

    def wait_sib(self, rel):
        for copy in self.sib[rel]:
            copy.wait_recv()

    def finish(self):
        self.pass_xn()
        self.pass_diag()
        for rel in QUADS:
            self.wait_sib(rel)


class FarGather:
    def __init__(self, tx, far, zh, y, ref):
        own, passed = ref(zh, y), ref(1 - zh, y)
        self.over_z = tx.plan(own, own, far((1, 0)))
        self.over_y = tx.plan(own, own, far((0, 1)))
        self.passed = tx.plan(passed, passed, far((0, 1)))

    def start(self):
        self.over_z.start()
        self.over_y.start()

    def forward(self):
        self.over_z.wait_recv()
        self.passed.start()

    def finish(self):
        self.over_y.wait_recv()
        self.passed.wait_recv()


class TeamScatter:
    def __init__(self, tx, near, slot, buf, first, cross, last, halves):
        self.tx, self.near, self.slot, self.buf = tx, near, slot, buf
        self.first, self.cross, self.last, self.halves = first, cross, last, halves
        self.sib, self.turned, self.ended = {}, [], []

    def push(self, order):
        rel = QUADS[order]
        src = self.buf(self.slot((rel[0], rel[1], 1)))
        self.sib[order] = self.tx.send(src, self.first.at[order], self.near(SIB))

    def add(self, order):
        self.sib[order].wait_recv()
        own = self.buf(self.slot(QUADS[order]))
        for half in self.halves:
            part, more = own.at[half], self.first.at[order].at[half]
            part[...] = (part[...].astype(F32) + more[...].astype(F32)).astype(BF)
            if order == 0:
                self.turned.append(self.tx.send(part, self.cross.at[0].at[half], self.near(XN)))
            if order == 1:
                self.ended.append(self.tx.send(part, self.cross.at[1].at[half], self.near(XN)))

    def turn(self):
        own = self.buf(self.slot(ZN))
        for half, copy in zip(self.halves, self.turned):
            copy.wait_recv()
            part, more = own.at[half], self.cross.at[0].at[half]
            part[...] = (part[...].astype(F32) + more[...].astype(F32)).astype(BF)
            self.ended.append(self.tx.send(part, self.last.at[half], self.near(ZN)))

    def total(self, own):
        for copy in self.ended:
            copy.wait_recv()
        return (
            self.buf(own)[...].astype(F32)
            + self.cross[1].astype(F32)
            + self.last[...].astype(F32)
        )


class FarSum:
    def __init__(self, tx, far, zh, y, own, first, mid, last):
        self.tx, self.far, self.zh, self.y, self.own = tx, far, zh, y, own
        self.first, self.mid, self.last, self.copies = first, mid, last, []

    def start(self, half):
        src = self.own(half, 1 - self.y)
        self.copies.append(self.tx.send(src, self.first.at[half], self.far((0, 1))))

    def both(self, half):
        return self.own(half, self.y)[...].astype(F32) + self.first[half].astype(F32)

    def turn(self):
        self.copies[0].wait_recv()
        self.mid[...] = self.both(1 - self.zh).astype(BF)
        self.ended = self.tx.send(self.mid, self.last, self.far((1, 0)))

    def total(self):
        self.copies[1].wait_recv()
        self.ended.wait_recv()
        return self.both(self.zh) + self.last[...].astype(F32)


def layer_kernel(T, M, D, FF, share, *refs):
    names = IN_NAMES + OUT_NAMES + list(scratch_list(T, M, D, FF))
    ssem, rsem = refs[len(names) :]
    g = type("Refs", (), dict(zip(names, refs)))
    R, H, Q, W, S = T + M, FF // 8, D // 4, D // 8, 8 * T
    H4, B = H // 4, D // 32
    MK = 8 * M
    tx = Sender(ssem, rsem)

    b, d = lax.axis_index("blk"), lax.axis_index("dp")
    z, x, y, c = b // 2, b % 2, d // 2, d % 2
    zh, zl = z // 2, z % 2
    zx = 2 * zl + x
    p = 2 * zx + c
    e = 2 * zh + y

    def dev(zh, zl, x, y, c):
        return (4 * zh + 2 * zl + x, 2 * y + c)

    def near(rel):
        return dev(zh, (zl + rel[0]) % 2, (x + rel[1]) % 2, y, (c + rel[2]) % 2)

    def slot(rel):
        return 4 * ((zl + rel[0]) % 2) + 2 * ((x + rel[1]) % 2) + (c + rel[2]) % 2

    def far(rel):
        return dev((zh + rel[0]) % 2, zl, x, (y + rel[1]) % 2, c)

    partner = dev(c, zl, x, y, zh)
    partner_slot = 2 * zx + zh
    stays = c == zh
    moves = jnp.logical_not(stays)
    outer = zl == zh
    inner = jnp.logical_not(outer)

    barrier = pltpu.get_barrier_semaphore()
    for rel in TEAM:
        pl.semaphore_signal(barrier, inc=1, device_id=near(rel), device_id_type=MESH)
    for rel in FAR:
        pl.semaphore_signal(barrier, inc=1, device_id=far(rel), device_id_type=MESH)

    @pl.when(moves)
    def _():
        pl.semaphore_signal(barrier, inc=1, device_id=partner, device_id_type=MESH)

    loads = [tx.local(w, g.f_qkv.at[i]) for i, w in enumerate((g.wq, g.wk, g.wv))]
    loads_o = tx.local(g.wo, g.f_o)
    loads_in = tx.local(g.win, g.f_in)
    loads_out = tx.local(g.wout, g.f_out)
    share_lane = lax.broadcasted_iota(jnp.int32, (8, W), 1) // share
    low = g.vec[...].astype(BF).astype(F32)
    spread = jnp.concatenate([low] * (W // share), axis=1)
    g.vg1[p] = jnp.where(share_lane == 2 * y + c, spread, 0.0)
    g.bslot[e] = jnp.broadcast_to(g.bias[...].astype(BF).astype(F32), (8, H4))
    loads_o.wait()
    g.w_o[zh, zx, y, c] = g.f_o[...].astype(BF)
    for copy in loads:
        copy.wait()
    for q in range(8):
        for i in range(3):
            g.pq[q, :, i * W : (i + 1) * W] = g.f_qkv[i, :, q * W : (q + 1) * W].astype(BF)
    g.wqkv[zh, zx, y, c] = g.pq[p]
    loads_in.wait()
    for q in range(8):
        for k in range(4):
            at = (16 * (k // 2) + 4 * (q // 2) + 2 * (k % 2) + q % 2) * H4
            g.pi[q, :, k * H4 : (k + 1) * H4] = g.f_in[:, at : at + H4].astype(BF)
    g.w_in[zh, zx, y, c] = g.pi[p]
    loads_out.wait()
    g.w_out[zh, y] = g.f_out[...].astype(BF)
    @pl.when(moves)
    def _():
        pl.semaphore_wait(barrier, 11)

    @pl.when(stays)
    def _():
        pl.semaphore_wait(barrier, 10)

    swaps = []

    class Swap:
        def __init__(self, src, dst_there, dst_here):
            self.copy = tx.make(src, dst_there, partner)
            self.here = pltpu.make_async_copy(src, dst_here, rsem.at[tx.count - 1])
            swaps.append(self.copy)

        def start(self):
            pl.when(moves)(self.copy.start)
            pl.when(stays)(self.here.start)

        def wait_recv(self):
            self.copy.wait_recv()

    def swap(src, dst_there, dst_here):
        copy = Swap(src, dst_there, dst_here)
        copy.start()
        return copy

    def team_send(src, dst):
        return [tx.send(src(slot(rel)), dst, near(rel)) for rel in TEAM]

    def wait_all(copies):
        for copy in copies:
            copy.wait_recv()

    vec_copies = [tx.send(g.vg1.at[p], g.vg1.at[p], near(rel)) for rel in TEAM]
    qkv_copies = team_send(lambda q: g.pq.at[q], g.wqkv.at[zh, zx, y, c])
    wo_far = FarGather(tx, far, zh, y, lambda i, j: g.w_o.at[i, zx, j, c])
    wo_far.start()
    half_rows, half_tok = R // 2, T // 2
    early = half_rows - M
    raw_here, raw_there = g.raw.at[p], g.raw.at[partner_slot]
    cuts = [
        (g.mem, pl.ds(0, M)),
        (g.x.at[pl.ds(0, early)], pl.ds(M, early)),
        (g.x.at[pl.ds(early, T - early)], pl.ds(half_rows, half_rows)),
    ]
    swap_m, swap_a, swap_b = [
        swap(src, raw_there.at[to], raw_here.at[to]) for src, to in cuts
    ]
    swap_c = Swap(g.cot, g.cot_all.at[partner_slot], g.cot_all.at[p])
    n_gather = TeamGather(
        tx, near, slot, lambda q, h: g.raw.at[q, pl.ds(h * half_rows, half_rows)]
    )
    cot_gather = TeamGather(
        tx, near, slot, lambda q, h: g.cot_all.at[q, pl.ds(h * half_tok, half_tok)]
    )
    wo_gather = TeamGather(
        tx, near, slot, lambda q, h: g.w_o.at[h, q // 2, :, q % 2]
    )
    qkv_far = FarGather(tx, far, zh, y, lambda i, j: g.wqkv.at[i, :, j])
    win_far = FarGather(tx, far, zh, y, lambda i, j: g.w_in.at[i, :, j])
    wout_far = FarGather(tx, far, zh, y, lambda i, j: g.w_out.at[i, j])

    def start_rows():
        swap_m.wait_recv()
        swap_a.wait_recv()
        n_gather.start(0)
        swap_b.wait_recv()
        n_gather.start(1)

    def start_cot():
        swap_c.wait_recv()
        cot_gather.start(0)
        cot_gather.start(1)

    @pl.when(stays)
    def _():
        swap_c.here.start()
        start_rows()
        start_cot()

    wait_all(vec_copies)
    for k in range(4):
        g.vg2[e, k] = g.vg1[2 * k] + g.vg1[2 * k + 1]
    vec_copies = [tx.send(g.vg2.at[e], g.vg2.at[e], far(rel)) for rel in FAR]
    vec_copies += [tx.send(g.bslot.at[e], g.bslot.at[e], far(rel)) for rel in FAR]
    wait_all(qkv_copies)
    qkv_far.start()
    wo_far.forward()

    @pl.when(stays)
    def _():
        n_gather.forward()
        cot_gather.forward()

    @pl.when(moves)
    def _():
        start_rows()

    wo_far.finish()
    wo_gather.start(0)
    wo_gather.start(1)

    wait_all(vec_copies)
    for k in range(8):
        group = g.vg2[2 * (k // 4), k % 4] + g.vg2[2 * (k // 4) + 1, k % 4]
        g.pg[k] = group
        g.prm[:, k * W : (k + 1) * W] = group
    prm = g.prm

    def norm_slot(rel, core):
        at = 2 * (slot(rel) // 2) + core

        def step(i, _):
            rows = pl.ds(pl.multiple_of(i * 32, 32), 32)
            hat, _unused = norm_parts(g.raw[at, rows, :].astype(F32))
            g.n_all[at, rows, :] = (hat * prm[0:1] + prm[1:2]).astype(BF)
            return 0

        lax.fori_loop(0, R // 32, step, 0)

    def early_rows(rel, step):
        @pl.when(stays)
        def _():
            step()

        @pl.when(moves)
        def _():
            n_gather.wait_sib(rel)

        norm_slot(rel, zh)

    def late_rows(rel, step):
        @pl.when(moves)
        def _():
            step()

        @pl.when(stays)
        def _():
            n_gather.wait_sib(rel)

        norm_slot(rel, 1 - zh)

    def nothing():
        pass

    early_rows((0, 0, 0), nothing)
    early_rows(ZN, nothing)
    early_rows(XN, n_gather.pass_xn)
    early_rows((1, 1, 0), n_gather.pass_diag)

    @pl.when(moves)
    def _():
        n_gather.forward()

    qkv_far.forward()
    late_rows((0, 0, 0), nothing)
    late_rows(ZN, nothing)

    wout_far.start()

    @pl.when(moves)
    def _():
        swap_c.copy.start()

    late_rows(XN, n_gather.pass_xn)
    wo_gather.forward()
    win_copies = team_send(lambda q: g.pi.at[q], g.w_in.at[zh, zx, y, c])
    qkv_far.finish()
    wqkv = lambda: flat(g.wqkv[...].reshape(32, B, 3 * W))
    own_vec = g.pg[p]
    qkv_bias = jnp.concatenate(
        [own_vec[2:3], jnp.zeros((1, W), F32), own_vec[3:4]], axis=1
    )

    def project(rel):
        pair = pl.ds(2 * (slot(rel) // 2), 2)
        out = dot(flat(g.n_all[pair]), wqkv()) + qkv_bias
        g.qkv[pair] = out.astype(BF).reshape(2, R, 3 * W)

    for rel in (SIB, ZN, XN):
        project(rel)
    late_rows((1, 1, 0), n_gather.pass_diag)
    project((1, 1, 0))
    place = [
        g.order[4 * qc + 2 * qz + qx] for qz in (0, 1) for qx in (0, 1) for qc in (0, 1)
    ]

    def pick(blocks, wanted):
        out = blocks[0]
        for block, (left, right) in zip(blocks[1:], wanted[1:]):
            out = jnp.where(jnp.full(out.shape, left, jnp.int32) == right, block, out)
        return out

    def to_sorted(load, store):
        def step(i, _):
            at = pl.multiple_of(i * 16, 16)
            blocks = [load(q, at).astype(F32) for q in range(8)]
            for j in range(8):
                store(j, at, pick(blocks, [(place[q], j) for q in range(8)]))
            return 0

        lax.fori_loop(0, T // 16, step, 0)

    def from_sorted(load, store):
        def step(i, _):
            at = pl.multiple_of(i * 16, 16)
            blocks = [load(j, at).astype(F32) for j in range(8)]
            for q in range(8):
                store(q, at, pick(blocks, [(place[q], j) for j in range(8)]))
            return 0

        lax.fori_loop(0, T // 16, step, 0)

    def store_qkv(j, at, rows):
        g.qs[pl.ds(j * T + at, 16), :] = (rows[:, :W] * 0.125).astype(BF)
        g.kk[pl.ds(MK + j * T + at, 16), :] = rows[:, W : 2 * W].astype(BF)
        g.vv[pl.ds(MK + j * T + at, 16), :] = rows[:, 2 * W :].astype(BF)

    to_sorted(lambda q, at: g.qkv[q, pl.ds(M + at, 16), :], store_qkv)
    for j in range(8):
        g.kk[j * M : (j + 1) * M, :] = g.qkv[j, :M, W : 2 * W]
        g.vv[j * M : (j + 1) * M, :] = g.qkv[j, :M, 2 * W :]
    N = 2 * T
    lane = lax.broadcasted_iota(jnp.int32, (N, W), 1)
    head_lanes = [lane < W // 2, lane >= W // 2]
    below = lax.broadcasted_iota(jnp.int32, (N, N), 1) <= lax.broadcasted_iota(
        jnp.int32, (N, N), 0
    )

    def only(value, h):
        return jnp.where(head_lanes[h], value, jnp.zeros_like(value))

    def attend(i):
        rows = slice(i * N, (i + 1) * N)
        past = MK + i * N
        end = past + N
        q_rows = g.qs[rows, :]
        parts = []
        for h in range(2):
            qh = only(q_rows, h)
            s0 = dot_nt(qh, g.kk[:past, :])
            s1 = dot_nt(qh, g.kk[past:end, :])
            s1 = jnp.where(below, s1, -1e30)
            top = jnp.maximum(
                jnp.max(s0, axis=1, keepdims=True), jnp.max(s1, axis=1, keepdims=True)
            )
            e0 = jnp.exp(s0 - top)
            e1 = jnp.exp(s1 - top)
            total = jnp.sum(e0, axis=1, keepdims=True) + jnp.sum(e1, axis=1, keepdims=True)
            scale = 1.0 / total
            w0 = (e0 * scale).astype(BF)
            w1 = (e1 * scale).astype(BF)
            g.wts[h, rows, :past] = w0
            g.wts[h, rows, past:end] = w1
            parts.append(dot(w0, g.vv[:past, :]) + dot(w1, g.vv[past:end, :]))
        g.ctx[rows, :] = jnp.where(head_lanes[0], parts[0], parts[1])

    wait_all(win_copies)

    @pl.when(inner)
    def _():
        win_far.start()

    attend(0)
    attend(1)

    @pl.when(moves)
    def _():
        start_cot()

    wout_far.forward()
    attend(2)
    attend(3)
    def store_ctx(q, at, rows):
        g.ctx_send[q, pl.ds(at, 16), :] = rows.astype(BF)

    from_sorted(lambda j, at: g.ctx[pl.ds(j * T + at, 16), :], store_ctx)
    ctx_copies = team_send(lambda q: g.ctx_send.at[q], g.ctx_own.at[p])
    g.ctx_own[p] = g.ctx_send[p]
    @pl.when(outer)
    def _():
        win_far.start()

    wo_gather.finish()

    @pl.when(moves)
    def _():
        cot_gather.forward()

    @pl.when(outer)
    def _():
        win_far.forward()

    wait_all(ctx_copies)
    for q in range(8):
        g.ctx2d[:, q * W : (q + 1) * W] = g.ctx_own[q]
    w_o = lambda: flat(g.w_o[...].reshape(32, B, D))
    g.mid[...] = dot(g.ctx2d[...], w_o()) + g.raw[p, M:, :].astype(F32) + prm[4:5]
    n2_gather = TeamGather(
        tx, near, slot, lambda q, h: g.n2_all.at[q, pl.ds(h * half_tok, half_tok)]
    )

    def norm_mid(i, _):
        rows = pl.ds(pl.multiple_of(i * 32, 32), 32)
        hat, _unused = norm_parts(g.mid[rows, :])
        g.n2_all[p, rows, :] = (hat * prm[5:6] + prm[6:7]).astype(BF)
        return 0

    for half in (0, 1):
        lax.fori_loop(half * (half_tok // 32), (half + 1) * (half_tok // 32), norm_mid, 0)
        n2_gather.start(half)
    n2_gather.forward()

    @pl.when(inner)
    def _():
        win_far.forward()

    n2_gather.pass_xn()
    cot_gather.finish()
    n2_gather.pass_diag()
    for rel in QUADS:
        n2_gather.wait_sib(rel)
    win_far.finish()
    wout_far.finish()
    tok_halves = [pl.ds(h * half_tok, half_tok) for h in (0, 1)]
    hidden_bias = jnp.concatenate([g.bslot[k, 0:1, :] for k in range(4)], axis=1)
    out_sum = TeamScatter(
        tx, near, slot, lambda q: g.pb_a.at[q], g.r1_a, g.rx_a, g.rz_a, tok_halves
    )
    n2_sum = TeamScatter(
        tx, near, slot, lambda q: g.pb_b.at[q], g.r1_b, g.rx_b, g.rz_b, tok_halves
    )
    for order in range(4):
        pair = 2 * (slot(QUADS[order]) // 2)
        w_in = flat(g.w_in[...].reshape(32, B, H))
        w_out = g.w_out[...].reshape(H, D)
        inner = dot(flat(g.n2_all[pl.ds(pair, 2)]), w_in) + hidden_bias
        act, slope = gelu_parts(inner)
        act = act.astype(BF)
        act_grad = dot_nt(flat(g.cot_all[pl.ds(pair, 2)]), w_out)
        inner_grad = (act_grad * slope).astype(BF)
        at = pl.ds(pl.multiple_of(pair * T, 2 * T), 2 * T)
        g.inner[at, :] = inner_grad
        for k in range(4):
            g.act[k, at, :] = act[:, k * H4 : (k + 1) * H4]
        g.pb_b[pl.ds(pair, 2)] = dot_nt(inner_grad, w_in).astype(BF).reshape(2, T, D)
        n2_sum.push(order)
        g.pb_a[pl.ds(pair, 2)] = dot(act, w_out).astype(BF).reshape(2, T, D)
        out_sum.push(order)
        if order:
            n2_sum.add(order - 1)
    n2_sum.add(3)
    out_sum.add(0)
    out_sum.add(1)
    cot = lambda: flat(g.cot_all[...])
    for j in (1 - y, y):
        for k in range(2):
            g.gout_s[k, j] = dot_tn(g.act[2 * k + j], cot()).astype(BF)
    gout_own = lambda i, j: g.gout_s.at[i, j]
    gout_sum = FarSum(tx, far, zh, y, gout_own, g.gout_a, g.gout_b, g.gout_c)
    gout_sum.start(1 - zh)
    n2_sum.turn()
    out_sum.add(2)
    out_sum.add(3)
    for k in range(4):
        grad = dot_tn(flat(g.n2_all[:, :, k * Q : (k + 1) * Q]), g.inner[...])
        cut = slice(2 * (k % 2), 2 * (k % 2) + 2)
        g.gin_s[k // 2, cut] = grad.astype(BF).reshape(2, 2, 2, B, H)
    gin_own = lambda i, j: g.gin_s.at[i, :, j]
    gin_sum = FarSum(tx, far, zh, y, gin_own, g.gin_a, g.gin_b, g.gin_c)
    gin_sum.start(1 - zh)
    gout_sum.start(zh)
    gin_sum.start(zh)
    inner_sum = col_sum(g.inner[...])
    for k in range(4):
        g.bp[k] = jnp.broadcast_to(inner_sum[:, k * H4 : (k + 1) * H4], (8, H4))
    gb_copies = []
    for i, rel in enumerate(FAR):
        to = 2 * ((zh + rel[0]) % 2) + (y + rel[1]) % 2
        gb_copies.append(tx.send(g.bp.at[to], g.br.at[i], far(rel)))
    gout_sum.turn()
    g.mg[...] = n2_sum.total(p)
    def norm_two_back(i, sums):
        rows = pl.ds(pl.multiple_of(i * 32, 32), 32)
        up = g.mg[rows, :]
        hat, scale = norm_parts(g.mid[rows, :])
        pull = up * prm[5:6]
        mean = jnp.mean(pull, axis=-1, keepdims=True)
        along_hat = jnp.mean(pull * hat, axis=-1, keepdims=True)
        cot_rows = g.cot_all[p, rows, :].astype(F32)
        out = cot_rows + scale * (pull - mean - hat * along_hat)
        low = out.astype(BF)
        g.mg[rows, :] = out
        g.attg[rows, :] = low
        return (
            sums[0] + col_sum(up * hat),
            sums[1] + col_sum(up),
            sums[2] + col_sum(low),
            sums[3] + col_sum(cot_rows),
        )

    zero_row = jnp.zeros((1, D), F32)
    gain_two, shift_two, bias_o, bias_out = lax.fori_loop(
        0, T // 32, norm_two_back, (zero_row, zero_row, zero_row, zero_row)
    )
    attg = g.attg[...]
    cg = dot_nt(attg, w_o()).astype(BF)
    for q in range(8):
        g.cg_send[q] = cg[:, q * W : (q + 1) * W]
    cg_copies = team_send(lambda q: g.cg_send.at[q], g.cg_all.at[p])
    g.cg_all[p] = g.cg_send[p]
    out_sum.turn()
    gin_sum.turn()
    for k in range(4):
        grad = dot_tn(g.ctx2d[:, k * Q : (k + 1) * Q], attg)
        cut = slice(2 * (k % 2), 2 * (k % 2) + 2)
        g.pb_o[k // 2, cut] = grad.astype(BF).reshape(2, 2, 2, B, D)
    o_sum = TeamScatter(
        tx, near, slot, lambda q: g.pb_o.at[:, q // 2, :, q % 2], g.r1_o, g.rx_o, g.rz_o, [0, 1]
    )
    for order in range(4):
        o_sum.push(order)

    wait_all(cg_copies)

    def store_cg(j, at, rows):
        g.cg_sorted[pl.ds(j * T + at, 16), :] = rows.astype(BF)

    to_sorted(lambda q, at: g.cg_all[q, pl.ds(at, 16), :], store_cg)
    g.dk[...] = jnp.zeros_like(g.dk)
    g.dv[...] = jnp.zeros_like(g.dv)

    def attend_back(i):
        rows = slice(i * N, (i + 1) * N)
        end = MK + (i + 1) * N
        cg_rows = g.cg_sorted[rows, :]
        q_rows = g.qs[rows, :]
        product = cg_rows.astype(F32) * g.ctx[rows, :]
        parts = []
        for h in range(2):
            qh, ch = only(q_rows, h), only(cg_rows, h)
            delta = jnp.sum(only(product, h), axis=1, keepdims=True)
            w = g.wts[h, rows, :end]
            pull = dot_nt(ch, g.vv[:end, :])
            ds = (w.astype(F32) * (pull - delta)).astype(BF)
            parts.append(dot(ds, g.kk[:end, :]))
            g.dk[:end, :] += dot_tn(ds, qh)
            g.dv[:end, :] += dot_tn(w, ch)
        g.dq[rows, :] = jnp.where(head_lanes[0], parts[0], parts[1]) * 0.125

    attend_back(0)
    attend_back(1)
    for order in range(4):
        o_sum.add(order)
    attend_back(2)
    attend_back(3)
    def load_grads(j, at):
        keys = pl.ds(MK + j * T + at, 16)
        return jnp.concatenate(
            [g.dq[pl.ds(j * T + at, 16), :], g.dk[keys, :], g.dv[keys, :]], axis=1
        )

    def store_grads(q, at, rows):
        g.dqkv[q, pl.ds(M + at, 16), :] = rows.astype(BF)

    from_sorted(load_grads, store_grads)
    for q in range(8):
        mt = slice(q * M, (q + 1) * M)
        g.dqkv[q, :M, :W] = jnp.zeros((M, W), BF)
        g.dqkv[q, :M, W : 2 * W] = g.dk[mt, :].astype(BF)
        g.dqkv[q, :M, 2 * W :] = g.dv[mt, :].astype(BF)
    n_sum = TeamScatter(
        tx, near, slot, lambda q: g.pb_n.at[q], g.r1_n, g.rx_n, g.rz_n, tok_halves
    )
    for order in range(4):
        pair = 2 * (slot(QUADS[order]) // 2)
        rows = flat(g.dqkv[pl.ds(pair, 2), M:, :])
        g.pb_n[pl.ds(pair, 2)] = dot_nt(rows, wqkv()).astype(BF).reshape(2, T, D)
        n_sum.push(order)
        if order:
            n_sum.add(order - 1)
    n_sum.add(3)
    g.vp[...] = jnp.zeros_like(g.vp)
    qkv_sum = jnp.zeros((1, 3 * W), F32)
    for q in range(8):
        qkv_sum = qkv_sum + col_sum(g.dqkv[q])
    qkv_sum8 = jnp.broadcast_to(qkv_sum, (8, 3 * W))
    ones = jnp.ones((8, 3 * W), F32)
    for k in range(4):
        grad = dot_tn(flat(g.n_all[:, :, k * Q : (k + 1) * Q]), flat(g.dqkv[...]))
        cut = slice(2 * (k % 2), 2 * (k % 2) + 2)
        g.gqkv_s[k // 2, cut] = grad.astype(BF).reshape(2, 2, 2, B, 3 * W)
        w = flat(g.wqkv[k // 2, cut].reshape(8, B, 3 * W)).astype(F32)
        gains = dot_nt(ones, grad * w, EXACT)
        shifts = dot_nt(qkv_sum8, w, EXACT)
        for i in range(2):
            at = slice(i * W, (i + 1) * W)
            shift = shifts[0:1, at]
            vec = g.pg[2 * k + i]
            g.vp[2 * k + i, 0:1, :] = (gains[0:1, at] - vec[1:2] * shift) / vec[0:1]
            g.vp[2 * k + i, 1:2, :] = shift
    gqkv_own = lambda i, j: g.gqkv_s.at[i, :, j]
    gqkv_sum = FarSum(tx, far, zh, y, gqkv_own, g.gqkv_a, g.gqkv_b, g.gqkv_c)
    gqkv_sum.start(1 - zh)
    gqkv_sum.start(zh)
    n_sum.turn()
    g.vp[p, 2:3, :] = qkv_sum[:, :W]
    g.vp[p, 3:4, :] = qkv_sum[:, 2 * W :]
    for k in range(8):
        at = slice(k * W, (k + 1) * W)
        g.vp[k, 4:5, :] = bias_o[:, at]
        g.vp[k, 5:6, :] = gain_two[:, at]
        g.vp[k, 6:7, :] = shift_two[:, at]
        g.vp[k, 7:8, :] = bias_out[:, at]
    vec_copies = []
    for i, rel in enumerate(FAR):
        to = pl.ds(4 * ((zh + rel[0]) % 2), 4)
        vec_copies.append(tx.send(g.vp.at[to], g.vr.at[i], far(rel)))
    lo = out_sum.total(p) + g.mid[...] + prm[7:8]
    g.lo_s[...] = lo.astype(BF)
    swap_lo = swap(g.lo_s, g.lo, g.lo)
    gqkv_sum.turn()
    o_sum.turn()
    g.gout[...] = gout_sum.total()
    g.gin_d[...] = flat_team(gin_sum.total())
    gin_copies = team_send(lambda q: g.gin_d.at[q], g.gin_e.at[p])
    g.gin_e[p] = g.gin_d[p]
    wait_all(gb_copies)
    g.gbin[...] = (g.bp[e] + g.br[0] + g.br[1] + g.br[2])[:1]
    wait_all(vec_copies)
    g.vs[...] = g.vp[pl.ds(4 * zh, 4)] + g.vr[0] + g.vr[1] + g.vr[2]
    vec_copies = team_send(lambda q: g.vs.at[q // 2], g.va.at[p])
    g.va[p] = g.vs[zx]
    g.mid[...] = n_sum.total(p)

    def norm_one_back(i, _):
        rows = pl.ds(pl.multiple_of(i * 32, 32), 32)
        hat, scale = norm_parts(
            g.raw[p, pl.ds(pl.multiple_of(M + i * 32, 32), 32), :].astype(F32)
        )
        pull = g.mid[rows, :] * prm[0:1]
        mean = jnp.mean(pull, axis=-1, keepdims=True)
        along_hat = jnp.mean(pull * hat, axis=-1, keepdims=True)
        out = g.mg[rows, :] + scale * (pull - mean - hat * along_hat)
        g.ig_s[rows, :] = out.astype(BF)
        return 0

    lax.fori_loop(0, T // 32, norm_one_back, 0)
    swap_ig = swap(g.ig_s, g.ig, g.ig)
    g.gqkv_d[...] = flat_team(gqkv_sum.total())
    gqkv_copies = team_send(lambda q: g.gqkv_d.at[q], g.gqkv_e.at[p])
    g.gqkv_e[p] = g.gqkv_d[p]
    g.go_s[...] = o_sum.total(p).astype(BF)
    go_own = lambda i, j: g.go_s.at[i, j]
    go_sum = FarSum(tx, far, zh, y, go_own, g.go_a, g.go_b, g.go_c)
    go_sum.start(1 - zh)
    go_sum.start(zh)
    wait_all(gin_copies)
    for q in range(8):
        for k in range(4):
            at = (16 * (k // 2) + 4 * (q // 2) + 2 * (k % 2) + q % 2) * H4
            g.gin[:, at : at + H4] = g.gin_e[q, :, k * H4 : (k + 1) * H4].astype(F32)
    go_sum.turn()
    wait_all(vec_copies)
    total = g.va[0]
    for q in range(1, 8):
        total = total + g.va[q]
    g.gvec[...] = total
    wait_all(gqkv_copies)
    for q in range(8):
        for i, out in enumerate((g.gq, g.gk, g.gv)):
            out[:, q * W : (q + 1) * W] = g.gqkv_e[q, :, i * W : (i + 1) * W].astype(F32)
    g.go[...] = go_sum.total()
    swap_lo.wait_recv()
    swap_ig.wait_recv()
    tx.drain()

    @pl.when(moves)
    def _():
        for copy in swaps:
            copy.wait_send()


def flat_team(value):
    return value.astype(BF).reshape((8,) + value.shape[2:])


def finish_kernel(share, *refs):
    ins, outs, held = refs[:10], refs[10:20], refs[20:30]
    wide, picked, sems = refs[30:]
    loads = [pltpu.make_async_copy(ins[i], held[i], sems.at[i]) for i in range(10)]
    for copy in loads:
        copy.start()
    stores = []
    for i in (0, 2, 3, 4, 5, 6, 7, 9, 1, 8):
        loads[i].wait()
        src = held[i]
        if i == 1:
            wide[...] = src[...].astype(F32)
            src = wide
        if i == 8:
            mine = lax.axis_index("dp")
            part = src[:, :share]
            for k in range(1, src.shape[1] // share):
                part = jnp.where(mine == k, src[:, k * share : (k + 1) * share], part)
            picked[...] = part
            src = picked
        stores.append(pltpu.make_async_copy(src, outs[i], sems.at[10 + i]))
        stores[-1].start()
    for copy in stores:
        copy.wait()


def run_layer(layer_input, memory, cotangent, block_order, w_query, w_key, w_value, w_output, w_in, w_out, vectors, b_in):
    T, D = layer_input.shape[1:]
    M = memory.shape[1]
    FF = w_in.shape[1]
    W = D // 8
    share = vectors.shape[1]
    shapes = scratch_list(T, M, D, FF)
    vmem = pl.BlockSpec(memory_space=pltpu.VMEM)
    smem = pl.BlockSpec(memory_space=pltpu.SMEM)
    hbm = pl.BlockSpec(memory_space=pl.ANY)
    outs = pl.pallas_call(
        functools.partial(layer_kernel, T, M, D, FF, share),
        out_shape=(
            jax.ShapeDtypeStruct((T, D), BF),
            jax.ShapeDtypeStruct((T, D), BF),
            jax.ShapeDtypeStruct(w_query.shape, F32),
            jax.ShapeDtypeStruct(w_key.shape, F32),
            jax.ShapeDtypeStruct(w_value.shape, F32),
            jax.ShapeDtypeStruct(w_output.shape, F32),
            jax.ShapeDtypeStruct(w_in.shape, F32),
            jax.ShapeDtypeStruct(w_out.shape, F32),
            jax.ShapeDtypeStruct((8, W), F32),
            jax.ShapeDtypeStruct((1, b_in.shape[0]), F32),
        ),
        in_specs=[hbm, hbm, hbm, smem] + [hbm] * 6 + [vmem] * 2,
        out_specs=[vmem] * 10,
        scratch_shapes=[pltpu.VMEM(shape, kind) for shape, kind in shapes.values()]
        + [pltpu.SemaphoreType.DMA((SEMS,)), pltpu.SemaphoreType.DMA((SEMS,))],
        compiler_params=pltpu.CompilerParams(
            collective_id=0, has_side_effects=True, vmem_limit_bytes=63 * 2**20
        ),
    )(layer_input[0], memory[0], cotangent[0], block_order, w_query, w_key, w_value, w_output, w_in, w_out, vectors, b_in[None])
    final = [jax.ShapeDtypeStruct(outs[0].shape, BF), jax.ShapeDtypeStruct(outs[1].shape, F32)]
    final += [jax.ShapeDtypeStruct(out.shape, F32) for out in outs[2:8]]
    final += [jax.ShapeDtypeStruct((8, share), F32), jax.ShapeDtypeStruct((1, b_in.shape[0]), F32)]
    lo, ig, gq, gk, gv, go, gin, gout, gvec, gbin = pl.pallas_call(
        functools.partial(finish_kernel, share),
        out_shape=final,
        in_specs=[hbm] * 10,
        out_specs=[hbm] * 10,
        scratch_shapes=[pltpu.VMEM(out.shape, out.dtype) for out in outs]
        + [
            pltpu.VMEM((T, D), F32),
            pltpu.VMEM((8, share), F32),
            pltpu.SemaphoreType.DMA((20,)),
        ],
        compiler_params=pltpu.CompilerParams(vmem_limit_bytes=60 * 2**20),
    )(*outs)
    return (lo[None], ig[None], gq, gk, gv, go, gin, gout, gvec, gbin[0])


masked_value = -1e30


def passed_along(block, axis, distance):
    devices = range(lax.axis_size(axis))
    route = [((i - distance) % len(devices), i) for i in devices]
    return lax.ppermute(block, axis, route)


def layer_norm(values, gain, shift):
    center = values - jnp.mean(values, axis=-1, keepdims=True)
    spread = jnp.mean(center * center, axis=-1, keepdims=True)
    return center * lax.rsqrt(spread + 1e-05) * gain + shift


def contract_rows(left, right):
    return lax.dot_general(
        left, right, (((0,), (0,)), ((), ())), preferred_element_type=jnp.float32
    )


def times_transposed(left, right):
    return lax.dot_general(
        left, right, (((1,), (1,)), ((), ())), preferred_element_type=jnp.float32
    )


def split_heads(matrix, heads):
    return matrix.reshape(matrix.shape[0], heads, matrix.shape[1] // heads)


def score_block(query_heads, key_rows):
    key_heads = split_heads(key_rows, query_heads.shape[1])
    return (
        jnp.einsum("qhd,khd->hqk", query_heads, key_heads, preferred_element_type=jnp.float32)
        * 0.125
    )


def lookup_block(order, device):
    return jnp.sum(jnp.where(jnp.arange(order.shape[0]) == device, order, 0))


def split_piece(piece, rows_dev, mem_rows):
    shards = piece.shape[0] // rows_dev
    blocks = piece.reshape(shards, rows_dev, piece.shape[1])
    memory_part = blocks[:, :mem_rows].reshape(shards * mem_rows, piece.shape[1])
    token_part = blocks[:, mem_rows:].reshape(shards * (rows_dev - mem_rows), piece.shape[1])
    return (shards, memory_part, token_part)


def piece_positions(order, shards, tok_rows):
    shard_ids = jnp.arange(shards)
    hits = shard_ids[:, None] == jnp.arange(order.shape[0])[None, :]
    starts = jnp.sum(jnp.where(hits, order[None, :], 0), axis=1)
    positions = (starts[:, None] * tok_rows + jnp.arange(tok_rows)[None, :]).reshape(
        shards * tok_rows
    )
    return (starts, positions)


def softmax_stats(carry, scores):
    running, total = carry
    top = jnp.maximum(running, jnp.max(scores, axis=2))
    total = total * jnp.exp(running - top) + jnp.sum(jnp.exp(scores - top[:, :, None]), axis=2)
    return (top, total)


def per_device(
    layer_input,
    memory,
    cotangent,
    block_order,
    w_query,
    w_key,
    w_value,
    w_output,
    w_in,
    w_out,
    vectors,
    b_in,
):
    bf16 = jnp.bfloat16
    gathered = (
        lax.all_gather(w_query.astype(bf16), ("blk", "dp"), axis=0, tiled=True),
        lax.all_gather(w_key.astype(bf16), ("blk", "dp"), axis=0, tiled=True),
        lax.all_gather(w_value.astype(bf16), ("blk", "dp"), axis=0, tiled=True),
        lax.all_gather(w_output.astype(bf16), ("blk", "dp"), axis=0, tiled=True),
        lax.all_gather(w_in.astype(bf16), ("blk", "dp"), axis=0, tiled=True),
        lax.all_gather(w_out.astype(bf16), ("blk", "dp"), axis=0, tiled=True),
        lax.all_gather(vectors.astype(bf16), ("blk", "dp"), axis=1, tiled=True),
        lax.all_gather(b_in.astype(bf16), ("blk", "dp"), axis=0, tiled=True),
    )
    (
        query_full,
        key_full,
        value_full,
        output_full,
        inner_full,
        outer_full,
        vector_full,
        inner_low,
    ) = gathered
    params = vector_full.astype(jnp.float32)
    inner_shift = inner_low.astype(jnp.float32)
    heads = HEADS
    tokens = layer_input[0].astype(jnp.float32)
    recalled = memory[0].astype(jnp.float32)
    tok_rows = tokens.shape[0]
    mem_rows = recalled.shape[0]
    rows_dev = tok_rows + mem_rows
    width = tokens.shape[1]
    blocks_total = lax.axis_size("blk")
    here = lax.axis_index("blk")
    own_block = lookup_block(block_order, here)
    query_pos = own_block * tok_rows + jnp.arange(tok_rows)
    both_rows = jnp.concatenate([recalled, tokens], axis=0)
    normed = layer_norm(both_rows, params[0], params[1]).astype(bf16)
    normed_tok = normed[mem_rows:]
    queries = (
        jnp.dot(normed_tok, query_full, preferred_element_type=jnp.float32) + params[2]
    ).astype(bf16)
    keys_all = jnp.dot(normed, key_full, preferred_element_type=jnp.float32).astype(bf16)
    values_all = (
        jnp.dot(normed, value_full, preferred_element_type=jnp.float32) + params[3]
    ).astype(bf16)
    query_heads = split_heads(queries, heads)

    def causal(scores, key_pos):
        return jnp.where(key_pos[None, None, :] <= query_pos[None, :, None], scores, masked_value)

    start_stats = (
        jnp.full((heads, tok_rows), masked_value, jnp.float32),
        jnp.zeros((heads, tok_rows), jnp.float32),
    )
    carry = start_stats
    shards, memory_part, token_part = split_piece(
        lax.all_gather(keys_all, "blk", axis=0, tiled=True), rows_dev, mem_rows
    )
    starts, token_pos = piece_positions(block_order, shards, tok_rows)
    carry = softmax_stats(carry, score_block(query_heads, memory_part))

    def with_tokens(state):
        return softmax_stats(state, causal(score_block(query_heads, token_part), token_pos))

    def without_tokens(state):
        return state

    running, total = lax.cond(jnp.any(starts <= own_block), with_tokens, without_tokens, carry)
    log_total = running + jnp.log(total)

    def value_part(context, part, key_pos):
        scores = score_block(query_heads, part[:, :width])
        if key_pos is not None:
            scores = causal(scores, key_pos)
        weights = jnp.exp(scores - log_total[:, :, None]).astype(bf16)
        return context + jnp.einsum(
            "hqk,khd->qhd",
            weights,
            split_heads(part[:, width:], heads),
            preferred_element_type=jnp.float32,
        )

    key_values = jnp.concatenate([keys_all, values_all], axis=1)
    context = jnp.zeros((tok_rows, heads, width // heads), jnp.float32)
    shards, memory_part, add_token_part = split_piece(
        lax.all_gather(key_values, "blk", axis=0, tiled=True), rows_dev, mem_rows
    )
    starts, add_token_pos = piece_positions(block_order, shards, tok_rows)
    context = value_part(context, memory_part, None)

    def with_tokens(state):
        return value_part(state, add_token_part, add_token_pos)

    def without_tokens(state):
        return state

    context = lax.cond(jnp.any(starts <= own_block), with_tokens, without_tokens, context)
    context_low = context.reshape(tok_rows, width).astype(bf16)
    attended = jnp.dot(context_low, output_full, preferred_element_type=jnp.float32) + params[4]
    middle = tokens + attended
    normed_two = layer_norm(middle, params[5], params[6]).astype(bf16)
    inner = jnp.dot(normed_two, inner_full, preferred_element_type=jnp.float32) + inner_shift
    activated = jax.nn.gelu(inner, approximate=True).astype(bf16)
    result = middle + jnp.dot(activated, outer_full, preferred_element_type=jnp.float32) + params[7]
    output = result.astype(bf16)
    upstream = cotangent[0]
    upstream_full = upstream.astype(jnp.float32)
    grad_outer = contract_rows(activated, upstream)
    grad_outer_bias = jnp.sum(upstream_full, axis=0)
    act_grad = times_transposed(upstream, outer_full)
    _, gelu_back = jax.vjp(functools.partial(jax.nn.gelu, approximate=True), inner)
    inner_grad = gelu_back(act_grad)[0].astype(bf16)
    grad_inner = contract_rows(normed_two, inner_grad)
    grad_inner_bias = jnp.sum(inner_grad.astype(jnp.float32), axis=0)
    normed_two_grad = times_transposed(inner_grad, inner_full)
    _, norm_two_back = jax.vjp(layer_norm, middle, params[5], params[6])
    middle_part, grad_gain_two, grad_shift_two = norm_two_back(normed_two_grad)
    middle_grad = upstream_full + middle_part
    attended_grad = middle_grad.astype(bf16)
    grad_output = contract_rows(context_low, attended_grad)
    grad_output_bias = jnp.sum(attended_grad.astype(jnp.float32), axis=0)
    context_grad = times_transposed(attended_grad, output_full).astype(bf16)
    context_heads = split_heads(context_grad, heads)
    delta = jnp.einsum("qhd,qhd->hq", context_heads.astype(jnp.float32), context)

    def attend_back(queries_grad, part, key_pos):
        count = part.shape[0]
        key_heads = split_heads(part[:, :width], heads)
        value_heads = split_heads(part[:, width:], heads)
        scores = score_block(query_heads, part[:, :width])
        if key_pos is not None:
            scores = causal(scores, key_pos)
        exact = jnp.exp(scores - log_total[:, :, None])
        weight_low = exact.astype(bf16)
        weight_grad = jnp.einsum(
            "qhd,khd->hqk", context_heads, value_heads, preferred_element_type=jnp.float32
        )
        score_grad = (exact * (weight_grad - delta[:, :, None])).astype(bf16)
        queries_grad = (
            queries_grad
            + jnp.einsum("hqk,khd->qhd", score_grad, key_heads, preferred_element_type=jnp.float32)
            * 0.125
        )
        key_grad = (
            jnp.einsum("hqk,qhd->khd", score_grad, query_heads, preferred_element_type=jnp.float32)
            * 0.125
        )
        value_grad = jnp.einsum(
            "hqk,qhd->khd", weight_low, context_heads, preferred_element_type=jnp.float32
        )
        return (
            queries_grad,
            jnp.concatenate(
                [key_grad.reshape(count, width), value_grad.reshape(count, width)], axis=1
            ),
        )

    def visit(queries_grad, travelling, travel_grad, anchor):
        anchor_block = lookup_block(block_order, anchor)
        queries_grad, memory_grad = attend_back(queries_grad, travelling[:mem_rows], None)
        token_pos = anchor_block * tok_rows + jnp.arange(tok_rows)

        def with_tokens(state):
            return attend_back(state, travelling[mem_rows:], token_pos)

        def without_tokens(state):
            return (state, jnp.zeros((tok_rows, 2 * width), jnp.float32))

        queries_grad, token_grad = lax.cond(
            anchor_block <= own_block, with_tokens, without_tokens, queries_grad
        )
        return (queries_grad, travel_grad + jnp.concatenate([memory_grad, token_grad], axis=0))

    def pass_grads(values):
        return passed_along(values.astype(jnp.bfloat16), "blk", 1).astype(values.dtype)

    queries_grad, travel_grad = visit(
        jnp.zeros((tok_rows, heads, width // heads), jnp.float32),
        key_values,
        jnp.zeros((rows_dev, 2 * width), jnp.float32),
        here,
    )

    def turn(step, state):
        queries_grad, travelling, travel_grad = state
        travelling = passed_along(travelling, "blk", 1)
        travel_grad = pass_grads(travel_grad)
        anchor = (here - step) % blocks_total
        queries_grad, travel_grad = visit(queries_grad, travelling, travel_grad, anchor)
        return (queries_grad, travelling, travel_grad)

    queries_grad, travelling, travel_grad = lax.fori_loop(
        1, blocks_total, turn, (queries_grad, key_values, travel_grad)
    )
    travel_grad = pass_grads(travel_grad)
    pair_grad = travel_grad.astype(bf16)
    key_grad = pair_grad[:, :width]
    value_grad = pair_grad[:, width:]
    query_grad = queries_grad.reshape(tok_rows, width).astype(bf16)
    grad_query = contract_rows(normed_tok, query_grad)
    grad_query_bias = jnp.sum(query_grad.astype(jnp.float32), axis=0)
    grad_key = contract_rows(normed, key_grad)
    grad_value = contract_rows(normed, value_grad)
    grad_value_bias = jnp.sum(value_grad.astype(jnp.float32), axis=0)
    normed_grad = times_transposed(key_grad, key_full) + times_transposed(value_grad, value_full)
    query_part = times_transposed(query_grad, query_full)
    normed_grad = normed_grad + jnp.concatenate(
        [jnp.zeros((mem_rows, width), jnp.float32), query_part], axis=0
    )
    _, norm_one_back = jax.vjp(layer_norm, both_rows, params[0], params[1])
    rows_grad, grad_gain_one, grad_shift_one = norm_one_back(normed_grad)
    input_grad = middle_grad + rows_grad[mem_rows:]
    vector_grad = jnp.stack(
        [
            grad_gain_one,
            grad_shift_one,
            grad_query_bias,
            grad_value_bias,
            grad_output_bias,
            grad_gain_two,
            grad_shift_two,
            grad_outer_bias,
        ]
    )
    out_query, out_key, out_value, out_output, out_inner, out_outer, out_vectors, out_bias = (
        lax.psum_scatter(grad_query, ("blk", "dp"), scatter_dimension=0, tiled=True),
        lax.psum_scatter(grad_key, ("blk", "dp"), scatter_dimension=0, tiled=True),
        lax.psum_scatter(grad_value, ("blk", "dp"), scatter_dimension=0, tiled=True),
        lax.psum_scatter(grad_output, ("blk", "dp"), scatter_dimension=0, tiled=True),
        lax.psum_scatter(grad_inner, ("blk", "dp"), scatter_dimension=0, tiled=True),
        lax.psum_scatter(grad_outer, ("blk", "dp"), scatter_dimension=0, tiled=True),
        lax.psum_scatter(vector_grad, ("blk", "dp"), scatter_dimension=1, tiled=True),
        lax.psum_scatter(grad_inner_bias, ("blk", "dp"), scatter_dimension=0, tiled=True),
    )
    return (
        output[None],
        input_grad[None],
        out_query,
        out_key,
        out_value,
        out_output,
        out_inner,
        out_outer,
        out_vectors,
        out_bias,
    )


def solution(mesh):
    rows = P("dp", "blk", None)
    shard = P(("blk", "dp"), None)
    in_specs = (rows, rows, rows, P()) + (shard,) * 6 + (P(None, ("blk", "dp")), P(("blk", "dp")))
    out_specs = (rows, rows) + (shard,) * 6 + (P(None, ("blk", "dp")), P(("blk", "dp")))
    planes = mesh.shape["blk"] == 8 and mesh.shape["dp"] == 4
    return jax.shard_map(
        run_layer if planes else per_device,
        mesh=mesh,
        in_specs=in_specs,
        out_specs=out_specs,
        check_vma=False,
    )
```

```python
import functools

import jax
import jax.numpy as jnp
from jax import lax
from jax.experimental import pallas as pl
from jax.experimental.pallas import tpu as pltpu
from jax.sharding import PartitionSpec as P

HEADS = 16
BF = jnp.bfloat16
F32 = jnp.float32
MESH = pl.DeviceIdType.MESH
EXACT = lax.Precision.HIGHEST


def dot(a, b):
    return lax.dot_general(a, b, (((1,), (0,)), ((), ())), preferred_element_type=F32)


def dot_nt(a, b, precision=None):
    return lax.dot_general(
        a, b, (((1,), (1,)), ((), ())), preferred_element_type=F32, precision=precision
    )


def dot_tn(a, b):
    return lax.dot_general(a, b, (((0,), (0,)), ((), ())), preferred_element_type=F32)


def flat(value):
    return value.reshape(-1, value.shape[-1])


def col_sum(value):
    return jnp.sum(value.astype(F32), axis=0, keepdims=True)


def norm_parts(rows):
    center = rows - jnp.mean(rows, axis=-1, keepdims=True)
    spread = jnp.mean(center * center, axis=-1, keepdims=True)
    scale = lax.rsqrt(spread + 1e-05)
    return center * scale, scale


def gelu_parts(v):
    square = v * v
    t = jnp.tanh(0.7978845608 * v * (1.0 + 0.044715 * square))
    half = 0.5 * (1.0 + t)
    slope = half + 0.5 * v * (1.0 - t * t) * (0.7978845608 * (1.0 + 3 * 0.044715 * square))
    return v * half, slope


IN_NAMES = ["x", "mem", "cot", "order", "wq", "wk", "wv", "wo", "win", "wout", "vec", "bias"]
OUT_NAMES = ["lo", "ig", "gq", "gk", "gv", "go", "gin", "gout", "gvec", "gbin"]
TEAM = [(1, 1, 1), (1, 1, 0), (1, 0, 1), (1, 0, 0), (0, 1, 1), (0, 1, 0), (0, 0, 1)]
FAR = [(1, 0), (0, 1), (1, 1)]
QUADS = [(1, 1, 0), (0, 1, 0), (1, 0, 0), (0, 0, 0)]
SIB, XN, ZN = (0, 0, 1), (0, 1, 0), (1, 0, 0)


def scratch_list(T, M, D, FF):
    R = T + M
    H = FF // 8
    H4 = H // 4
    W = D // 8
    B = D // 32
    S = 8 * T
    K = 8 * R
    grid = (2, 4, 2, 2, B)
    return dict(
        f_qkv=((3, B, D), F32),
        f_o=((B, D), F32),
        f_in=((B, FF), F32),
        f_out=((H4, D), F32),
        n_all=((8, R, D), BF),
        raw=((8, R, D), BF),
        cot_all=((8, T, D), BF),
        n2_all=((8, T, D), BF),
        pq=((8, B, 3 * W), BF),
        pi=((8, B, H), BF),
        wqkv=(grid + (3 * W,), BF),
        w_in=(grid + (H,), BF),
        w_out=((2, 2, H4, D), BF),
        w_o=(grid + (D,), BF),
        vg1=((8, 8, W), F32),
        vg2=((4, 4, 8, W), F32),
        pg=((8, 8, W), F32),
        bslot=((4, 8, H4), F32),
        prm=((8, D), F32),
        qkv=((8, R, 3 * W), BF),
        qs=((S, W), BF),
        kk=((K, W), BF),
        vv=((K, W), BF),
        wts=((2, S, K), BF),
        ctx=((S, W), F32),
        ctx_send=((8, T, W), BF),
        ctx_own=((8, T, W), BF),
        ctx2d=((T, D), BF),
        mid=((T, D), F32),
        act=((4, S, H4), BF),
        inner=((S, H), BF),
        pb_a=((8, T, D), BF),
        r1_a=((4, T, D), BF),
        rx_a=((2, T, D), BF),
        rz_a=((T, D), BF),
        pb_b=((8, T, D), BF),
        r1_b=((4, T, D), BF),
        rx_b=((2, T, D), BF),
        rz_b=((T, D), BF),
        pb_n=((8, T, D), BF),
        r1_n=((4, T, D), BF),
        rx_n=((2, T, D), BF),
        rz_n=((T, D), BF),
        mg=((T, D), F32),
        attg=((T, D), BF),
        cg_send=((8, T, W), BF),
        cg_all=((8, T, W), BF),
        pb_o=(grid + (D,), BF),
        r1_o=((4, 2, 2, B, D), BF),
        rx_o=((2, 2, B, D), BF),
        rz_o=((2, B, D), BF),
        go_y=((2, 4, B, D), BF),
        go_m=((4, 2, B, D), BF),
        go_s=((2, B, D), BF),
        go_c=((B, D), BF),
        cg_sorted=((S, W), BF),
        dq=((S, W), F32),
        dk=((K, W), F32),
        dv=((K, W), F32),
        dqkv=((8, R, 3 * W), BF),
        gout_s=((2, 2, H4, D), BF),
        gout_a=((2, H4, D), BF),
        gout_b=((H4, D), BF),
        gout_c=((H4, D), BF),
        gin_s=(grid + (H,), BF),
        gin_a=((2, 4, 2, B, H), BF),
        gin_b=((4, 2, B, H), BF),
        gin_c=((4, 2, B, H), BF),
        gin_d=((8, B, H), BF),
        gin_e=((8, B, H), BF),
        gqkv_s=(grid + (3 * W,), BF),
        gqkv_a=((2, 4, 2, B, 3 * W), BF),
        gqkv_b=((4, 2, B, 3 * W), BF),
        gqkv_c=((4, 2, B, 3 * W), BF),
        gqkv_d=((8, B, 3 * W), BF),
        gqkv_e=((8, B, 3 * W), BF),
        vp=((8, 8, W), F32),
        vr=((3, 4, 8, W), F32),
        vs=((4, 8, W), F32),
        va=((8, 8, W), F32),
        bp=((4, 8, H4), F32),
        br=((3, 8, H4), F32),
        lo_s=((T, D), BF),
        ig_s=((T, D), BF),
    )


SEMS = 320


class Sender:
    def __init__(self, ssem, rsem):
        self.ssem, self.rsem, self.count, self.pending = ssem, rsem, 0, []

    def make(self, src, dst, target):
        at = self.count
        self.count += 1
        return pltpu.make_async_remote_copy(
            src_ref=src,
            dst_ref=dst,
            send_sem=self.ssem.at[at],
            recv_sem=self.rsem.at[at],
            device_id=target,
            device_id_type=MESH,
        )

    def local(self, src, dst):
        at = self.count
        self.count += 1
        copy = pltpu.make_async_copy(src, dst, self.rsem.at[at])
        copy.start()
        return copy

    def plan(self, src, dst, target):
        copy = self.make(src, dst, target)
        self.pending.append(copy)
        return copy

    def send(self, src, dst, target):
        copy = self.plan(src, dst, target)
        copy.start()
        return copy

    def drain(self):
        for copy in self.pending:
            copy.wait_send()


class TeamGather:
    def __init__(self, tx, near, slot, ref):
        def plan(rel, to):
            ats = [ref(slot(rel), half) for half in (0, 1)]
            return [tx.plan(at, at, near(to)) for at in ats]

        self.zn, self.xn = plan((0, 0, 0), ZN), plan((0, 0, 0), XN)
        self.diag = plan(ZN, XN)
        self.sib = {rel: plan(rel, SIB) for rel in QUADS}

    def start(self, half):
        self.zn[half].start()
        self.xn[half].start()
        self.sib[(0, 0, 0)][half].start()

    def forward(self):
        for half in (0, 1):
            self.zn[half].wait_recv()
            self.diag[half].start()
            self.sib[ZN][half].start()

    def pass_xn(self):
        for half in (0, 1):
            self.xn[half].wait_recv()
            self.sib[XN][half].start()

    def pass_diag(self):
        for half in (0, 1):
            self.diag[half].wait_recv()
            self.sib[(1, 1, 0)][half].start()

    def wait_sib(self, rel):
        for copy in self.sib[rel]:
            copy.wait_recv()

    def finish(self):
        self.pass_xn()
        self.pass_diag()
        for rel in QUADS:
            self.wait_sib(rel)


class FarGather:
    def __init__(self, tx, far, zh, y, ref):
        own, passed = ref(zh, y), ref(1 - zh, y)
        self.over_z = tx.plan(own, own, far((1, 0)))
        self.over_y = tx.plan(own, own, far((0, 1)))
        self.passed = tx.plan(passed, passed, far((0, 1)))

    def start(self):
        self.over_z.start()
        self.over_y.start()

    def forward(self):
        self.over_z.wait_recv()
        self.passed.start()

    def finish(self):
        self.over_y.wait_recv()
        self.passed.wait_recv()


class TeamScatter:
    def __init__(self, tx, near, slot, buf, first, cross, last, halves):
        self.tx, self.near, self.slot, self.buf = tx, near, slot, buf
        self.first, self.cross, self.last, self.halves = first, cross, last, halves
        self.sib, self.turned, self.ended = {}, [], []

    def push(self, order):
        rel = QUADS[order]
        src = self.buf(self.slot((rel[0], rel[1], 1)))
        self.sib[order] = self.tx.send(src, self.first.at[order], self.near(SIB))

    def sum(self, order, half):
        own = self.buf(self.slot(QUADS[order]))
        part, more = own.at[half], self.first.at[order].at[half]
        part[...] = (part[...].astype(F32) + more[...].astype(F32)).astype(BF)

    def hand(self, order, half):
        part = self.buf(self.slot(QUADS[order])).at[half]
        to = self.cross.at[order].at[half]
        copy = self.tx.send(part, to, self.near(XN))
        (self.ended if order else self.turned).append(copy)

    def add(self, order, hand=True):
        self.sib[order].wait_recv()
        for half in self.halves:
            self.sum(order, half)
            if hand and order < 2:
                self.hand(order, half)

    def turn(self):
        own = self.buf(self.slot(ZN))
        for half, copy in zip(self.halves, self.turned):
            copy.wait_recv()
            part, more = own.at[half], self.cross.at[0].at[half]
            part[...] = (part[...].astype(F32) + more[...].astype(F32)).astype(BF)
            self.ended.append(self.tx.send(part, self.last.at[half], self.near(ZN)))

    def total(self, own):
        for copy in self.ended:
            copy.wait_recv()
        return (
            self.buf(own)[...].astype(F32)
            + self.cross[1].astype(F32)
            + self.last[...].astype(F32)
        )


class FarSum:
    def __init__(self, tx, far, zh, y, own, first, mid, last):
        self.tx, self.far, self.zh, self.y, self.own = tx, far, zh, y, own
        self.first, self.mid, self.last, self.copies = first, mid, last, []

    def start(self, half):
        src = self.own(half, 1 - self.y)
        self.copies.append(self.tx.send(src, self.first.at[half], self.far((0, 1))))

    def both(self, half):
        return self.own(half, self.y)[...].astype(F32) + self.first[half].astype(F32)

    def turn(self):
        self.copies[0].wait_recv()
        self.mid[...] = self.both(1 - self.zh).astype(BF)
        self.ended = self.tx.send(self.mid, self.last, self.far((1, 0)))

    def total(self):
        self.copies[1].wait_recv()
        self.ended.wait_recv()
        return self.both(self.zh) + self.last[...].astype(F32)


def layer_kernel(T, M, D, FF, share, *refs):
    names = IN_NAMES + OUT_NAMES + list(scratch_list(T, M, D, FF))
    ssem, rsem = refs[len(names) :]
    g = type("Refs", (), dict(zip(names, refs)))
    R, H, Q, W, S = T + M, FF // 8, D // 4, D // 8, 8 * T
    H4, B = H // 4, D // 32
    MK = 8 * M
    tx = Sender(ssem, rsem)

    b, d = lax.axis_index("blk"), lax.axis_index("dp")
    z, x, y, c = b // 2, b % 2, d // 2, d % 2
    zh, zl = z // 2, z % 2
    zx = 2 * zl + x
    p = 2 * zx + c
    e = 2 * zh + y

    def dev(zh, zl, x, y, c):
        return (4 * zh + 2 * zl + x, 2 * y + c)

    def near(rel):
        return dev(zh, (zl + rel[0]) % 2, (x + rel[1]) % 2, y, (c + rel[2]) % 2)

    def slot(rel):
        return 4 * ((zl + rel[0]) % 2) + 2 * ((x + rel[1]) % 2) + (c + rel[2]) % 2

    def far(rel):
        return dev((zh + rel[0]) % 2, zl, x, (y + rel[1]) % 2, c)

    partner = dev(c, zl, x, y, zh)
    partner_slot = 2 * zx + zh
    stays = c == zh
    moves = jnp.logical_not(stays)
    outer = zl == zh
    inner = jnp.logical_not(outer)

    barrier = pltpu.get_barrier_semaphore()
    for rel in TEAM:
        pl.semaphore_signal(barrier, inc=1, device_id=near(rel), device_id_type=MESH)
    for rel in FAR:
        pl.semaphore_signal(barrier, inc=1, device_id=far(rel), device_id_type=MESH)

    @pl.when(moves)
    def _():
        pl.semaphore_signal(barrier, inc=1, device_id=partner, device_id_type=MESH)

    loads = [tx.local(w, g.f_qkv.at[i]) for i, w in enumerate((g.wq, g.wk, g.wv))]
    loads_o = tx.local(g.wo, g.f_o)
    loads_in = tx.local(g.win, g.f_in)
    loads_out = tx.local(g.wout, g.f_out)
    share_lane = lax.broadcasted_iota(jnp.int32, (8, W), 1) // share
    low = g.vec[...].astype(BF).astype(F32)
    spread = jnp.concatenate([low] * (W // share), axis=1)
    g.vg1[p] = jnp.where(share_lane == 2 * y + c, spread, 0.0)
    g.bslot[e] = jnp.broadcast_to(g.bias[...].astype(BF).astype(F32), (8, H4))
    loads_o.wait()
    g.w_o[zh, zx, y, c] = g.f_o[...].astype(BF)
    for copy in loads:
        copy.wait()
    for q in range(8):
        for i in range(3):
            g.pq[q, :, i * W : (i + 1) * W] = g.f_qkv[i, :, q * W : (q + 1) * W].astype(BF)
    g.wqkv[zh, zx, y, c] = g.pq[p]
    loads_in.wait()
    for q in range(8):
        for k in range(4):
            at = (16 * (k // 2) + 4 * (q // 2) + 2 * (k % 2) + q % 2) * H4
            g.pi[q, :, k * H4 : (k + 1) * H4] = g.f_in[:, at : at + H4].astype(BF)
    g.w_in[zh, zx, y, c] = g.pi[p]
    loads_out.wait()
    g.w_out[zh, y] = g.f_out[...].astype(BF)
    @pl.when(moves)
    def _():
        pl.semaphore_wait(barrier, 11)

    @pl.when(stays)
    def _():
        pl.semaphore_wait(barrier, 10)

    swaps = []

    class Swap:
        def __init__(self, src, dst_there, dst_here):
            self.copy = tx.make(src, dst_there, partner)
            self.here = pltpu.make_async_copy(src, dst_here, rsem.at[tx.count - 1])
            swaps.append(self.copy)

        def start(self):
            pl.when(moves)(self.copy.start)
            pl.when(stays)(self.here.start)

        def wait_recv(self):
            self.copy.wait_recv()

    def swap(src, dst_there, dst_here):
        copy = Swap(src, dst_there, dst_here)
        copy.start()
        return copy

    def team_send(src, dst):
        return [tx.send(src(slot(rel)), dst, near(rel)) for rel in TEAM]

    def wait_all(copies):
        for copy in copies:
            copy.wait_recv()

    vec_copies = [tx.send(g.vg1.at[p], g.vg1.at[p], near(rel)) for rel in TEAM]
    qkv_copies = team_send(lambda q: g.pq.at[q], g.wqkv.at[zh, zx, y, c])
    wo_far = FarGather(tx, far, zh, y, lambda i, j: g.w_o.at[i, zx, j, c])
    wo_far.start()
    half_rows, half_tok = R // 2, T // 2
    early = half_rows - M
    raw_here, raw_there = g.raw.at[p], g.raw.at[partner_slot]
    cuts = [
        (g.mem, pl.ds(0, M)),
        (g.x.at[pl.ds(0, early)], pl.ds(M, early)),
        (g.x.at[pl.ds(early, T - early)], pl.ds(half_rows, half_rows)),
    ]
    swap_m, swap_a, swap_b = [
        swap(src, raw_there.at[to], raw_here.at[to]) for src, to in cuts
    ]
    swap_c = Swap(g.cot, g.cot_all.at[partner_slot], g.cot_all.at[p])
    n_gather = TeamGather(
        tx, near, slot, lambda q, h: g.raw.at[q, pl.ds(h * half_rows, half_rows)]
    )
    cot_gather = TeamGather(
        tx, near, slot, lambda q, h: g.cot_all.at[q, pl.ds(h * half_tok, half_tok)]
    )
    wo_gather = TeamGather(
        tx, near, slot, lambda q, h: g.w_o.at[h, q // 2, :, q % 2]
    )
    qkv_far = FarGather(tx, far, zh, y, lambda i, j: g.wqkv.at[i, :, j])
    win_far = FarGather(tx, far, zh, y, lambda i, j: g.w_in.at[i, :, j])
    wout_far = FarGather(tx, far, zh, y, lambda i, j: g.w_out.at[i, j])

    def start_rows():
        swap_m.wait_recv()
        swap_a.wait_recv()
        n_gather.start(0)
        swap_b.wait_recv()
        n_gather.start(1)

    def start_cot():
        swap_c.wait_recv()
        cot_gather.start(0)
        cot_gather.start(1)

    @pl.when(stays)
    def _():
        swap_c.here.start()
        start_rows()
        start_cot()

    wait_all(vec_copies)
    for k in range(4):
        g.vg2[e, k] = g.vg1[2 * k] + g.vg1[2 * k + 1]
    vec_copies = [tx.send(g.vg2.at[e], g.vg2.at[e], far(rel)) for rel in FAR]
    vec_copies += [tx.send(g.bslot.at[e], g.bslot.at[e], far(rel)) for rel in FAR]
    wait_all(qkv_copies)
    qkv_far.start()
    wo_far.forward()

    @pl.when(stays)
    def _():
        n_gather.forward()
        cot_gather.forward()

    @pl.when(moves)
    def _():
        start_rows()

    wo_far.finish()
    wo_gather.start(0)
    wo_gather.start(1)

    wait_all(vec_copies)
    for k in range(8):
        group = g.vg2[2 * (k // 4), k % 4] + g.vg2[2 * (k // 4) + 1, k % 4]
        g.pg[k] = group
        g.prm[:, k * W : (k + 1) * W] = group
    prm = g.prm

    def norm_slot(rel, core):
        at = 2 * (slot(rel) // 2) + core

        def step(i, _):
            rows = pl.ds(pl.multiple_of(i * 32, 32), 32)
            hat, _unused = norm_parts(g.raw[at, rows, :].astype(F32))
            g.n_all[at, rows, :] = (hat * prm[0:1] + prm[1:2]).astype(BF)
            return 0

        lax.fori_loop(0, R // 32, step, 0)

    def early_rows(rel, step):
        @pl.when(stays)
        def _():
            step()

        @pl.when(moves)
        def _():
            n_gather.wait_sib(rel)

        norm_slot(rel, zh)

    def late_rows(rel, step):
        @pl.when(moves)
        def _():
            step()

        @pl.when(stays)
        def _():
            n_gather.wait_sib(rel)

        norm_slot(rel, 1 - zh)

    def nothing():
        pass

    early_rows((0, 0, 0), nothing)
    early_rows(ZN, nothing)
    early_rows(XN, n_gather.pass_xn)
    early_rows((1, 1, 0), n_gather.pass_diag)

    @pl.when(moves)
    def _():
        n_gather.forward()
        swap_c.copy.start()

    qkv_far.forward()
    late_rows((0, 0, 0), nothing)
    late_rows(ZN, nothing)
    win_copies = team_send(lambda q: g.pi.at[q], g.w_in.at[zh, zx, y, c])
    late_rows(XN, n_gather.pass_xn)
    wo_gather.forward()
    wout_far.start()
    qkv_far.finish()
    wqkv = lambda: flat(g.wqkv[...].reshape(32, B, 3 * W))
    own_vec = g.pg[p]
    qkv_bias = jnp.concatenate(
        [own_vec[2:3], jnp.zeros((1, W), F32), own_vec[3:4]], axis=1
    )

    def project(rel):
        pair = pl.ds(2 * (slot(rel) // 2), 2)
        out = dot(flat(g.n_all[pair]), wqkv()) + qkv_bias
        g.qkv[pair] = out.astype(BF).reshape(2, R, 3 * W)

    for rel in (SIB, ZN, XN):
        project(rel)
    late_rows((1, 1, 0), n_gather.pass_diag)
    project((1, 1, 0))
    place = [
        g.order[4 * qc + 2 * qz + qx] for qz in (0, 1) for qx in (0, 1) for qc in (0, 1)
    ]

    def pick(blocks, wanted):
        out = blocks[0]
        for block, (left, right) in zip(blocks[1:], wanted[1:]):
            out = jnp.where(jnp.full(out.shape, left, jnp.int32) == right, block, out)
        return out

    def to_sorted(load, store):
        def step(i, _):
            at = pl.multiple_of(i * 16, 16)
            blocks = [load(q, at).astype(F32) for q in range(8)]
            for j in range(8):
                store(j, at, pick(blocks, [(place[q], j) for q in range(8)]))
            return 0

        lax.fori_loop(0, T // 16, step, 0)

    def from_sorted(load, store):
        def step(i, _):
            at = pl.multiple_of(i * 16, 16)
            blocks = [load(j, at).astype(F32) for j in range(8)]
            for q in range(8):
                store(q, at, pick(blocks, [(place[q], j) for j in range(8)]))
            return 0

        lax.fori_loop(0, T // 16, step, 0)

    def store_qkv(j, at, rows):
        g.qs[pl.ds(j * T + at, 16), :] = (rows[:, :W] * 0.125).astype(BF)
        g.kk[pl.ds(MK + j * T + at, 16), :] = rows[:, W : 2 * W].astype(BF)
        g.vv[pl.ds(MK + j * T + at, 16), :] = rows[:, 2 * W :].astype(BF)

    to_sorted(lambda q, at: g.qkv[q, pl.ds(M + at, 16), :], store_qkv)
    for j in range(8):
        g.kk[j * M : (j + 1) * M, :] = g.qkv[j, :M, W : 2 * W]
        g.vv[j * M : (j + 1) * M, :] = g.qkv[j, :M, 2 * W :]
    N = 2 * T
    lane = lax.broadcasted_iota(jnp.int32, (N, W), 1)
    head_lanes = [lane < W // 2, lane >= W // 2]
    below = lax.broadcasted_iota(jnp.int32, (N, N), 1) <= lax.broadcasted_iota(
        jnp.int32, (N, N), 0
    )

    def only(value, h):
        return jnp.where(head_lanes[h], value, jnp.zeros_like(value))

    def attend(i):
        rows = slice(i * N, (i + 1) * N)
        past = MK + i * N
        end = past + N
        q_rows = g.qs[rows, :]
        parts = []
        for h in range(2):
            qh = only(q_rows, h)
            s0 = dot_nt(qh, g.kk[:past, :])
            s1 = dot_nt(qh, g.kk[past:end, :])
            s1 = jnp.where(below, s1, -1e30)
            top = jnp.maximum(
                jnp.max(s0, axis=1, keepdims=True), jnp.max(s1, axis=1, keepdims=True)
            )
            e0 = jnp.exp(s0 - top)
            e1 = jnp.exp(s1 - top)
            total = jnp.sum(e0, axis=1, keepdims=True) + jnp.sum(e1, axis=1, keepdims=True)
            scale = 1.0 / total
            w0 = (e0 * scale).astype(BF)
            w1 = (e1 * scale).astype(BF)
            g.wts[h, rows, :past] = w0
            g.wts[h, rows, past:end] = w1
            parts.append(dot(w0, g.vv[:past, :]) + dot(w1, g.vv[past:end, :]))
        g.ctx[rows, :] = jnp.where(head_lanes[0], parts[0], parts[1])

    wait_all(win_copies)

    @pl.when(inner)
    def _():
        win_far.start()

    attend(0)
    attend(1)

    @pl.when(moves)
    def _():
        start_cot()

    attend(2)
    attend(3)
    def store_ctx(q, at, rows):
        g.ctx_send[q, pl.ds(at, 16), :] = rows.astype(BF)

    from_sorted(lambda j, at: g.ctx[pl.ds(j * T + at, 16), :], store_ctx)
    ctx_copies = team_send(lambda q: g.ctx_send.at[q], g.ctx_own.at[p])
    g.ctx_own[p] = g.ctx_send[p]
    @pl.when(outer)
    def _():
        win_far.start()

    wout_far.forward()

    @pl.when(moves)
    def _():
        cot_gather.forward()

    wo_gather.finish()
    wait_all(ctx_copies)
    for q in range(8):
        g.ctx2d[:, q * W : (q + 1) * W] = g.ctx_own[q]
    w_o = lambda: flat(g.w_o[...].reshape(32, B, D))
    g.mid[...] = dot(g.ctx2d[...], w_o()) + g.raw[p, M:, :].astype(F32) + prm[4:5]
    n2_gather = TeamGather(
        tx, near, slot, lambda q, h: g.n2_all.at[q, pl.ds(h * half_tok, half_tok)]
    )

    def norm_mid(i, _):
        rows = pl.ds(pl.multiple_of(i * 32, 32), 32)
        hat, _unused = norm_parts(g.mid[rows, :])
        g.n2_all[p, rows, :] = (hat * prm[5:6] + prm[6:7]).astype(BF)
        return 0

    for half in (0, 1):
        lax.fori_loop(half * (half_tok // 32), (half + 1) * (half_tok // 32), norm_mid, 0)
        n2_gather.start(half)
    n2_gather.forward()
    win_far.forward()
    n2_gather.pass_xn()
    cot_gather.finish()
    n2_gather.pass_diag()
    for rel in QUADS:
        n2_gather.wait_sib(rel)
    win_far.finish()
    wout_far.finish()
    tok_halves = [pl.ds(h * half_tok, half_tok) for h in (0, 1)]
    hidden_bias = jnp.concatenate([g.bslot[k, 0:1, :] for k in range(4)], axis=1)
    out_sum = TeamScatter(
        tx, near, slot, lambda q: g.pb_a.at[q], g.r1_a, g.rx_a, g.rz_a, tok_halves
    )
    n2_sum = TeamScatter(
        tx, near, slot, lambda q: g.pb_b.at[q], g.r1_b, g.rx_b, g.rz_b, tok_halves
    )
    for order in range(4):
        pair = 2 * (slot(QUADS[order]) // 2)
        w_in = flat(g.w_in[...].reshape(32, B, H))
        w_out = g.w_out[...].reshape(H, D)
        inner = dot(flat(g.n2_all[pl.ds(pair, 2)]), w_in) + hidden_bias
        act, slope = gelu_parts(inner)
        act = act.astype(BF)
        act_grad = dot_nt(flat(g.cot_all[pl.ds(pair, 2)]), w_out)
        inner_grad = (act_grad * slope).astype(BF)
        at = pl.ds(pl.multiple_of(pair * T, 2 * T), 2 * T)
        g.inner[at, :] = inner_grad
        for k in range(4):
            g.act[k, at, :] = act[:, k * H4 : (k + 1) * H4]
        g.pb_b[pl.ds(pair, 2)] = dot_nt(inner_grad, w_in).astype(BF).reshape(2, T, D)
        n2_sum.push(order)
        g.pb_a[pl.ds(pair, 2)] = dot(act, w_out).astype(BF).reshape(2, T, D)
        out_sum.push(order)
        if order:
            n2_sum.add(order - 1)
    n2_sum.add(3)
    out_sum.add(0)
    cot = lambda: flat(g.cot_all[...])
    for j in (1 - y, y):
        for k in range(2):
            g.gout_s[k, j] = dot_tn(g.act[2 * k + j], cot()).astype(BF)
    gout_own = lambda i, j: g.gout_s.at[i, j]
    gout_sum = FarSum(tx, far, zh, y, gout_own, g.gout_a, g.gout_b, g.gout_c)
    gout_sum.start(1 - zh)
    n2_sum.turn()
    out_sum.add(2)
    out_sum.add(3)
    for k in range(4):
        grad = dot_tn(flat(g.n2_all[:, :, k * Q : (k + 1) * Q]), g.inner[...])
        cut = slice(2 * (k % 2), 2 * (k % 2) + 2)
        g.gin_s[k // 2, cut] = grad.astype(BF).reshape(2, 2, 2, B, H)
    gin_own = lambda i, j: g.gin_s.at[i, :, j]
    gin_sum = FarSum(tx, far, zh, y, gin_own, g.gin_a, g.gin_b, g.gin_c)
    gin_sum.start(1 - zh)
    gout_sum.start(zh)
    inner_sum = col_sum(g.inner[...])
    for k in range(4):
        g.bp[k] = jnp.broadcast_to(inner_sum[:, k * H4 : (k + 1) * H4], (8, H4))
    gb_copies = []
    for i, rel in enumerate(FAR):
        to = 2 * ((zh + rel[0]) % 2) + (y + rel[1]) % 2
        gb_copies.append(tx.send(g.bp.at[to], g.br.at[i], far(rel)))
    gout_sum.turn()
    g.mg[...] = n2_sum.total(p)
    def norm_two_back(i, sums):
        rows = pl.ds(pl.multiple_of(i * 32, 32), 32)
        up = g.mg[rows, :]
        hat, scale = norm_parts(g.mid[rows, :])
        pull = up * prm[5:6]
        mean = jnp.mean(pull, axis=-1, keepdims=True)
        along_hat = jnp.mean(pull * hat, axis=-1, keepdims=True)
        cot_rows = g.cot_all[p, rows, :].astype(F32)
        out = cot_rows + scale * (pull - mean - hat * along_hat)
        low = out.astype(BF)
        g.mg[rows, :] = out
        g.attg[rows, :] = low
        return (
            sums[0] + col_sum(up * hat),
            sums[1] + col_sum(up),
            sums[2] + col_sum(low),
            sums[3] + col_sum(cot_rows),
        )

    zero_row = jnp.zeros((1, D), F32)
    gain_two, shift_two, bias_o, bias_out = lax.fori_loop(
        0, T // 32, norm_two_back, (zero_row, zero_row, zero_row, zero_row)
    )
    attg = g.attg[...]
    cg = dot_nt(attg, w_o()).astype(BF)
    for q in range(8):
        g.cg_send[q] = cg[:, q * W : (q + 1) * W]
    cg_copies = team_send(lambda q: g.cg_send.at[q], g.cg_all.at[p])
    g.cg_all[p] = g.cg_send[p]
    out_sum.add(1)
    for k in range(4):
        grad = dot_tn(g.ctx2d[:, k * Q : (k + 1) * Q], attg)
        cut = slice(2 * (k % 2), 2 * (k % 2) + 2)
        g.pb_o[k // 2, cut] = grad.astype(BF).reshape(2, 2, 2, B, D)
    o_sum = TeamScatter(
        tx, near, slot, lambda q: g.pb_o.at[:, q // 2, :, q % 2], g.r1_o, None, None, [0, 1]
    )
    for order in range(4):
        o_sum.push(order)
    out_sum.turn()
    gin_sum.turn()

    wait_all(cg_copies)

    def store_cg(j, at, rows):
        g.cg_sorted[pl.ds(j * T + at, 16), :] = rows.astype(BF)

    to_sorted(lambda q, at: g.cg_all[q, pl.ds(at, 16), :], store_cg)
    g.dk[...] = jnp.zeros_like(g.dk)
    g.dv[...] = jnp.zeros_like(g.dv)

    def attend_back(i):
        rows = slice(i * N, (i + 1) * N)
        end = MK + (i + 1) * N
        cg_rows = g.cg_sorted[rows, :]
        q_rows = g.qs[rows, :]
        product = cg_rows.astype(F32) * g.ctx[rows, :]
        parts = []
        for h in range(2):
            qh, ch = only(q_rows, h), only(cg_rows, h)
            delta = jnp.sum(only(product, h), axis=1, keepdims=True)
            w = g.wts[h, rows, :end]
            pull = dot_nt(ch, g.vv[:end, :])
            ds = (w.astype(F32) * (pull - delta)).astype(BF)
            parts.append(dot(ds, g.kk[:end, :]))
            g.dk[:end, :] += dot_tn(ds, qh)
            g.dv[:end, :] += dot_tn(w, ch)
        g.dq[rows, :] = jnp.where(head_lanes[0], parts[0], parts[1]) * 0.125

    attend_back(0)
    for order in range(4):
        o_sum.add(order, hand=False)
    go_copy = tx.send(g.pb_o.at[:, :, 1 - y, c], g.go_y, far((0, 1)))
    attend_back(1)
    attend_back(2)
    attend_back(3)
    def load_grads(j, at):
        keys = pl.ds(MK + j * T + at, 16)
        return jnp.concatenate(
            [g.dq[pl.ds(j * T + at, 16), :], g.dk[keys, :], g.dv[keys, :]], axis=1
        )

    def store_grads(q, at, rows):
        g.dqkv[q, pl.ds(M + at, 16), :] = rows.astype(BF)

    from_sorted(load_grads, store_grads)
    for q in range(8):
        mt = slice(q * M, (q + 1) * M)
        g.dqkv[q, :M, :W] = jnp.zeros((M, W), BF)
        g.dqkv[q, :M, W : 2 * W] = g.dk[mt, :].astype(BF)
        g.dqkv[q, :M, 2 * W :] = g.dv[mt, :].astype(BF)
    n_sum = TeamScatter(
        tx, near, slot, lambda q: g.pb_n.at[q], g.r1_n, g.rx_n, g.rz_n, tok_halves
    )
    for order in range(4):
        pair = 2 * (slot(QUADS[order]) // 2)
        rows = flat(g.dqkv[pl.ds(pair, 2), M:, :])
        g.pb_n[pl.ds(pair, 2)] = dot_nt(rows, wqkv()).astype(BF).reshape(2, T, D)
        n_sum.push(order)
        if order:
            n_sum.add(order - 1)
    n_sum.add(3)
    lo = out_sum.total(p) + g.mid[...] + prm[7:8]
    g.lo_s[...] = lo.astype(BF)
    swap_lo = swap(g.lo_s, g.lo, g.lo)
    g.vp[...] = jnp.zeros_like(g.vp)
    qkv_sum = jnp.zeros((1, 3 * W), F32)
    for q in range(8):
        qkv_sum = qkv_sum + col_sum(g.dqkv[q])
    qkv_sum8 = jnp.broadcast_to(qkv_sum, (8, 3 * W))
    ones = jnp.ones((8, 3 * W), F32)
    gains = []
    for k in range(4):
        grad = dot_tn(flat(g.n_all[:, :, k * Q : (k + 1) * Q]), flat(g.dqkv[...]))
        cut = slice(2 * (k % 2), 2 * (k % 2) + 2)
        g.gqkv_s[k // 2, cut] = grad.astype(BF).reshape(2, 2, 2, B, 3 * W)
        w = flat(g.wqkv[k // 2, cut].reshape(8, B, 3 * W)).astype(F32)
        gains.append(dot_nt(ones, grad * w, EXACT)[0:1])
    gqkv_own = lambda i, j: g.gqkv_s.at[i, :, j]
    gqkv_sum = FarSum(tx, far, zh, y, gqkv_own, g.gqkv_a, g.gqkv_b, g.gqkv_c)
    gqkv_sum.start(1 - zh)
    gin_sum.start(zh)
    gqkv_sum.start(zh)
    n_sum.turn()
    for k in range(4):
        cut = slice(2 * (k % 2), 2 * (k % 2) + 2)
        w = flat(g.wqkv[k // 2, cut].reshape(8, B, 3 * W)).astype(F32)
        shifts = dot_nt(qkv_sum8, w, EXACT)
        for i in range(2):
            at = slice(i * W, (i + 1) * W)
            shift = shifts[0:1, at]
            vec = g.pg[2 * k + i]
            g.vp[2 * k + i, 0:1, :] = (gains[k][:, at] - vec[1:2] * shift) / vec[0:1]
            g.vp[2 * k + i, 1:2, :] = shift
    g.vp[p, 2:3, :] = qkv_sum[:, :W]
    g.vp[p, 3:4, :] = qkv_sum[:, 2 * W :]
    for k in range(8):
        at = slice(k * W, (k + 1) * W)
        g.vp[k, 4:5, :] = bias_o[:, at]
        g.vp[k, 5:6, :] = gain_two[:, at]
        g.vp[k, 6:7, :] = shift_two[:, at]
        g.vp[k, 7:8, :] = bias_out[:, at]
    vec_copies = []
    for i, rel in enumerate(FAR):
        to = pl.ds(4 * ((zh + rel[0]) % 2), 4)
        vec_copies.append(tx.send(g.vp.at[to], g.vr.at[i], far(rel)))
    go_copy.wait_recv()
    for k in range(4):
        total = g.pb_o[:, k, y, c].astype(F32) + g.go_y[:, k].astype(F32)
        g.go_m[k] = total.astype(BF)
    go_team = TeamScatter(
        tx, near, slot, lambda q: g.go_m.at[q // 2], None, g.rx_o, g.rz_o, [0, 1]
    )
    for order in (0, 1):
        for half in (0, 1):
            go_team.hand(order, half)
    gqkv_sum.turn()
    g.gout[...] = gout_sum.total()
    g.gin_d[...] = flat_team(gin_sum.total())
    gin_copies = team_send(lambda q: g.gin_d.at[q], g.gin_e.at[p])
    g.gin_e[p] = g.gin_d[p]
    wait_all(gb_copies)
    g.gbin[...] = (g.bp[e] + g.br[0] + g.br[1] + g.br[2])[:1]
    wait_all(vec_copies)
    g.vs[...] = g.vp[pl.ds(4 * zh, 4)] + g.vr[0] + g.vr[1] + g.vr[2]
    vec_copies = team_send(lambda q: g.vs.at[q // 2], g.va.at[p])
    g.va[p] = g.vs[zx]
    g.mid[...] = n_sum.total(p)

    def norm_one_back(i, _):
        rows = pl.ds(pl.multiple_of(i * 32, 32), 32)
        hat, scale = norm_parts(
            g.raw[p, pl.ds(pl.multiple_of(M + i * 32, 32), 32), :].astype(F32)
        )
        pull = g.mid[rows, :] * prm[0:1]
        mean = jnp.mean(pull, axis=-1, keepdims=True)
        along_hat = jnp.mean(pull * hat, axis=-1, keepdims=True)
        out = g.mg[rows, :] + scale * (pull - mean - hat * along_hat)
        g.ig_s[rows, :] = out.astype(BF)
        return 0

    lax.fori_loop(0, T // 32, norm_one_back, 0)
    swap_ig = swap(g.ig_s, g.ig, g.ig)
    go_team.turn()
    g.gqkv_d[...] = flat_team(gqkv_sum.total())
    gqkv_copies = team_send(lambda q: g.gqkv_d.at[q], g.gqkv_e.at[p])
    g.gqkv_e[p] = g.gqkv_d[p]
    g.go_s[...] = go_team.total(p).astype(BF)
    go_copy = tx.send(g.go_s.at[1 - zh], g.go_c, far((1, 0)))
    wait_all(gin_copies)
    for q in range(8):
        for k in range(4):
            at = (16 * (k // 2) + 4 * (q // 2) + 2 * (k % 2) + q % 2) * H4
            g.gin[:, at : at + H4] = g.gin_e[q, :, k * H4 : (k + 1) * H4].astype(F32)
    wait_all(vec_copies)
    total = g.va[0]
    for q in range(1, 8):
        total = total + g.va[q]
    g.gvec[...] = total
    wait_all(gqkv_copies)
    for q in range(8):
        for i, out in enumerate((g.gq, g.gk, g.gv)):
            out[:, q * W : (q + 1) * W] = g.gqkv_e[q, :, i * W : (i + 1) * W].astype(F32)
    go_copy.wait_recv()
    g.go[...] = g.go_s[zh].astype(F32) + g.go_c[...].astype(F32)
    swap_lo.wait_recv()
    swap_ig.wait_recv()
    tx.drain()

    @pl.when(moves)
    def _():
        for copy in swaps:
            copy.wait_send()


def flat_team(value):
    return value.astype(BF).reshape((8,) + value.shape[2:])


def finish_kernel(share, *refs):
    ins, outs, held = refs[:10], refs[10:20], refs[20:30]
    wide, picked, sems = refs[30:]
    loads = [pltpu.make_async_copy(ins[i], held[i], sems.at[i]) for i in range(10)]
    for copy in loads:
        copy.start()
    stores = []
    for i in (0, 2, 3, 4, 5, 6, 7, 9, 1, 8):
        loads[i].wait()
        src = held[i]
        if i == 1:
            wide[...] = src[...].astype(F32)
            src = wide
        if i == 8:
            mine = lax.axis_index("dp")
            part = src[:, :share]
            for k in range(1, src.shape[1] // share):
                part = jnp.where(mine == k, src[:, k * share : (k + 1) * share], part)
            picked[...] = part
            src = picked
        stores.append(pltpu.make_async_copy(src, outs[i], sems.at[10 + i]))
        stores[-1].start()
    for copy in stores:
        copy.wait()


def run_layer(layer_input, memory, cotangent, block_order, w_query, w_key, w_value, w_output, w_in, w_out, vectors, b_in):
    T, D = layer_input.shape[1:]
    M = memory.shape[1]
    FF = w_in.shape[1]
    W = D // 8
    share = vectors.shape[1]
    shapes = scratch_list(T, M, D, FF)
    vmem = pl.BlockSpec(memory_space=pltpu.VMEM)
    smem = pl.BlockSpec(memory_space=pltpu.SMEM)
    hbm = pl.BlockSpec(memory_space=pl.ANY)
    outs = pl.pallas_call(
        functools.partial(layer_kernel, T, M, D, FF, share),
        out_shape=(
            jax.ShapeDtypeStruct((T, D), BF),
            jax.ShapeDtypeStruct((T, D), BF),
            jax.ShapeDtypeStruct(w_query.shape, F32),
            jax.ShapeDtypeStruct(w_key.shape, F32),
            jax.ShapeDtypeStruct(w_value.shape, F32),
            jax.ShapeDtypeStruct(w_output.shape, F32),
            jax.ShapeDtypeStruct(w_in.shape, F32),
            jax.ShapeDtypeStruct(w_out.shape, F32),
            jax.ShapeDtypeStruct((8, W), F32),
            jax.ShapeDtypeStruct((1, b_in.shape[0]), F32),
        ),
        in_specs=[hbm, hbm, hbm, smem] + [hbm] * 6 + [vmem] * 2,
        out_specs=[vmem] * 10,
        scratch_shapes=[pltpu.VMEM(shape, kind) for shape, kind in shapes.values()]
        + [pltpu.SemaphoreType.DMA((SEMS,)), pltpu.SemaphoreType.DMA((SEMS,))],
        compiler_params=pltpu.CompilerParams(
            collective_id=0, has_side_effects=True, vmem_limit_bytes=63 * 2**20
        ),
    )(layer_input[0], memory[0], cotangent[0], block_order, w_query, w_key, w_value, w_output, w_in, w_out, vectors, b_in[None])
    final = [jax.ShapeDtypeStruct(outs[0].shape, BF), jax.ShapeDtypeStruct(outs[1].shape, F32)]
    final += [jax.ShapeDtypeStruct(out.shape, F32) for out in outs[2:8]]
    final += [jax.ShapeDtypeStruct((8, share), F32), jax.ShapeDtypeStruct((1, b_in.shape[0]), F32)]
    lo, ig, gq, gk, gv, go, gin, gout, gvec, gbin = pl.pallas_call(
        functools.partial(finish_kernel, share),
        out_shape=final,
        in_specs=[hbm] * 10,
        out_specs=[hbm] * 10,
        scratch_shapes=[pltpu.VMEM(out.shape, out.dtype) for out in outs]
        + [
            pltpu.VMEM((T, D), F32),
            pltpu.VMEM((8, share), F32),
            pltpu.SemaphoreType.DMA((20,)),
        ],
        compiler_params=pltpu.CompilerParams(vmem_limit_bytes=60 * 2**20),
    )(*outs)
    return (lo[None], ig[None], gq, gk, gv, go, gin, gout, gvec, gbin[0])


masked_value = -1e30


def passed_along(block, axis, distance):
    devices = range(lax.axis_size(axis))
    route = [((i - distance) % len(devices), i) for i in devices]
    return lax.ppermute(block, axis, route)


def layer_norm(values, gain, shift):
    center = values - jnp.mean(values, axis=-1, keepdims=True)
    spread = jnp.mean(center * center, axis=-1, keepdims=True)
    return center * lax.rsqrt(spread + 1e-05) * gain + shift


def contract_rows(left, right):
    return lax.dot_general(
        left, right, (((0,), (0,)), ((), ())), preferred_element_type=jnp.float32
    )


def times_transposed(left, right):
    return lax.dot_general(
        left, right, (((1,), (1,)), ((), ())), preferred_element_type=jnp.float32
    )


def split_heads(matrix, heads):
    return matrix.reshape(matrix.shape[0], heads, matrix.shape[1] // heads)


def score_block(query_heads, key_rows):
    key_heads = split_heads(key_rows, query_heads.shape[1])
    return (
        jnp.einsum("qhd,khd->hqk", query_heads, key_heads, preferred_element_type=jnp.float32)
        * 0.125
    )


def lookup_block(order, device):
    return jnp.sum(jnp.where(jnp.arange(order.shape[0]) == device, order, 0))


def split_piece(piece, rows_dev, mem_rows):
    shards = piece.shape[0] // rows_dev
    blocks = piece.reshape(shards, rows_dev, piece.shape[1])
    memory_part = blocks[:, :mem_rows].reshape(shards * mem_rows, piece.shape[1])
    token_part = blocks[:, mem_rows:].reshape(shards * (rows_dev - mem_rows), piece.shape[1])
    return (shards, memory_part, token_part)


def piece_positions(order, shards, tok_rows):
    shard_ids = jnp.arange(shards)
    hits = shard_ids[:, None] == jnp.arange(order.shape[0])[None, :]
    starts = jnp.sum(jnp.where(hits, order[None, :], 0), axis=1)
    positions = (starts[:, None] * tok_rows + jnp.arange(tok_rows)[None, :]).reshape(
        shards * tok_rows
    )
    return (starts, positions)


def softmax_stats(carry, scores):
    running, total = carry
    top = jnp.maximum(running, jnp.max(scores, axis=2))
    total = total * jnp.exp(running - top) + jnp.sum(jnp.exp(scores - top[:, :, None]), axis=2)
    return (top, total)


def per_device(
    layer_input,
    memory,
    cotangent,
    block_order,
    w_query,
    w_key,
    w_value,
    w_output,
    w_in,
    w_out,
    vectors,
    b_in,
):
    bf16 = jnp.bfloat16
    gathered = (
        lax.all_gather(w_query.astype(bf16), ("blk", "dp"), axis=0, tiled=True),
        lax.all_gather(w_key.astype(bf16), ("blk", "dp"), axis=0, tiled=True),
        lax.all_gather(w_value.astype(bf16), ("blk", "dp"), axis=0, tiled=True),
        lax.all_gather(w_output.astype(bf16), ("blk", "dp"), axis=0, tiled=True),
        lax.all_gather(w_in.astype(bf16), ("blk", "dp"), axis=0, tiled=True),
        lax.all_gather(w_out.astype(bf16), ("blk", "dp"), axis=0, tiled=True),
        lax.all_gather(vectors.astype(bf16), ("blk", "dp"), axis=1, tiled=True),
        lax.all_gather(b_in.astype(bf16), ("blk", "dp"), axis=0, tiled=True),
    )
    (
        query_full,
        key_full,
        value_full,
        output_full,
        inner_full,
        outer_full,
        vector_full,
        inner_low,
    ) = gathered
    params = vector_full.astype(jnp.float32)
    inner_shift = inner_low.astype(jnp.float32)
    heads = HEADS
    tokens = layer_input[0].astype(jnp.float32)
    recalled = memory[0].astype(jnp.float32)
    tok_rows = tokens.shape[0]
    mem_rows = recalled.shape[0]
    rows_dev = tok_rows + mem_rows
    width = tokens.shape[1]
    blocks_total = lax.axis_size("blk")
    here = lax.axis_index("blk")
    own_block = lookup_block(block_order, here)
    query_pos = own_block * tok_rows + jnp.arange(tok_rows)
    both_rows = jnp.concatenate([recalled, tokens], axis=0)
    normed = layer_norm(both_rows, params[0], params[1]).astype(bf16)
    normed_tok = normed[mem_rows:]
    queries = (
        jnp.dot(normed_tok, query_full, preferred_element_type=jnp.float32) + params[2]
    ).astype(bf16)
    keys_all = jnp.dot(normed, key_full, preferred_element_type=jnp.float32).astype(bf16)
    values_all = (
        jnp.dot(normed, value_full, preferred_element_type=jnp.float32) + params[3]
    ).astype(bf16)
    query_heads = split_heads(queries, heads)

    def causal(scores, key_pos):
        return jnp.where(key_pos[None, None, :] <= query_pos[None, :, None], scores, masked_value)

    start_stats = (
        jnp.full((heads, tok_rows), masked_value, jnp.float32),
        jnp.zeros((heads, tok_rows), jnp.float32),
    )
    carry = start_stats
    shards, memory_part, token_part = split_piece(
        lax.all_gather(keys_all, "blk", axis=0, tiled=True), rows_dev, mem_rows
    )
    starts, token_pos = piece_positions(block_order, shards, tok_rows)
    carry = softmax_stats(carry, score_block(query_heads, memory_part))

    def with_tokens(state):
        return softmax_stats(state, causal(score_block(query_heads, token_part), token_pos))

    def without_tokens(state):
        return state

    running, total = lax.cond(jnp.any(starts <= own_block), with_tokens, without_tokens, carry)
    log_total = running + jnp.log(total)

    def value_part(context, part, key_pos):
        scores = score_block(query_heads, part[:, :width])
        if key_pos is not None:
            scores = causal(scores, key_pos)
        weights = jnp.exp(scores - log_total[:, :, None]).astype(bf16)
        return context + jnp.einsum(
            "hqk,khd->qhd",
            weights,
            split_heads(part[:, width:], heads),
            preferred_element_type=jnp.float32,
        )

    key_values = jnp.concatenate([keys_all, values_all], axis=1)
    context = jnp.zeros((tok_rows, heads, width // heads), jnp.float32)
    shards, memory_part, add_token_part = split_piece(
        lax.all_gather(key_values, "blk", axis=0, tiled=True), rows_dev, mem_rows
    )
    starts, add_token_pos = piece_positions(block_order, shards, tok_rows)
    context = value_part(context, memory_part, None)

    def with_tokens(state):
        return value_part(state, add_token_part, add_token_pos)

    def without_tokens(state):
        return state

    context = lax.cond(jnp.any(starts <= own_block), with_tokens, without_tokens, context)
    context_low = context.reshape(tok_rows, width).astype(bf16)
    attended = jnp.dot(context_low, output_full, preferred_element_type=jnp.float32) + params[4]
    middle = tokens + attended
    normed_two = layer_norm(middle, params[5], params[6]).astype(bf16)
    inner = jnp.dot(normed_two, inner_full, preferred_element_type=jnp.float32) + inner_shift
    activated = jax.nn.gelu(inner, approximate=True).astype(bf16)
    result = middle + jnp.dot(activated, outer_full, preferred_element_type=jnp.float32) + params[7]
    output = result.astype(bf16)
    upstream = cotangent[0]
    upstream_full = upstream.astype(jnp.float32)
    grad_outer = contract_rows(activated, upstream)
    grad_outer_bias = jnp.sum(upstream_full, axis=0)
    act_grad = times_transposed(upstream, outer_full)
    _, gelu_back = jax.vjp(functools.partial(jax.nn.gelu, approximate=True), inner)
    inner_grad = gelu_back(act_grad)[0].astype(bf16)
    grad_inner = contract_rows(normed_two, inner_grad)
    grad_inner_bias = jnp.sum(inner_grad.astype(jnp.float32), axis=0)
    normed_two_grad = times_transposed(inner_grad, inner_full)
    _, norm_two_back = jax.vjp(layer_norm, middle, params[5], params[6])
    middle_part, grad_gain_two, grad_shift_two = norm_two_back(normed_two_grad)
    middle_grad = upstream_full + middle_part
    attended_grad = middle_grad.astype(bf16)
    grad_output = contract_rows(context_low, attended_grad)
    grad_output_bias = jnp.sum(attended_grad.astype(jnp.float32), axis=0)
    context_grad = times_transposed(attended_grad, output_full).astype(bf16)
    context_heads = split_heads(context_grad, heads)
    delta = jnp.einsum("qhd,qhd->hq", context_heads.astype(jnp.float32), context)

    def attend_back(queries_grad, part, key_pos):
        count = part.shape[0]
        key_heads = split_heads(part[:, :width], heads)
        value_heads = split_heads(part[:, width:], heads)
        scores = score_block(query_heads, part[:, :width])
        if key_pos is not None:
            scores = causal(scores, key_pos)
        exact = jnp.exp(scores - log_total[:, :, None])
        weight_low = exact.astype(bf16)
        weight_grad = jnp.einsum(
            "qhd,khd->hqk", context_heads, value_heads, preferred_element_type=jnp.float32
        )
        score_grad = (exact * (weight_grad - delta[:, :, None])).astype(bf16)
        queries_grad = (
            queries_grad
            + jnp.einsum("hqk,khd->qhd", score_grad, key_heads, preferred_element_type=jnp.float32)
            * 0.125
        )
        key_grad = (
            jnp.einsum("hqk,qhd->khd", score_grad, query_heads, preferred_element_type=jnp.float32)
            * 0.125
        )
        value_grad = jnp.einsum(
            "hqk,qhd->khd", weight_low, context_heads, preferred_element_type=jnp.float32
        )
        return (
            queries_grad,
            jnp.concatenate(
                [key_grad.reshape(count, width), value_grad.reshape(count, width)], axis=1
            ),
        )

    def visit(queries_grad, travelling, travel_grad, anchor):
        anchor_block = lookup_block(block_order, anchor)
        queries_grad, memory_grad = attend_back(queries_grad, travelling[:mem_rows], None)
        token_pos = anchor_block * tok_rows + jnp.arange(tok_rows)

        def with_tokens(state):
            return attend_back(state, travelling[mem_rows:], token_pos)

        def without_tokens(state):
            return (state, jnp.zeros((tok_rows, 2 * width), jnp.float32))

        queries_grad, token_grad = lax.cond(
            anchor_block <= own_block, with_tokens, without_tokens, queries_grad
        )
        return (queries_grad, travel_grad + jnp.concatenate([memory_grad, token_grad], axis=0))

    def pass_grads(values):
        return passed_along(values.astype(jnp.bfloat16), "blk", 1).astype(values.dtype)

    queries_grad, travel_grad = visit(
        jnp.zeros((tok_rows, heads, width // heads), jnp.float32),
        key_values,
        jnp.zeros((rows_dev, 2 * width), jnp.float32),
        here,
    )

    def turn(step, state):
        queries_grad, travelling, travel_grad = state
        travelling = passed_along(travelling, "blk", 1)
        travel_grad = pass_grads(travel_grad)
        anchor = (here - step) % blocks_total
        queries_grad, travel_grad = visit(queries_grad, travelling, travel_grad, anchor)
        return (queries_grad, travelling, travel_grad)

    queries_grad, travelling, travel_grad = lax.fori_loop(
        1, blocks_total, turn, (queries_grad, key_values, travel_grad)
    )
    travel_grad = pass_grads(travel_grad)
    pair_grad = travel_grad.astype(bf16)
    key_grad = pair_grad[:, :width]
    value_grad = pair_grad[:, width:]
    query_grad = queries_grad.reshape(tok_rows, width).astype(bf16)
    grad_query = contract_rows(normed_tok, query_grad)
    grad_query_bias = jnp.sum(query_grad.astype(jnp.float32), axis=0)
    grad_key = contract_rows(normed, key_grad)
    grad_value = contract_rows(normed, value_grad)
    grad_value_bias = jnp.sum(value_grad.astype(jnp.float32), axis=0)
    normed_grad = times_transposed(key_grad, key_full) + times_transposed(value_grad, value_full)
    query_part = times_transposed(query_grad, query_full)
    normed_grad = normed_grad + jnp.concatenate(
        [jnp.zeros((mem_rows, width), jnp.float32), query_part], axis=0
    )
    _, norm_one_back = jax.vjp(layer_norm, both_rows, params[0], params[1])
    rows_grad, grad_gain_one, grad_shift_one = norm_one_back(normed_grad)
    input_grad = middle_grad + rows_grad[mem_rows:]
    vector_grad = jnp.stack(
        [
            grad_gain_one,
            grad_shift_one,
            grad_query_bias,
            grad_value_bias,
            grad_output_bias,
            grad_gain_two,
            grad_shift_two,
            grad_outer_bias,
        ]
    )
    out_query, out_key, out_value, out_output, out_inner, out_outer, out_vectors, out_bias = (
        lax.psum_scatter(grad_query, ("blk", "dp"), scatter_dimension=0, tiled=True),
        lax.psum_scatter(grad_key, ("blk", "dp"), scatter_dimension=0, tiled=True),
        lax.psum_scatter(grad_value, ("blk", "dp"), scatter_dimension=0, tiled=True),
        lax.psum_scatter(grad_output, ("blk", "dp"), scatter_dimension=0, tiled=True),
        lax.psum_scatter(grad_inner, ("blk", "dp"), scatter_dimension=0, tiled=True),
        lax.psum_scatter(grad_outer, ("blk", "dp"), scatter_dimension=0, tiled=True),
        lax.psum_scatter(vector_grad, ("blk", "dp"), scatter_dimension=1, tiled=True),
        lax.psum_scatter(grad_inner_bias, ("blk", "dp"), scatter_dimension=0, tiled=True),
    )
    return (
        output[None],
        input_grad[None],
        out_query,
        out_key,
        out_value,
        out_output,
        out_inner,
        out_outer,
        out_vectors,
        out_bias,
    )


def solution(mesh):
    rows = P("dp", "blk", None)
    shard = P(("blk", "dp"), None)
    in_specs = (rows, rows, rows, P()) + (shard,) * 6 + (P(None, ("blk", "dp")), P(("blk", "dp")))
    out_specs = (rows, rows) + (shard,) * 6 + (P(None, ("blk", "dp")), P(("blk", "dp")))
    planes = mesh.shape["blk"] == 8 and mesh.shape["dp"] == 4
    return jax.shard_map(
        run_layer if planes else per_device,
        mesh=mesh,
        in_specs=in_specs,
        out_specs=out_specs,
        check_vma=False,
    )
```

```python
import functools

import jax
import jax.numpy as jnp
from jax import lax
from jax.experimental import pallas as pl
from jax.experimental.pallas import tpu as pltpu
from jax.sharding import PartitionSpec as P

HEADS = 16
BF = jnp.bfloat16
F32 = jnp.float32
MESH = pl.DeviceIdType.MESH
EXACT = lax.Precision.HIGHEST


def dot(a, b):
    return lax.dot_general(a, b, (((1,), (0,)), ((), ())), preferred_element_type=F32)


def dot_nt(a, b, precision=None):
    return lax.dot_general(
        a, b, (((1,), (1,)), ((), ())), preferred_element_type=F32, precision=precision
    )


def dot_tn(a, b):
    return lax.dot_general(a, b, (((0,), (0,)), ((), ())), preferred_element_type=F32)


def flat(value):
    return value.reshape(-1, value.shape[-1])


def col_sum(value):
    return jnp.sum(value.astype(F32), axis=0, keepdims=True)


def norm_parts(rows):
    center = rows - jnp.mean(rows, axis=-1, keepdims=True)
    spread = jnp.mean(center * center, axis=-1, keepdims=True)
    scale = lax.rsqrt(spread + 1e-05)
    return center * scale, scale


def gelu_parts(v):
    square = v * v
    t = jnp.tanh(0.7978845608 * v * (1.0 + 0.044715 * square))
    half = 0.5 * (1.0 + t)
    slope = half + 0.5 * v * (1.0 - t * t) * (0.7978845608 * (1.0 + 3 * 0.044715 * square))
    return v * half, slope


IN_NAMES = ["x", "mem", "cot", "order", "wq", "wk", "wv", "wo", "win", "wout", "vec", "bias"]
OUT_NAMES = ["lo", "ig", "gq", "gk", "gv", "go", "gin", "gout", "gvec", "gbin"]
TEAM = [(1, 1, 1), (1, 1, 0), (1, 0, 1), (1, 0, 0), (0, 1, 1), (0, 1, 0), (0, 0, 1)]
FAR = [(1, 0), (0, 1), (1, 1)]
QUADS = [(1, 1, 0), (0, 1, 0), (1, 0, 0), (0, 0, 0)]
SIB, XN, ZN = (0, 0, 1), (0, 1, 0), (1, 0, 0)


def scratch_list(T, M, D, FF):
    R = T + M
    H = FF // 8
    H4 = H // 4
    W = D // 8
    B = D // 32
    S = 8 * T
    K = 8 * R
    grid = (2, 4, 2, 2, B)
    return dict(
        f_qkv=((3, B, D), F32),
        f_o=((B, D), F32),
        f_in=((B, FF), F32),
        f_out=((H4, D), F32),
        n_all=((8, R, D), BF),
        raw=((8, R, D), BF),
        cot_all=((8, T, D), BF),
        n2_all=((8, T, D), BF),
        pq=((8, B, 3 * W), BF),
        pi=((8, B, H), BF),
        wqkv=(grid + (3 * W,), BF),
        w_in=(grid + (H,), BF),
        w_out=((2, 2, H4, D), BF),
        w_o=(grid + (D,), BF),
        vg1=((8, 8, W), F32),
        vg2=((4, 4, 8, W), F32),
        pg=((8, 8, W), F32),
        bslot=((4, 8, H4), F32),
        prm=((8, D), F32),
        qkv=((8, R, 3 * W), BF),
        qs=((S, W), BF),
        kk=((K, W), BF),
        vv=((K, W), BF),
        wts=((2, S, K), BF),
        ctx=((S, W), F32),
        ctx_send=((8, T, W), BF),
        ctx_own=((8, T, W), BF),
        ctx2d=((T, D), BF),
        mid=((T, D), F32),
        act=((4, S, H4), BF),
        inner=((S, H), BF),
        pb_a=((8, T, D), BF),
        r1_a=((4, T, D), BF),
        rx_a=((2, T, D), BF),
        rz_a=((T, D), BF),
        pb_b=((8, T, D), BF),
        r1_b=((4, T, D), BF),
        rx_b=((2, T, D), BF),
        rz_b=((T, D), BF),
        pb_n=((8, T, D), BF),
        r1_n=((4, T, D), BF),
        rx_n=((2, T, D), BF),
        rz_n=((T, D), BF),
        mg=((T, D), F32),
        attg=((T, D), BF),
        cg_send=((8, T, W), BF),
        cg_all=((8, T, W), BF),
        pb_o=(grid + (D,), BF),
        r1_o=((4, 2, 2, B, D), BF),
        rx_o=((2, 2, B, D), BF),
        rz_o=((2, B, D), BF),
        go_y=((2, 4, B, D), BF),
        go_m=((4, 2, B, D), BF),
        go_s=((2, B, D), BF),
        go_c=((B, D), BF),
        cg_sorted=((S, W), BF),
        dq=((S, W), F32),
        dk=((K, W), F32),
        dv=((K, W), F32),
        dqkv=((8, R, 3 * W), BF),
        gout_s=((2, 2, H4, D), BF),
        gout_a=((2, H4, D), BF),
        gout_b=((H4, D), BF),
        gout_c=((H4, D), BF),
        gin_s=(grid + (H,), BF),
        gin_a=((2, 4, 2, B, H), BF),
        gin_b=((4, 2, B, H), BF),
        gin_c=((4, 2, B, H), BF),
        gin_d=((8, B, H), BF),
        gin_e=((8, B, H), BF),
        gqkv_s=(grid + (3 * W,), BF),
        gqkv_a=((2, 4, 2, B, 3 * W), BF),
        gqkv_b=((4, 2, B, 3 * W), BF),
        gqkv_c=((4, 2, B, 3 * W), BF),
        gqkv_d=((8, B, 3 * W), BF),
        gqkv_e=((8, B, 3 * W), BF),
        vp=((8, 8, W), F32),
        vr=((3, 4, 8, W), F32),
        vs=((4, 8, W), F32),
        va=((8, 8, W), F32),
        bp=((4, 8, H4), F32),
        br=((3, 8, H4), F32),
        lo_s=((T, D), BF),
        ig_s=((T, D), BF),
    )


SEMS = 320


class Sender:
    def __init__(self, ssem, rsem):
        self.ssem, self.rsem, self.count, self.pending = ssem, rsem, 0, []

    def make(self, src, dst, target):
        at = self.count
        self.count += 1
        return pltpu.make_async_remote_copy(
            src_ref=src,
            dst_ref=dst,
            send_sem=self.ssem.at[at],
            recv_sem=self.rsem.at[at],
            device_id=target,
            device_id_type=MESH,
        )

    def local(self, src, dst):
        at = self.count
        self.count += 1
        copy = pltpu.make_async_copy(src, dst, self.rsem.at[at])
        copy.start()
        return copy

    def plan(self, src, dst, target):
        copy = self.make(src, dst, target)
        self.pending.append(copy)
        return copy

    def send(self, src, dst, target):
        copy = self.plan(src, dst, target)
        copy.start()
        return copy

    def drain(self):
        for copy in self.pending:
            copy.wait_send()


class TeamGather:
    def __init__(self, tx, near, slot, ref):
        def plan(rel, to):
            ats = [ref(slot(rel), half) for half in (0, 1)]
            return [tx.plan(at, at, near(to)) for at in ats]

        self.zn, self.xn = plan((0, 0, 0), ZN), plan((0, 0, 0), XN)
        self.diag = plan(ZN, XN)
        self.sib = {rel: plan(rel, SIB) for rel in QUADS}

    def start(self, half):
        self.zn[half].start()
        self.xn[half].start()
        self.sib[(0, 0, 0)][half].start()

    def forward(self):
        for half in (0, 1):
            self.zn[half].wait_recv()
            self.diag[half].start()
            self.sib[ZN][half].start()

    def pass_xn(self):
        for half in (0, 1):
            self.xn[half].wait_recv()
            self.sib[XN][half].start()

    def pass_diag(self):
        for half in (0, 1):
            self.diag[half].wait_recv()
            self.sib[(1, 1, 0)][half].start()

    def wait_sib(self, rel):
        for copy in self.sib[rel]:
            copy.wait_recv()

    def finish(self):
        self.pass_xn()
        self.pass_diag()
        for rel in QUADS:
            self.wait_sib(rel)


class FarGather:
    def __init__(self, tx, far, zh, y, ref):
        own, passed = ref(zh, y), ref(1 - zh, y)
        self.over_z = tx.plan(own, own, far((1, 0)))
        self.over_y = tx.plan(own, own, far((0, 1)))
        self.passed = tx.plan(passed, passed, far((0, 1)))

    def start(self):
        self.over_z.start()
        self.over_y.start()

    def forward(self):
        self.over_z.wait_recv()
        self.passed.start()

    def finish(self):
        self.over_y.wait_recv()
        self.passed.wait_recv()


class TeamScatter:
    def __init__(self, tx, near, slot, buf, first, cross, last, halves):
        self.tx, self.near, self.slot, self.buf = tx, near, slot, buf
        self.first, self.cross, self.last, self.halves = first, cross, last, halves
        self.sib, self.turned, self.ended = {}, [], []

    def push(self, order):
        rel = QUADS[order]
        src = self.buf(self.slot((rel[0], rel[1], 1)))
        self.sib[order] = self.tx.send(src, self.first.at[order], self.near(SIB))

    def sum(self, order, half):
        own = self.buf(self.slot(QUADS[order]))
        part, more = own.at[half], self.first.at[order].at[half]
        part[...] = (part[...].astype(F32) + more[...].astype(F32)).astype(BF)

    def hand(self, order, half):
        part = self.buf(self.slot(QUADS[order])).at[half]
        to = self.cross.at[order].at[half]
        copy = self.tx.send(part, to, self.near(XN))
        (self.ended if order else self.turned).append(copy)

    def add(self, order, hand=True):
        self.sib[order].wait_recv()
        for half in self.halves:
            self.sum(order, half)
            if hand and order < 2:
                self.hand(order, half)

    def turn(self):
        own = self.buf(self.slot(ZN))
        for half, copy in zip(self.halves, self.turned):
            copy.wait_recv()
            part, more = own.at[half], self.cross.at[0].at[half]
            part[...] = (part[...].astype(F32) + more[...].astype(F32)).astype(BF)
            self.ended.append(self.tx.send(part, self.last.at[half], self.near(ZN)))

    def total_half(self, own, at):
        half = self.halves[at]
        self.ended[at].wait_recv()
        self.ended[2 + at].wait_recv()
        return (
            self.buf(own).at[half][...].astype(F32)
            + self.cross.at[1].at[half][...].astype(F32)
            + self.last.at[half][...].astype(F32)
        )

    def total(self, own):
        for copy in self.ended:
            copy.wait_recv()
        return (
            self.buf(own)[...].astype(F32)
            + self.cross[1].astype(F32)
            + self.last[...].astype(F32)
        )


class FarSum:
    def __init__(self, tx, far, zh, y, own, first, mid, last):
        self.tx, self.far, self.zh, self.y, self.own = tx, far, zh, y, own
        self.first, self.mid, self.last, self.copies = first, mid, last, []

    def start(self, half):
        src = self.own(half, 1 - self.y)
        self.copies.append(self.tx.send(src, self.first.at[half], self.far((0, 1))))

    def both(self, half):
        return self.own(half, self.y)[...].astype(F32) + self.first[half].astype(F32)

    def turn(self):
        self.copies[0].wait_recv()
        self.mid[...] = self.both(1 - self.zh).astype(BF)
        self.ended = self.tx.send(self.mid, self.last, self.far((1, 0)))

    def total(self):
        self.copies[1].wait_recv()
        self.ended.wait_recv()
        return self.both(self.zh) + self.last[...].astype(F32)


def layer_kernel(T, M, D, FF, share, *refs):
    names = IN_NAMES + OUT_NAMES + list(scratch_list(T, M, D, FF))
    ssem, rsem = refs[len(names) :]
    g = type("Refs", (), dict(zip(names, refs)))
    R, H, Q, W, S = T + M, FF // 8, D // 4, D // 8, 8 * T
    H4, B = H // 4, D // 32
    MK = 8 * M
    tx = Sender(ssem, rsem)

    b, d = lax.axis_index("blk"), lax.axis_index("dp")
    z, x, y, c = b // 2, b % 2, d // 2, d % 2
    zh, zl = z // 2, z % 2
    zx = 2 * zl + x
    p = 2 * zx + c
    e = 2 * zh + y

    def dev(zh, zl, x, y, c):
        return (4 * zh + 2 * zl + x, 2 * y + c)

    def near(rel):
        return dev(zh, (zl + rel[0]) % 2, (x + rel[1]) % 2, y, (c + rel[2]) % 2)

    def slot(rel):
        return 4 * ((zl + rel[0]) % 2) + 2 * ((x + rel[1]) % 2) + (c + rel[2]) % 2

    def far(rel):
        return dev((zh + rel[0]) % 2, zl, x, (y + rel[1]) % 2, c)

    partner = dev(c, zl, x, y, zh)
    partner_slot = 2 * zx + zh
    stays = c == zh
    moves = jnp.logical_not(stays)
    outer = zl == zh
    inner = jnp.logical_not(outer)

    barrier = pltpu.get_barrier_semaphore()
    for rel in TEAM:
        pl.semaphore_signal(barrier, inc=1, device_id=near(rel), device_id_type=MESH)
    for rel in FAR:
        pl.semaphore_signal(barrier, inc=1, device_id=far(rel), device_id_type=MESH)

    @pl.when(moves)
    def _():
        pl.semaphore_signal(barrier, inc=1, device_id=partner, device_id_type=MESH)

    loads = [tx.local(w, g.f_qkv.at[i]) for i, w in enumerate((g.wq, g.wk, g.wv))]
    loads_o = tx.local(g.wo, g.f_o)
    loads_in = tx.local(g.win, g.f_in)
    loads_out = tx.local(g.wout, g.f_out)
    share_lane = lax.broadcasted_iota(jnp.int32, (8, W), 1) // share
    low = g.vec[...].astype(BF).astype(F32)
    spread = jnp.concatenate([low] * (W // share), axis=1)
    g.vg1[p] = jnp.where(share_lane == 2 * y + c, spread, 0.0)
    g.bslot[e] = jnp.broadcast_to(g.bias[...].astype(BF).astype(F32), (8, H4))
    loads_o.wait()
    g.w_o[zh, zx, y, c] = g.f_o[...].astype(BF)
    for copy in loads:
        copy.wait()
    for q in range(8):
        for i in range(3):
            g.pq[q, :, i * W : (i + 1) * W] = g.f_qkv[i, :, q * W : (q + 1) * W].astype(BF)
    g.wqkv[zh, zx, y, c] = g.pq[p]
    loads_in.wait()
    for q in range(8):
        for k in range(4):
            at = (16 * (k // 2) + 4 * (q // 2) + 2 * (k % 2) + q % 2) * H4
            g.pi[q, :, k * H4 : (k + 1) * H4] = g.f_in[:, at : at + H4].astype(BF)
    g.w_in[zh, zx, y, c] = g.pi[p]
    loads_out.wait()
    g.w_out[zh, y] = g.f_out[...].astype(BF)
    @pl.when(moves)
    def _():
        pl.semaphore_wait(barrier, 11)

    @pl.when(stays)
    def _():
        pl.semaphore_wait(barrier, 10)

    swaps = []

    class Swap:
        def __init__(self, src, dst_there, dst_here):
            self.copy = tx.make(src, dst_there, partner)
            self.here = pltpu.make_async_copy(src, dst_here, rsem.at[tx.count - 1])
            swaps.append(self.copy)

        def start(self):
            pl.when(moves)(self.copy.start)
            pl.when(stays)(self.here.start)

        def wait_recv(self):
            self.copy.wait_recv()

    def swap(src, dst_there, dst_here):
        copy = Swap(src, dst_there, dst_here)
        copy.start()
        return copy

    def team_send(src, dst):
        return [tx.send(src(slot(rel)), dst, near(rel)) for rel in TEAM]

    def wait_all(copies):
        for copy in copies:
            copy.wait_recv()

    vec_copies = [tx.send(g.vg1.at[p], g.vg1.at[p], near(rel)) for rel in TEAM]
    qkv_copies = team_send(lambda q: g.pq.at[q], g.wqkv.at[zh, zx, y, c])
    wo_far = FarGather(tx, far, zh, y, lambda i, j: g.w_o.at[i, zx, j, c])
    wo_far.start()
    half_rows, half_tok = R // 2, T // 2
    early = half_rows - M
    raw_here, raw_there = g.raw.at[p], g.raw.at[partner_slot]
    cuts = [
        (g.mem, pl.ds(0, M)),
        (g.x.at[pl.ds(0, early)], pl.ds(M, early)),
        (g.x.at[pl.ds(early, T - early)], pl.ds(half_rows, half_rows)),
    ]
    swap_m, swap_a, swap_b = [
        swap(src, raw_there.at[to], raw_here.at[to]) for src, to in cuts
    ]
    swap_c = Swap(g.cot, g.cot_all.at[partner_slot], g.cot_all.at[p])
    n_gather = TeamGather(
        tx, near, slot, lambda q, h: g.raw.at[q, pl.ds(h * half_rows, half_rows)]
    )
    cot_gather = TeamGather(
        tx, near, slot, lambda q, h: g.cot_all.at[q, pl.ds(h * half_tok, half_tok)]
    )
    wo_gather = TeamGather(
        tx, near, slot, lambda q, h: g.w_o.at[h, q // 2, :, q % 2]
    )
    qkv_far = FarGather(tx, far, zh, y, lambda i, j: g.wqkv.at[i, :, j])
    win_far = FarGather(tx, far, zh, y, lambda i, j: g.w_in.at[i, :, j])
    wout_far = FarGather(tx, far, zh, y, lambda i, j: g.w_out.at[i, j])

    def start_rows():
        swap_m.wait_recv()
        swap_a.wait_recv()
        n_gather.start(0)
        swap_b.wait_recv()
        n_gather.start(1)

    def start_cot():
        swap_c.wait_recv()
        cot_gather.start(0)
        cot_gather.start(1)

    @pl.when(stays)
    def _():
        swap_c.here.start()
        start_rows()
        start_cot()

    wait_all(vec_copies)
    for k in range(4):
        g.vg2[e, k] = g.vg1[2 * k] + g.vg1[2 * k + 1]
    vec_copies = [tx.send(g.vg2.at[e], g.vg2.at[e], far(rel)) for rel in FAR]
    vec_copies += [tx.send(g.bslot.at[e], g.bslot.at[e], far(rel)) for rel in FAR]
    wait_all(qkv_copies)
    qkv_far.start()
    wo_far.forward()

    @pl.when(stays)
    def _():
        n_gather.forward()
        cot_gather.forward()

    @pl.when(moves)
    def _():
        start_rows()

    wo_far.finish()
    wo_gather.start(0)
    wo_gather.start(1)

    wait_all(vec_copies)
    for k in range(8):
        group = g.vg2[2 * (k // 4), k % 4] + g.vg2[2 * (k // 4) + 1, k % 4]
        g.pg[k] = group
        g.prm[:, k * W : (k + 1) * W] = group
    prm = g.prm

    def norm_slot(rel, core):
        at = 2 * (slot(rel) // 2) + core

        def step(i, _):
            rows = pl.ds(pl.multiple_of(i * 32, 32), 32)
            hat, _unused = norm_parts(g.raw[at, rows, :].astype(F32))
            g.n_all[at, rows, :] = (hat * prm[0:1] + prm[1:2]).astype(BF)
            return 0

        lax.fori_loop(0, R // 32, step, 0)

    def early_rows(rel, step):
        @pl.when(stays)
        def _():
            step()

        @pl.when(moves)
        def _():
            n_gather.wait_sib(rel)

        norm_slot(rel, zh)

    def late_rows(rel, step):
        @pl.when(moves)
        def _():
            step()

        @pl.when(stays)
        def _():
            n_gather.wait_sib(rel)

        norm_slot(rel, 1 - zh)

    def nothing():
        pass

    early_rows((0, 0, 0), nothing)
    early_rows(ZN, nothing)
    early_rows(XN, n_gather.pass_xn)
    early_rows((1, 1, 0), n_gather.pass_diag)

    @pl.when(moves)
    def _():
        n_gather.forward()
        swap_c.copy.start()

    qkv_far.forward()
    late_rows((0, 0, 0), nothing)
    late_rows(ZN, nothing)
    win_copies = team_send(lambda q: g.pi.at[q], g.w_in.at[zh, zx, y, c])
    late_rows(XN, n_gather.pass_xn)
    wo_gather.forward()
    wout_far.start()
    qkv_far.finish()
    wqkv = lambda: flat(g.wqkv[...].reshape(32, B, 3 * W))
    own_vec = g.pg[p]
    qkv_bias = jnp.concatenate(
        [own_vec[2:3], jnp.zeros((1, W), F32), own_vec[3:4]], axis=1
    )

    def project(rel):
        pair = pl.ds(2 * (slot(rel) // 2), 2)
        out = dot(flat(g.n_all[pair]), wqkv()) + qkv_bias
        g.qkv[pair] = out.astype(BF).reshape(2, R, 3 * W)

    for rel in (SIB, ZN, XN):
        project(rel)
    late_rows((1, 1, 0), n_gather.pass_diag)
    project((1, 1, 0))
    place = [
        g.order[4 * qc + 2 * qz + qx] for qz in (0, 1) for qx in (0, 1) for qc in (0, 1)
    ]

    def pick(blocks, wanted):
        out = blocks[0]
        for block, (left, right) in zip(blocks[1:], wanted[1:]):
            out = jnp.where(jnp.full(out.shape, left, jnp.int32) == right, block, out)
        return out

    def to_sorted(load, store):
        def step(i, _):
            at = pl.multiple_of(i * 16, 16)
            blocks = [load(q, at).astype(F32) for q in range(8)]
            for j in range(8):
                store(j, at, pick(blocks, [(place[q], j) for q in range(8)]))
            return 0

        lax.fori_loop(0, T // 16, step, 0)

    def from_sorted(load, store):
        def step(i, _):
            at = pl.multiple_of(i * 16, 16)
            blocks = [load(j, at).astype(F32) for j in range(8)]
            for q in range(8):
                store(q, at, pick(blocks, [(place[q], j) for j in range(8)]))
            return 0

        lax.fori_loop(0, T // 16, step, 0)

    def store_qkv(j, at, rows):
        g.qs[pl.ds(j * T + at, 16), :] = (rows[:, :W] * 0.125).astype(BF)
        g.kk[pl.ds(MK + j * T + at, 16), :] = rows[:, W : 2 * W].astype(BF)
        g.vv[pl.ds(MK + j * T + at, 16), :] = rows[:, 2 * W :].astype(BF)

    to_sorted(lambda q, at: g.qkv[q, pl.ds(M + at, 16), :], store_qkv)
    for j in range(8):
        g.kk[j * M : (j + 1) * M, :] = g.qkv[j, :M, W : 2 * W]
        g.vv[j * M : (j + 1) * M, :] = g.qkv[j, :M, 2 * W :]
    N = 2 * T
    lane = lax.broadcasted_iota(jnp.int32, (N, W), 1)
    head_lanes = [lane < W // 2, lane >= W // 2]
    below = lax.broadcasted_iota(jnp.int32, (N, N), 1) <= lax.broadcasted_iota(
        jnp.int32, (N, N), 0
    )

    def only(value, h):
        return jnp.where(head_lanes[h], value, jnp.zeros_like(value))

    def attend(i):
        rows = slice(i * N, (i + 1) * N)
        past = MK + i * N
        end = past + N
        q_rows = g.qs[rows, :]
        parts = []
        for h in range(2):
            qh = only(q_rows, h)
            s0 = dot_nt(qh, g.kk[:past, :])
            s1 = dot_nt(qh, g.kk[past:end, :])
            s1 = jnp.where(below, s1, -1e30)
            top = jnp.maximum(
                jnp.max(s0, axis=1, keepdims=True), jnp.max(s1, axis=1, keepdims=True)
            )
            e0 = jnp.exp(s0 - top)
            e1 = jnp.exp(s1 - top)
            total = jnp.sum(e0, axis=1, keepdims=True) + jnp.sum(e1, axis=1, keepdims=True)
            scale = 1.0 / total
            w0 = (e0 * scale).astype(BF)
            w1 = (e1 * scale).astype(BF)
            g.wts[h, rows, :past] = w0
            g.wts[h, rows, past:end] = w1
            parts.append(dot(w0, g.vv[:past, :]) + dot(w1, g.vv[past:end, :]))
        g.ctx[rows, :] = jnp.where(head_lanes[0], parts[0], parts[1])

    wait_all(win_copies)

    @pl.when(inner)
    def _():
        win_far.start()

    attend(0)
    attend(1)

    @pl.when(moves)
    def _():
        start_cot()

    attend(2)
    attend(3)
    def store_ctx(q, at, rows):
        g.ctx_send[q, pl.ds(at, 16), :] = rows.astype(BF)

    from_sorted(lambda j, at: g.ctx[pl.ds(j * T + at, 16), :], store_ctx)
    ctx_copies = team_send(lambda q: g.ctx_send.at[q], g.ctx_own.at[p])
    g.ctx_own[p] = g.ctx_send[p]
    @pl.when(outer)
    def _():
        win_far.start()

    wout_far.forward()

    @pl.when(moves)
    def _():
        cot_gather.forward()

    wo_gather.finish()
    wait_all(ctx_copies)
    for q in range(8):
        g.ctx2d[:, q * W : (q + 1) * W] = g.ctx_own[q]
    w_o = lambda: flat(g.w_o[...].reshape(32, B, D))
    g.mid[...] = dot(g.ctx2d[...], w_o()) + g.raw[p, M:, :].astype(F32) + prm[4:5]
    n2_gather = TeamGather(
        tx, near, slot, lambda q, h: g.n2_all.at[q, pl.ds(h * half_tok, half_tok)]
    )

    def norm_mid(i, _):
        rows = pl.ds(pl.multiple_of(i * 32, 32), 32)
        hat, _unused = norm_parts(g.mid[rows, :])
        g.n2_all[p, rows, :] = (hat * prm[5:6] + prm[6:7]).astype(BF)
        return 0

    for half in (0, 1):
        lax.fori_loop(half * (half_tok // 32), (half + 1) * (half_tok // 32), norm_mid, 0)
        n2_gather.start(half)
    n2_gather.forward()
    win_far.forward()
    n2_gather.pass_xn()
    cot_gather.finish()
    n2_gather.pass_diag()
    for rel in QUADS:
        n2_gather.wait_sib(rel)
    win_far.finish()
    wout_far.finish()
    tok_halves = [pl.ds(h * half_tok, half_tok) for h in (0, 1)]
    hidden_bias = jnp.concatenate([g.bslot[k, 0:1, :] for k in range(4)], axis=1)
    out_sum = TeamScatter(
        tx, near, slot, lambda q: g.pb_a.at[q], g.r1_a, g.rx_a, g.rz_a, tok_halves
    )
    n2_sum = TeamScatter(
        tx, near, slot, lambda q: g.pb_b.at[q], g.r1_b, g.rx_b, g.rz_b, tok_halves
    )
    for order in range(4):
        pair = 2 * (slot(QUADS[order]) // 2)
        w_in = flat(g.w_in[...].reshape(32, B, H))
        w_out = g.w_out[...].reshape(H, D)
        inner = dot(flat(g.n2_all[pl.ds(pair, 2)]), w_in) + hidden_bias
        act, slope = gelu_parts(inner)
        act = act.astype(BF)
        act_grad = dot_nt(flat(g.cot_all[pl.ds(pair, 2)]), w_out)
        inner_grad = (act_grad * slope).astype(BF)
        at = pl.ds(pl.multiple_of(pair * T, 2 * T), 2 * T)
        g.inner[at, :] = inner_grad
        for k in range(4):
            g.act[k, at, :] = act[:, k * H4 : (k + 1) * H4]
        g.pb_b[pl.ds(pair, 2)] = dot_nt(inner_grad, w_in).astype(BF).reshape(2, T, D)
        n2_sum.push(order)
        if order:
            n2_sum.add(order - 1)
    n2_sum.add(3)
    for order in range(4):
        pair = 2 * (slot(QUADS[order]) // 2)
        at = pl.ds(pl.multiple_of(pair * T, 2 * T), 2 * T)
        act = jnp.concatenate([g.act[k, at, :] for k in range(4)], axis=1)
        out = dot(act, g.w_out[...].reshape(H, D))
        g.pb_a[pl.ds(pair, 2)] = out.astype(BF).reshape(2, T, D)
        out_sum.push(order)
    out_sum.add(0)
    cot = lambda: flat(g.cot_all[...])
    for j in (1 - y, y):
        for k in range(2):
            g.gout_s[k, j] = dot_tn(g.act[2 * k + j], cot()).astype(BF)
    gout_own = lambda i, j: g.gout_s.at[i, j]
    gout_sum = FarSum(tx, far, zh, y, gout_own, g.gout_a, g.gout_b, g.gout_c)
    gout_sum.start(1 - zh)
    n2_sum.turn()
    out_sum.add(2)
    out_sum.add(3)
    for k in range(4):
        grad = dot_tn(flat(g.n2_all[:, :, k * Q : (k + 1) * Q]), g.inner[...])
        cut = slice(2 * (k % 2), 2 * (k % 2) + 2)
        g.gin_s[k // 2, cut] = grad.astype(BF).reshape(2, 2, 2, B, H)
    gin_own = lambda i, j: g.gin_s.at[i, :, j]
    gin_sum = FarSum(tx, far, zh, y, gin_own, g.gin_a, g.gin_b, g.gin_c)
    gin_sum.start(1 - zh)
    gout_sum.start(zh)
    inner_sum = col_sum(g.inner[...])
    for k in range(4):
        g.bp[k] = jnp.broadcast_to(inner_sum[:, k * H4 : (k + 1) * H4], (8, H4))
    gb_copies = []
    for i, rel in enumerate(FAR):
        to = 2 * ((zh + rel[0]) % 2) + (y + rel[1]) % 2
        gb_copies.append(tx.send(g.bp.at[to], g.br.at[i], far(rel)))
    def norm_two_back(i, sums):
        rows = pl.ds(pl.multiple_of(i * 32, 32), 32)
        up = g.mg[rows, :]
        hat, scale = norm_parts(g.mid[rows, :])
        pull = up * prm[5:6]
        mean = jnp.mean(pull, axis=-1, keepdims=True)
        along_hat = jnp.mean(pull * hat, axis=-1, keepdims=True)
        cot_rows = g.cot_all[p, rows, :].astype(F32)
        out = cot_rows + scale * (pull - mean - hat * along_hat)
        low = out.astype(BF)
        g.mg[rows, :] = out
        g.attg[rows, :] = low
        return (
            sums[0] + col_sum(up * hat),
            sums[1] + col_sum(up),
            sums[2] + col_sum(low),
            sums[3] + col_sum(cot_rows),
        )

    zero_row = jnp.zeros((1, D), F32)
    sums = (zero_row, zero_row, zero_row, zero_row)
    steps = half_tok // 32
    for half in (0, 1):
        g.mg[tok_halves[half], :] = n2_sum.total_half(p, half)
        sums = lax.fori_loop(half * steps, (half + 1) * steps, norm_two_back, sums)
    gain_two, shift_two, bias_o, bias_out = sums
    attg = g.attg[...]
    cg = dot_nt(attg, w_o()).astype(BF)
    for q in range(8):
        g.cg_send[q] = cg[:, q * W : (q + 1) * W]
    cg_copies = team_send(lambda q: g.cg_send.at[q], g.cg_all.at[p])
    g.cg_all[p] = g.cg_send[p]
    out_sum.add(1)
    for k in range(4):
        grad = dot_tn(g.ctx2d[:, k * Q : (k + 1) * Q], attg)
        cut = slice(2 * (k % 2), 2 * (k % 2) + 2)
        g.pb_o[k // 2, cut] = grad.astype(BF).reshape(2, 2, 2, B, D)
    o_sum = TeamScatter(
        tx, near, slot, lambda q: g.pb_o.at[:, q // 2, :, q % 2], g.r1_o, None, None, [0, 1]
    )
    for order in range(4):
        o_sum.push(order)
    gout_sum.turn()
    out_sum.turn()

    wait_all(cg_copies)

    def store_cg(j, at, rows):
        g.cg_sorted[pl.ds(j * T + at, 16), :] = rows.astype(BF)

    to_sorted(lambda q, at: g.cg_all[q, pl.ds(at, 16), :], store_cg)
    g.dk[...] = jnp.zeros_like(g.dk)
    g.dv[...] = jnp.zeros_like(g.dv)

    def attend_back(i):
        rows = slice(i * N, (i + 1) * N)
        end = MK + (i + 1) * N
        cg_rows = g.cg_sorted[rows, :]
        q_rows = g.qs[rows, :]
        product = cg_rows.astype(F32) * g.ctx[rows, :]
        parts = []
        for h in range(2):
            qh, ch = only(q_rows, h), only(cg_rows, h)
            delta = jnp.sum(only(product, h), axis=1, keepdims=True)
            w = g.wts[h, rows, :end]
            pull = dot_nt(ch, g.vv[:end, :])
            ds = (w.astype(F32) * (pull - delta)).astype(BF)
            parts.append(dot(ds, g.kk[:end, :]))
            g.dk[:end, :] += dot_tn(ds, qh)
            g.dv[:end, :] += dot_tn(w, ch)
        g.dq[rows, :] = jnp.where(head_lanes[0], parts[0], parts[1]) * 0.125

    attend_back(0)
    for order in range(4):
        o_sum.add(order, hand=False)
    go_copy = tx.send(g.pb_o.at[:, :, 1 - y, c], g.go_y, far((0, 1)))
    attend_back(1)
    gin_sum.turn()
    attend_back(2)
    attend_back(3)
    def load_grads(j, at):
        keys = pl.ds(MK + j * T + at, 16)
        return jnp.concatenate(
            [g.dq[pl.ds(j * T + at, 16), :], g.dk[keys, :], g.dv[keys, :]], axis=1
        )

    def store_grads(q, at, rows):
        g.dqkv[q, pl.ds(M + at, 16), :] = rows.astype(BF)

    from_sorted(load_grads, store_grads)
    for q in range(8):
        mt = slice(q * M, (q + 1) * M)
        g.dqkv[q, :M, :W] = jnp.zeros((M, W), BF)
        g.dqkv[q, :M, W : 2 * W] = g.dk[mt, :].astype(BF)
        g.dqkv[q, :M, 2 * W :] = g.dv[mt, :].astype(BF)
    n_sum = TeamScatter(
        tx, near, slot, lambda q: g.pb_n.at[q], g.r1_n, g.rx_n, g.rz_n, tok_halves
    )
    for order in range(4):
        pair = 2 * (slot(QUADS[order]) // 2)
        rows = flat(g.dqkv[pl.ds(pair, 2), M:, :])
        g.pb_n[pl.ds(pair, 2)] = dot_nt(rows, wqkv()).astype(BF).reshape(2, T, D)
        n_sum.push(order)
        if order:
            n_sum.add(order - 1)
    n_sum.add(3)
    g.vp[...] = jnp.zeros_like(g.vp)
    qkv_sum = jnp.zeros((1, 3 * W), F32)
    for q in range(8):
        qkv_sum = qkv_sum + col_sum(g.dqkv[q])
    qkv_sum8 = jnp.broadcast_to(qkv_sum, (8, 3 * W))
    ones = jnp.ones((8, 3 * W), F32)
    gains = []
    for k in range(4):
        grad = dot_tn(flat(g.n_all[:, :, k * Q : (k + 1) * Q]), flat(g.dqkv[...]))
        cut = slice(2 * (k % 2), 2 * (k % 2) + 2)
        g.gqkv_s[k // 2, cut] = grad.astype(BF).reshape(2, 2, 2, B, 3 * W)
        w = flat(g.wqkv[k // 2, cut].reshape(8, B, 3 * W)).astype(F32)
        gains.append(dot_nt(ones, grad * w, EXACT)[0:1])
    gqkv_own = lambda i, j: g.gqkv_s.at[i, :, j]
    gqkv_sum = FarSum(tx, far, zh, y, gqkv_own, g.gqkv_a, g.gqkv_b, g.gqkv_c)
    gqkv_sum.start(1 - zh)
    gin_sum.start(zh)
    gqkv_sum.start(zh)
    n_sum.turn()
    for k in range(4):
        cut = slice(2 * (k % 2), 2 * (k % 2) + 2)
        w = flat(g.wqkv[k // 2, cut].reshape(8, B, 3 * W)).astype(F32)
        shifts = dot_nt(qkv_sum8, w, EXACT)
        for i in range(2):
            at = slice(i * W, (i + 1) * W)
            shift = shifts[0:1, at]
            vec = g.pg[2 * k + i]
            g.vp[2 * k + i, 0:1, :] = (gains[k][:, at] - vec[1:2] * shift) / vec[0:1]
            g.vp[2 * k + i, 1:2, :] = shift
    g.vp[p, 2:3, :] = qkv_sum[:, :W]
    g.vp[p, 3:4, :] = qkv_sum[:, 2 * W :]
    for k in range(8):
        at = slice(k * W, (k + 1) * W)
        g.vp[k, 4:5, :] = bias_o[:, at]
        g.vp[k, 5:6, :] = gain_two[:, at]
        g.vp[k, 6:7, :] = shift_two[:, at]
        g.vp[k, 7:8, :] = bias_out[:, at]
    vec_copies = []
    for i, rel in enumerate(FAR):
        to = pl.ds(4 * ((zh + rel[0]) % 2), 4)
        vec_copies.append(tx.send(g.vp.at[to], g.vr.at[i], far(rel)))
    go_copy.wait_recv()
    for k in range(4):
        total = g.pb_o[:, k, y, c].astype(F32) + g.go_y[:, k].astype(F32)
        g.go_m[k] = total.astype(BF)
    go_team = TeamScatter(
        tx, near, slot, lambda q: g.go_m.at[q // 2], None, g.rx_o, g.rz_o, [0, 1]
    )
    for order in (0, 1):
        for half in (0, 1):
            go_team.hand(order, half)
    gqkv_sum.turn()
    lo = out_sum.total(p) + g.mid[...] + prm[7:8]
    g.lo_s[...] = lo.astype(BF)
    swap_lo = swap(g.lo_s, g.lo, g.lo)
    g.gout[...] = gout_sum.total()
    g.gin_d[...] = flat_team(gin_sum.total())
    gin_copies = team_send(lambda q: g.gin_d.at[q], g.gin_e.at[p])
    g.gin_e[p] = g.gin_d[p]
    wait_all(gb_copies)
    g.gbin[...] = (g.bp[e] + g.br[0] + g.br[1] + g.br[2])[:1]
    wait_all(vec_copies)
    g.vs[...] = g.vp[pl.ds(4 * zh, 4)] + g.vr[0] + g.vr[1] + g.vr[2]
    vec_copies = team_send(lambda q: g.vs.at[q // 2], g.va.at[p])
    g.va[p] = g.vs[zx]
    def norm_one_back(i, _):
        rows = pl.ds(pl.multiple_of(i * 32, 32), 32)
        hat, scale = norm_parts(
            g.raw[p, pl.ds(pl.multiple_of(M + i * 32, 32), 32), :].astype(F32)
        )
        pull = g.mid[rows, :] * prm[0:1]
        mean = jnp.mean(pull, axis=-1, keepdims=True)
        along_hat = jnp.mean(pull * hat, axis=-1, keepdims=True)
        out = g.mg[rows, :] + scale * (pull - mean - hat * along_hat)
        g.ig_s[rows, :] = out.astype(BF)
        return 0

    swap_ig = []
    for half in (0, 1):
        at = tok_halves[half]
        g.mid[at, :] = n_sum.total_half(p, half)
        lax.fori_loop(half * steps, (half + 1) * steps, norm_one_back, 0)
        swap_ig.append(swap(g.ig_s.at[at], g.ig.at[at], g.ig.at[at]))
    go_team.turn()
    g.gqkv_d[...] = flat_team(gqkv_sum.total())
    gqkv_copies = team_send(lambda q: g.gqkv_d.at[q], g.gqkv_e.at[p])
    g.gqkv_e[p] = g.gqkv_d[p]
    g.go_s[...] = go_team.total(p).astype(BF)
    go_copy = tx.send(g.go_s.at[1 - zh], g.go_c, far((1, 0)))
    wait_all(gin_copies)
    for q in range(8):
        for k in range(4):
            at = (16 * (k // 2) + 4 * (q // 2) + 2 * (k % 2) + q % 2) * H4
            g.gin[:, at : at + H4] = g.gin_e[q, :, k * H4 : (k + 1) * H4].astype(F32)
    wait_all(vec_copies)
    total = g.va[0]
    for q in range(1, 8):
        total = total + g.va[q]
    g.gvec[...] = total
    wait_all(gqkv_copies)
    for q in range(8):
        for i, out in enumerate((g.gq, g.gk, g.gv)):
            out[:, q * W : (q + 1) * W] = g.gqkv_e[q, :, i * W : (i + 1) * W].astype(F32)
    go_copy.wait_recv()
    g.go[...] = g.go_s[zh].astype(F32) + g.go_c[...].astype(F32)
    swap_lo.wait_recv()
    for copy in swap_ig:
        copy.wait_recv()
    tx.drain()

    @pl.when(moves)
    def _():
        for copy in swaps:
            copy.wait_send()


def flat_team(value):
    return value.astype(BF).reshape((8,) + value.shape[2:])


def finish_kernel(share, *refs):
    ins, outs, held = refs[:10], refs[10:20], refs[20:30]
    wide, picked, sems = refs[30:]
    loads = [pltpu.make_async_copy(ins[i], held[i], sems.at[i]) for i in range(10)]
    for copy in loads:
        copy.start()
    stores = []
    for i in (0, 2, 3, 4, 5, 6, 7, 9, 1, 8):
        loads[i].wait()
        src = held[i]
        if i == 1:
            wide[...] = src[...].astype(F32)
            src = wide
        if i == 8:
            mine = lax.axis_index("dp")
            part = src[:, :share]
            for k in range(1, src.shape[1] // share):
                part = jnp.where(mine == k, src[:, k * share : (k + 1) * share], part)
            picked[...] = part
            src = picked
        stores.append(pltpu.make_async_copy(src, outs[i], sems.at[10 + i]))
        stores[-1].start()
    for copy in stores:
        copy.wait()


def run_layer(layer_input, memory, cotangent, block_order, w_query, w_key, w_value, w_output, w_in, w_out, vectors, b_in):
    T, D = layer_input.shape[1:]
    M = memory.shape[1]
    FF = w_in.shape[1]
    W = D // 8
    share = vectors.shape[1]
    shapes = scratch_list(T, M, D, FF)
    vmem = pl.BlockSpec(memory_space=pltpu.VMEM)
    smem = pl.BlockSpec(memory_space=pltpu.SMEM)
    hbm = pl.BlockSpec(memory_space=pl.ANY)
    outs = pl.pallas_call(
        functools.partial(layer_kernel, T, M, D, FF, share),
        out_shape=(
            jax.ShapeDtypeStruct((T, D), BF),
            jax.ShapeDtypeStruct((T, D), BF),
            jax.ShapeDtypeStruct(w_query.shape, F32),
            jax.ShapeDtypeStruct(w_key.shape, F32),
            jax.ShapeDtypeStruct(w_value.shape, F32),
            jax.ShapeDtypeStruct(w_output.shape, F32),
            jax.ShapeDtypeStruct(w_in.shape, F32),
            jax.ShapeDtypeStruct(w_out.shape, F32),
            jax.ShapeDtypeStruct((8, W), F32),
            jax.ShapeDtypeStruct((1, b_in.shape[0]), F32),
        ),
        in_specs=[hbm, hbm, hbm, smem] + [hbm] * 6 + [vmem] * 2,
        out_specs=[vmem] * 10,
        scratch_shapes=[pltpu.VMEM(shape, kind) for shape, kind in shapes.values()]
        + [pltpu.SemaphoreType.DMA((SEMS,)), pltpu.SemaphoreType.DMA((SEMS,))],
        compiler_params=pltpu.CompilerParams(
            collective_id=0, has_side_effects=True, vmem_limit_bytes=63 * 2**20
        ),
    )(layer_input[0], memory[0], cotangent[0], block_order, w_query, w_key, w_value, w_output, w_in, w_out, vectors, b_in[None])
    final = [jax.ShapeDtypeStruct(outs[0].shape, BF), jax.ShapeDtypeStruct(outs[1].shape, F32)]
    final += [jax.ShapeDtypeStruct(out.shape, F32) for out in outs[2:8]]
    final += [jax.ShapeDtypeStruct((8, share), F32), jax.ShapeDtypeStruct((1, b_in.shape[0]), F32)]
    lo, ig, gq, gk, gv, go, gin, gout, gvec, gbin = pl.pallas_call(
        functools.partial(finish_kernel, share),
        out_shape=final,
        in_specs=[hbm] * 10,
        out_specs=[hbm] * 10,
        scratch_shapes=[pltpu.VMEM(out.shape, out.dtype) for out in outs]
        + [
            pltpu.VMEM((T, D), F32),
            pltpu.VMEM((8, share), F32),
            pltpu.SemaphoreType.DMA((20,)),
        ],
        compiler_params=pltpu.CompilerParams(vmem_limit_bytes=60 * 2**20),
    )(*outs)
    return (lo[None], ig[None], gq, gk, gv, go, gin, gout, gvec, gbin[0])


masked_value = -1e30


def passed_along(block, axis, distance):
    devices = range(lax.axis_size(axis))
    route = [((i - distance) % len(devices), i) for i in devices]
    return lax.ppermute(block, axis, route)


def layer_norm(values, gain, shift):
    center = values - jnp.mean(values, axis=-1, keepdims=True)
    spread = jnp.mean(center * center, axis=-1, keepdims=True)
    return center * lax.rsqrt(spread + 1e-05) * gain + shift


def contract_rows(left, right):
    return lax.dot_general(
        left, right, (((0,), (0,)), ((), ())), preferred_element_type=jnp.float32
    )


def times_transposed(left, right):
    return lax.dot_general(
        left, right, (((1,), (1,)), ((), ())), preferred_element_type=jnp.float32
    )


def split_heads(matrix, heads):
    return matrix.reshape(matrix.shape[0], heads, matrix.shape[1] // heads)


def score_block(query_heads, key_rows):
    key_heads = split_heads(key_rows, query_heads.shape[1])
    return (
        jnp.einsum("qhd,khd->hqk", query_heads, key_heads, preferred_element_type=jnp.float32)
        * 0.125
    )


def lookup_block(order, device):
    return jnp.sum(jnp.where(jnp.arange(order.shape[0]) == device, order, 0))


def split_piece(piece, rows_dev, mem_rows):
    shards = piece.shape[0] // rows_dev
    blocks = piece.reshape(shards, rows_dev, piece.shape[1])
    memory_part = blocks[:, :mem_rows].reshape(shards * mem_rows, piece.shape[1])
    token_part = blocks[:, mem_rows:].reshape(shards * (rows_dev - mem_rows), piece.shape[1])
    return (shards, memory_part, token_part)


def piece_positions(order, shards, tok_rows):
    shard_ids = jnp.arange(shards)
    hits = shard_ids[:, None] == jnp.arange(order.shape[0])[None, :]
    starts = jnp.sum(jnp.where(hits, order[None, :], 0), axis=1)
    positions = (starts[:, None] * tok_rows + jnp.arange(tok_rows)[None, :]).reshape(
        shards * tok_rows
    )
    return (starts, positions)


def softmax_stats(carry, scores):
    running, total = carry
    top = jnp.maximum(running, jnp.max(scores, axis=2))
    total = total * jnp.exp(running - top) + jnp.sum(jnp.exp(scores - top[:, :, None]), axis=2)
    return (top, total)


def per_device(
    layer_input,
    memory,
    cotangent,
    block_order,
    w_query,
    w_key,
    w_value,
    w_output,
    w_in,
    w_out,
    vectors,
    b_in,
):
    bf16 = jnp.bfloat16
    gathered = (
        lax.all_gather(w_query.astype(bf16), ("blk", "dp"), axis=0, tiled=True),
        lax.all_gather(w_key.astype(bf16), ("blk", "dp"), axis=0, tiled=True),
        lax.all_gather(w_value.astype(bf16), ("blk", "dp"), axis=0, tiled=True),
        lax.all_gather(w_output.astype(bf16), ("blk", "dp"), axis=0, tiled=True),
        lax.all_gather(w_in.astype(bf16), ("blk", "dp"), axis=0, tiled=True),
        lax.all_gather(w_out.astype(bf16), ("blk", "dp"), axis=0, tiled=True),
        lax.all_gather(vectors.astype(bf16), ("blk", "dp"), axis=1, tiled=True),
        lax.all_gather(b_in.astype(bf16), ("blk", "dp"), axis=0, tiled=True),
    )
    (
        query_full,
        key_full,
        value_full,
        output_full,
        inner_full,
        outer_full,
        vector_full,
        inner_low,
    ) = gathered
    params = vector_full.astype(jnp.float32)
    inner_shift = inner_low.astype(jnp.float32)
    heads = HEADS
    tokens = layer_input[0].astype(jnp.float32)
    recalled = memory[0].astype(jnp.float32)
    tok_rows = tokens.shape[0]
    mem_rows = recalled.shape[0]
    rows_dev = tok_rows + mem_rows
    width = tokens.shape[1]
    blocks_total = lax.axis_size("blk")
    here = lax.axis_index("blk")
    own_block = lookup_block(block_order, here)
    query_pos = own_block * tok_rows + jnp.arange(tok_rows)
    both_rows = jnp.concatenate([recalled, tokens], axis=0)
    normed = layer_norm(both_rows, params[0], params[1]).astype(bf16)
    normed_tok = normed[mem_rows:]
    queries = (
        jnp.dot(normed_tok, query_full, preferred_element_type=jnp.float32) + params[2]
    ).astype(bf16)
    keys_all = jnp.dot(normed, key_full, preferred_element_type=jnp.float32).astype(bf16)
    values_all = (
        jnp.dot(normed, value_full, preferred_element_type=jnp.float32) + params[3]
    ).astype(bf16)
    query_heads = split_heads(queries, heads)

    def causal(scores, key_pos):
        return jnp.where(key_pos[None, None, :] <= query_pos[None, :, None], scores, masked_value)

    start_stats = (
        jnp.full((heads, tok_rows), masked_value, jnp.float32),
        jnp.zeros((heads, tok_rows), jnp.float32),
    )
    carry = start_stats
    shards, memory_part, token_part = split_piece(
        lax.all_gather(keys_all, "blk", axis=0, tiled=True), rows_dev, mem_rows
    )
    starts, token_pos = piece_positions(block_order, shards, tok_rows)
    carry = softmax_stats(carry, score_block(query_heads, memory_part))

    def with_tokens(state):
        return softmax_stats(state, causal(score_block(query_heads, token_part), token_pos))

    def without_tokens(state):
        return state

    running, total = lax.cond(jnp.any(starts <= own_block), with_tokens, without_tokens, carry)
    log_total = running + jnp.log(total)

    def value_part(context, part, key_pos):
        scores = score_block(query_heads, part[:, :width])
        if key_pos is not None:
            scores = causal(scores, key_pos)
        weights = jnp.exp(scores - log_total[:, :, None]).astype(bf16)
        return context + jnp.einsum(
            "hqk,khd->qhd",
            weights,
            split_heads(part[:, width:], heads),
            preferred_element_type=jnp.float32,
        )

    key_values = jnp.concatenate([keys_all, values_all], axis=1)
    context = jnp.zeros((tok_rows, heads, width // heads), jnp.float32)
    shards, memory_part, add_token_part = split_piece(
        lax.all_gather(key_values, "blk", axis=0, tiled=True), rows_dev, mem_rows
    )
    starts, add_token_pos = piece_positions(block_order, shards, tok_rows)
    context = value_part(context, memory_part, None)

    def with_tokens(state):
        return value_part(state, add_token_part, add_token_pos)

    def without_tokens(state):
        return state

    context = lax.cond(jnp.any(starts <= own_block), with_tokens, without_tokens, context)
    context_low = context.reshape(tok_rows, width).astype(bf16)
    attended = jnp.dot(context_low, output_full, preferred_element_type=jnp.float32) + params[4]
    middle = tokens + attended
    normed_two = layer_norm(middle, params[5], params[6]).astype(bf16)
    inner = jnp.dot(normed_two, inner_full, preferred_element_type=jnp.float32) + inner_shift
    activated = jax.nn.gelu(inner, approximate=True).astype(bf16)
    result = middle + jnp.dot(activated, outer_full, preferred_element_type=jnp.float32) + params[7]
    output = result.astype(bf16)
    upstream = cotangent[0]
    upstream_full = upstream.astype(jnp.float32)
    grad_outer = contract_rows(activated, upstream)
    grad_outer_bias = jnp.sum(upstream_full, axis=0)
    act_grad = times_transposed(upstream, outer_full)
    _, gelu_back = jax.vjp(functools.partial(jax.nn.gelu, approximate=True), inner)
    inner_grad = gelu_back(act_grad)[0].astype(bf16)
    grad_inner = contract_rows(normed_two, inner_grad)
    grad_inner_bias = jnp.sum(inner_grad.astype(jnp.float32), axis=0)
    normed_two_grad = times_transposed(inner_grad, inner_full)
    _, norm_two_back = jax.vjp(layer_norm, middle, params[5], params[6])
    middle_part, grad_gain_two, grad_shift_two = norm_two_back(normed_two_grad)
    middle_grad = upstream_full + middle_part
    attended_grad = middle_grad.astype(bf16)
    grad_output = contract_rows(context_low, attended_grad)
    grad_output_bias = jnp.sum(attended_grad.astype(jnp.float32), axis=0)
    context_grad = times_transposed(attended_grad, output_full).astype(bf16)
    context_heads = split_heads(context_grad, heads)
    delta = jnp.einsum("qhd,qhd->hq", context_heads.astype(jnp.float32), context)

    def attend_back(queries_grad, part, key_pos):
        count = part.shape[0]
        key_heads = split_heads(part[:, :width], heads)
        value_heads = split_heads(part[:, width:], heads)
        scores = score_block(query_heads, part[:, :width])
        if key_pos is not None:
            scores = causal(scores, key_pos)
        exact = jnp.exp(scores - log_total[:, :, None])
        weight_low = exact.astype(bf16)
        weight_grad = jnp.einsum(
            "qhd,khd->hqk", context_heads, value_heads, preferred_element_type=jnp.float32
        )
        score_grad = (exact * (weight_grad - delta[:, :, None])).astype(bf16)
        queries_grad = (
            queries_grad
            + jnp.einsum("hqk,khd->qhd", score_grad, key_heads, preferred_element_type=jnp.float32)
            * 0.125
        )
        key_grad = (
            jnp.einsum("hqk,qhd->khd", score_grad, query_heads, preferred_element_type=jnp.float32)
            * 0.125
        )
        value_grad = jnp.einsum(
            "hqk,qhd->khd", weight_low, context_heads, preferred_element_type=jnp.float32
        )
        return (
            queries_grad,
            jnp.concatenate(
                [key_grad.reshape(count, width), value_grad.reshape(count, width)], axis=1
            ),
        )

    def visit(queries_grad, travelling, travel_grad, anchor):
        anchor_block = lookup_block(block_order, anchor)
        queries_grad, memory_grad = attend_back(queries_grad, travelling[:mem_rows], None)
        token_pos = anchor_block * tok_rows + jnp.arange(tok_rows)

        def with_tokens(state):
            return attend_back(state, travelling[mem_rows:], token_pos)

        def without_tokens(state):
            return (state, jnp.zeros((tok_rows, 2 * width), jnp.float32))

        queries_grad, token_grad = lax.cond(
            anchor_block <= own_block, with_tokens, without_tokens, queries_grad
        )
        return (queries_grad, travel_grad + jnp.concatenate([memory_grad, token_grad], axis=0))

    def pass_grads(values):
        return passed_along(values.astype(jnp.bfloat16), "blk", 1).astype(values.dtype)

    queries_grad, travel_grad = visit(
        jnp.zeros((tok_rows, heads, width // heads), jnp.float32),
        key_values,
        jnp.zeros((rows_dev, 2 * width), jnp.float32),
        here,
    )

    def turn(step, state):
        queries_grad, travelling, travel_grad = state
        travelling = passed_along(travelling, "blk", 1)
        travel_grad = pass_grads(travel_grad)
        anchor = (here - step) % blocks_total
        queries_grad, travel_grad = visit(queries_grad, travelling, travel_grad, anchor)
        return (queries_grad, travelling, travel_grad)

    queries_grad, travelling, travel_grad = lax.fori_loop(
        1, blocks_total, turn, (queries_grad, key_values, travel_grad)
    )
    travel_grad = pass_grads(travel_grad)
    pair_grad = travel_grad.astype(bf16)
    key_grad = pair_grad[:, :width]
    value_grad = pair_grad[:, width:]
    query_grad = queries_grad.reshape(tok_rows, width).astype(bf16)
    grad_query = contract_rows(normed_tok, query_grad)
    grad_query_bias = jnp.sum(query_grad.astype(jnp.float32), axis=0)
    grad_key = contract_rows(normed, key_grad)
    grad_value = contract_rows(normed, value_grad)
    grad_value_bias = jnp.sum(value_grad.astype(jnp.float32), axis=0)
    normed_grad = times_transposed(key_grad, key_full) + times_transposed(value_grad, value_full)
    query_part = times_transposed(query_grad, query_full)
    normed_grad = normed_grad + jnp.concatenate(
        [jnp.zeros((mem_rows, width), jnp.float32), query_part], axis=0
    )
    _, norm_one_back = jax.vjp(layer_norm, both_rows, params[0], params[1])
    rows_grad, grad_gain_one, grad_shift_one = norm_one_back(normed_grad)
    input_grad = middle_grad + rows_grad[mem_rows:]
    vector_grad = jnp.stack(
        [
            grad_gain_one,
            grad_shift_one,
            grad_query_bias,
            grad_value_bias,
            grad_output_bias,
            grad_gain_two,
            grad_shift_two,
            grad_outer_bias,
        ]
    )
    out_query, out_key, out_value, out_output, out_inner, out_outer, out_vectors, out_bias = (
        lax.psum_scatter(grad_query, ("blk", "dp"), scatter_dimension=0, tiled=True),
        lax.psum_scatter(grad_key, ("blk", "dp"), scatter_dimension=0, tiled=True),
        lax.psum_scatter(grad_value, ("blk", "dp"), scatter_dimension=0, tiled=True),
        lax.psum_scatter(grad_output, ("blk", "dp"), scatter_dimension=0, tiled=True),
        lax.psum_scatter(grad_inner, ("blk", "dp"), scatter_dimension=0, tiled=True),
        lax.psum_scatter(grad_outer, ("blk", "dp"), scatter_dimension=0, tiled=True),
        lax.psum_scatter(vector_grad, ("blk", "dp"), scatter_dimension=1, tiled=True),
        lax.psum_scatter(grad_inner_bias, ("blk", "dp"), scatter_dimension=0, tiled=True),
    )
    return (
        output[None],
        input_grad[None],
        out_query,
        out_key,
        out_value,
        out_output,
        out_inner,
        out_outer,
        out_vectors,
        out_bias,
    )


def solution(mesh):
    rows = P("dp", "blk", None)
    shard = P(("blk", "dp"), None)
    in_specs = (rows, rows, rows, P()) + (shard,) * 6 + (P(None, ("blk", "dp")), P(("blk", "dp")))
    out_specs = (rows, rows) + (shard,) * 6 + (P(None, ("blk", "dp")), P(("blk", "dp")))
    planes = mesh.shape["blk"] == 8 and mesh.shape["dp"] == 4
    return jax.shard_map(
        run_layer if planes else per_device,
        mesh=mesh,
        in_specs=in_specs,
        out_specs=out_specs,
        check_vma=False,
    )
```
